512 devices in a mesh: pipe: 4 (over x), sp: 32 (over z, core), dp: 4 (over y).
Axes of the slice: x: 4, y: 4, z: 16, core: 2. Of those that a mesh axis runs over, the one named last changes fastest.
Arguments:
- fresh_input: bfloat16 [4, 4, 128, 240, 128], P('pipe', 'dp', 'sp'), may hold values from -6 to 6
- saved_input: bfloat16 [4, 4, 128, 240, 128], P('pipe', 'dp', 'sp'), may hold values from -6 to 6
- output_grad: bfloat16 [4, 4, 128, 240, 128], P('pipe', 'dp', 'sp'), may hold values from -6 to 6
- expand_weight: bfloat16 [4, 128, 768], P('pipe'), may hold values from -0.5 to 0.5
- reduce_weight: bfloat16 [4, 768, 128], P('pipe'), may hold values from -0.21875 to 0.21875
- filter_weight: float32 [4, 2, 120, 128], P('pipe'), may hold values from -6 to 6
- cycle_table: int32 [128], replicated, may hold values from 0 to 127, each once
Outputs:
- next_input: bfloat16 [4, 4, 128, 240, 128], P('pipe', 'dp', 'sp')
- input_grad: bfloat16 [4, 4, 128, 240, 128], P('pipe', 'dp', 'sp')
- expand_grad: float32 [4, 128, 768], P('pipe', None, 'dp')
- reduce_grad: float32 [4, 768, 128], P('pipe', 'dp')
- filter_grad: float32 [4, 2, 120, 128], P('pipe')
The draws below stay inside these ranges and needn't reach their ends.
Inputs may be any that keep to these rules, and one draw needn't show every extreme that they name: `cycle_table`: each of 0 .. 127 appears once; values 120 or more mark empty cycle slots.
All inputs are finite; a program needn't handle non-finite values.
Results may differ from the reference program's by a relative error of at most 0.025.
Values may be sent and summed in bfloat16 or wider, within the bound.
No kernel may reach another device: no remote copies, remote signals or barrier semaphores. Data moves between devices by JAX's collectives and lax.ppermute only.
A program may use at most 64 MiB of HBM per device.

```python
import math
import jax
import jax.numpy as jnp
from jax import lax

NLAT = 120
NLON = 240
CH = 128
HID = 768
SECTIONS = 4
GROUPS = 4
SLOTS_ALL = 128


def block_scale(stream_key, dims, split, low, top_value):
    level = 1.0
    for axis_at, shards_of in split:
        draws = jax.random.uniform(jax.random.fold_in(jax.random.fold_in(stream_key, 6), axis_at), (shards_of,), jnp.float32, low / len(split), top_value / len(split))
        level = level * jnp.repeat(jnp.exp(draws), dims[axis_at] // shards_of).reshape((-1,) + (1,) * (len(dims) - 1 - axis_at))
    return level


def bell_draw(stream_key, dims, spread, most, pieces=(), kind=jnp.bfloat16):
    array = spread * jax.random.normal(stream_key, dims, jnp.float32)
    if pieces:
        array = array * block_scale(stream_key, dims, pieces, -0.22, 0.18)
    return jnp.clip(array, -most, most).astype(kind)


def setup_inputs(seed: int = 0) -> dict:
    keys = jax.random.split(jax.random.key(seed), 8)
    return {
        "fresh_input": bell_draw(keys[0], (SECTIONS, GROUPS, SLOTS_ALL, NLON, CH), 1.0, 6.0, ((0, 4), (1, 4), (2, 32))),
        "saved_input": bell_draw(keys[1], (SECTIONS, GROUPS, SLOTS_ALL, NLON, CH), 1.0, 6.0, ((0, 4), (1, 4), (2, 32))),
        "output_grad": bell_draw(keys[2], (SECTIONS, GROUPS, SLOTS_ALL, NLON, CH), 1.0, 6.0, ((0, 4), (1, 4), (2, 32))),
        "expand_weight": bell_draw(keys[3], (SECTIONS, CH, HID), CH ** -0.5, 0.5, ((0, 4),)),
        "reduce_weight": bell_draw(keys[4], (SECTIONS, HID, CH), HID ** -0.5, 0.21875, ((0, 4),)),
        "filter_weight": bell_draw(keys[5], (SECTIONS, 2, NLAT, CH), 1.0, 6.0, ((0, 4),), jnp.float32),
        "cycle_table": jax.random.permutation(keys[6], SLOTS_ALL).astype(jnp.int32),
    }


ROOT_HALF = 0.7071067811865476
INV_ROOT_TAU = 0.3989422804014327

def gelu_value(pre_act):
    return 0.5 * pre_act * (1.0 + lax.erf(pre_act * ROOT_HALF))

def gelu_slope(pre_act):
    return 0.5 * (1.0 + lax.erf(pre_act * ROOT_HALF)) + pre_act * jnp.exp(-0.5 * pre_act * pre_act) * INV_ROOT_TAU

def legendre(lat_index, order_index, cycles):
    lat_ok = (lat_index < cycles).astype(jnp.float32)
    order_ok = (order_index < cycles).astype(jnp.float32)
    colatitude = math.pi * (jnp.minimum(lat_index, cycles - 1).astype(jnp.float32) + 0.5) / cycles
    cosine = jnp.cos(colatitude)[None, :]
    sine_value = jnp.sin(colatitude)[None, :]
    order_value = jnp.minimum(order_index, cycles - 1).astype(jnp.float32)[:, None]
    log_start = 0.5 * (jnp.log((2.0 * order_value + 1.0) / (4.0 * math.pi)) + lax.lgamma(2.0 * order_value + 1.0) - 2.0 * lax.lgamma(order_value + 1.0) - order_value * math.log(4.0)) + order_value * jnp.log(sine_value)
    starting = jnp.exp(log_start)
    zero_rows = jnp.zeros_like(starting)

    def advance(state_pair, degree):
        previous, earlier = state_pair
        degree_value = degree.astype(jnp.float32)
        upper_term = jnp.maximum(4.0 * degree_value * degree_value - 1.0, 0.0)
        ratio_main = jnp.sqrt(upper_term / jnp.maximum(degree_value * degree_value - order_value * order_value, 1.0))
        ratio_back = jnp.sqrt(jnp.maximum((degree_value - 1.0) ** 2 - order_value * order_value, 0.0) / jnp.maximum(4.0 * (degree_value - 1.0) ** 2 - 1.0, 1.0))
        rising = ratio_main * (cosine * previous - ratio_back * earlier)
        current = jnp.where(degree_value == order_value, starting, jnp.where(degree_value > order_value, rising, 0.0))
        return ((current, previous), current)
    _, stacked = lax.scan(advance, (zero_rows, zero_rows), jnp.arange(cycles, dtype=jnp.int32))
    valid_mask = order_ok[:, None] * lat_ok[None, :]
    return jnp.transpose(stacked, (1, 0, 2)) * valid_mask[:, None, :]

def cycle_weights(lat_index, cycles):
    valid_cycle = (lat_index < cycles).astype(jnp.float32)
    colatitude = math.pi * (jnp.minimum(lat_index, cycles - 1).astype(jnp.float32) + 0.5) / cycles
    return math.pi / cycles * jnp.sin(colatitude) * valid_cycle

def fourier_tables(order_index, cycles, points):
    valid_order = (order_index < cycles).astype(jnp.float32)[None, :]
    order_value = jnp.minimum(order_index, cycles - 1).astype(jnp.int32)
    longitude = jnp.arange(points, dtype=jnp.int32)
    phase_angle = 2.0 * math.pi / points * (longitude[:, None] * order_value[None, :] % points).astype(jnp.float32)
    scaled = valid_order * (2.0 * math.pi / points)
    forward = jnp.concatenate([jnp.cos(phase_angle) * scaled, -jnp.sin(phase_angle) * scaled], axis=1)
    order_scale = jnp.where(order_value == 0, 1.0, 2.0)[None, :] * valid_order / (2.0 * math.pi)
    inverse = jnp.concatenate([jnp.cos(phase_angle) * order_scale, -jnp.sin(phase_angle) * order_scale], axis=1).T
    return (forward.astype(jnp.bfloat16), inverse.astype(jnp.bfloat16))

def spectral_pass(tokens, filt, forward, analysis, synthesis, inverse):
    row_count, points, chan_count = tokens.shape
    order_count = synthesis.shape[0]
    coeffs = jnp.einsum('jnc,nk->jkc', tokens.astype(jnp.float32), forward.astype(jnp.float32)).astype(jnp.bfloat16)
    coeffs = coeffs.reshape(row_count, 2, order_count, chan_count)
    spectra = jnp.einsum('tlj,jrtc->trlc', analysis.astype(jnp.float32), coeffs.astype(jnp.float32))
    real_part = filt[0] * spectra[:, 0] - filt[1] * spectra[:, 1]
    imag_part = filt[0] * spectra[:, 1] + filt[1] * spectra[:, 0]
    filtered = jnp.stack([real_part, imag_part], axis=1).astype(jnp.bfloat16)
    values = jnp.einsum('tlj,trlc->jrtc', synthesis.astype(jnp.float32), filtered.astype(jnp.float32)).astype(jnp.bfloat16)
    values = values.reshape(row_count, 2 * order_count, chan_count)
    spatial = jnp.einsum('jkc,kn->jnc', values.astype(jnp.float32), inverse.astype(jnp.float32))
    return (spatial, spectra)

def mlp_pass(tokens, spatial, expand, contract, cycle_mask):
    grid_shape = tokens.shape
    flat_rows = (tokens.astype(jnp.float32) + spatial).reshape(-1, grid_shape[-1])
    mixed_b = flat_rows.astype(jnp.bfloat16)
    hidden_pre = jnp.dot(mixed_b, expand, preferred_element_type=jnp.float32)
    hidden = gelu_value(hidden_pre).astype(jnp.bfloat16)
    result = flat_rows + jnp.dot(hidden, contract, preferred_element_type=jnp.float32)
    result = (result.reshape(grid_shape) * cycle_mask[:, None, None]).astype(jnp.bfloat16)
    return (result, mixed_b, hidden_pre, hidden)

def backward_rows(cotangent, cycle_mask, mixed_b, hidden_pre, hidden, expand, contract):
    chan_count = cotangent.shape[-1]
    masked = (cotangent * cycle_mask.astype(jnp.bfloat16)[:, None, None]).reshape(-1, chan_count)
    grad_reduce = jnp.dot(hidden.T, masked, preferred_element_type=jnp.float32)
    grad_hidden = jnp.dot(masked, contract.T, preferred_element_type=jnp.float32)
    grad_pre = (grad_hidden * gelu_slope(hidden_pre)).astype(jnp.bfloat16)
    grad_expand = jnp.dot(mixed_b.T, grad_pre, preferred_element_type=jnp.float32)
    grad_mixed = masked.astype(jnp.float32) + jnp.dot(grad_pre, expand.T, preferred_element_type=jnp.float32)
    return (grad_mixed, grad_expand, grad_reduce)

def spectral_back(grad_mixed, spectra, filt, forward, inverse, analysis, synthesis, grid_shape):
    row_count, points, chan_count = grid_shape
    order_count = synthesis.shape[0]
    grad_rows = grad_mixed.reshape(grid_shape).astype(jnp.bfloat16)
    grad_values = jnp.einsum('jnc,kn->jkc', grad_rows.astype(jnp.float32), inverse.astype(jnp.float32)).astype(jnp.bfloat16)
    grad_values = grad_values.reshape(row_count, 2, order_count, chan_count)
    grad_filtered = jnp.einsum('tlj,jrtc->trlc', synthesis.astype(jnp.float32), grad_values.astype(jnp.float32))
    filter_real = lax.optimization_barrier(jnp.sum(grad_filtered[:, 0] * spectra[:, 0] + grad_filtered[:, 1] * spectra[:, 1], axis=0))
    filter_imag = lax.optimization_barrier(jnp.sum(grad_filtered[:, 1] * spectra[:, 0] - grad_filtered[:, 0] * spectra[:, 1], axis=0))
    grad_spectra = jnp.stack([filt[0] * grad_filtered[:, 0] + filt[1] * grad_filtered[:, 1], filt[0] * grad_filtered[:, 1] - filt[1] * grad_filtered[:, 0]], axis=1).astype(jnp.bfloat16)
    grad_coeffs = jnp.einsum('tlj,trlc->jrtc', analysis.astype(jnp.float32), grad_spectra.astype(jnp.float32)).astype(jnp.bfloat16)
    grad_coeffs = grad_coeffs.reshape(row_count, 2 * order_count, chan_count)
    grad_tokens = jnp.einsum('jkc,nk->jnc', grad_coeffs.astype(jnp.float32), forward.astype(jnp.float32))
    return (grad_tokens, jnp.stack([filter_real, filter_imag]))

def reference(fresh_input, saved_input, output_grad, expand_weight, reduce_weight, filter_weight, cycle_table):
    order_table = jnp.arange(SLOTS_ALL, dtype=jnp.int32)
    table = legendre(cycle_table, order_table, NLAT)
    analysis = (table * cycle_weights(cycle_table, NLAT)[None, None, :]).astype(jnp.bfloat16)
    synthesis = table.astype(jnp.bfloat16)
    forward, inverse = fourier_tables(order_table, NLAT, NLON)
    cycle_mask = (cycle_table < NLAT).astype(jnp.float32)
    zero_block = jnp.zeros(fresh_input.shape[2:], jnp.bfloat16)
    next_rows = [[zero_block] * GROUPS]
    for section in range(1, SECTIONS):
        members = []
        for member in range(GROUPS):
            tokens = fresh_input[section - 1, member]
            spatial, _ = spectral_pass(tokens, filter_weight[section - 1], forward, analysis, synthesis, inverse)
            members.append(mlp_pass(tokens, spatial, expand_weight[section - 1], reduce_weight[section - 1], cycle_mask)[0])
        next_rows.append(members)
    grad_rows = []
    expand_list, reduce_list, filter_list = ([], [], [])
    for section in range(SECTIONS):
        filt = filter_weight[section]
        expand_total = jnp.zeros(expand_weight.shape[1:], jnp.float32)
        reduce_total = jnp.zeros(reduce_weight.shape[1:], jnp.float32)
        filter_total = jnp.zeros(filter_weight.shape[1:], jnp.float32)
        members = []
        for member in range(GROUPS):
            tokens = saved_input[section, member]
            spatial, spectra = spectral_pass(tokens, filt, forward, analysis, synthesis, inverse)
            _, mixed_b, hidden_pre, hidden = mlp_pass(tokens, spatial, expand_weight[section], reduce_weight[section], cycle_mask)
            grad_mixed, grad_expand, grad_reduce = backward_rows(output_grad[section, member], cycle_mask, mixed_b, hidden_pre, hidden, expand_weight[section], reduce_weight[section])
            grad_tokens, filter_part = spectral_back(grad_mixed, spectra, filt, forward, inverse, analysis, synthesis, tokens.shape)
            members.append(((grad_mixed.reshape(tokens.shape) + grad_tokens) * cycle_mask[:, None, None]).astype(jnp.bfloat16))
            expand_total = expand_total + grad_expand
            reduce_total = reduce_total + grad_reduce
            filter_total = filter_total + filter_part
        if section > 0:
            grad_rows.append(members)
        expand_list.append(expand_total)
        reduce_list.append(reduce_total)
        filter_list.append(filter_total)
    grad_rows.append([zero_block] * GROUPS)
    next_input = jnp.stack([jnp.stack(group_row) for group_row in next_rows])
    input_grad = jnp.stack([jnp.stack(group_row) for group_row in grad_rows])
    return (next_input, input_grad, jnp.stack(expand_list), jnp.stack(reduce_list), jnp.stack(filter_list))
```

```python
import functools
import math

import jax
import jax.numpy as jnp
import numpy as np
from jax import lax
from jax.experimental import pallas as pl
from jax.experimental.pallas import tpu as pltpu
from jax.sharding import Mesh
from jax.sharding import PartitionSpec as P

NLAT = 120
NLON = 240
CH = 128
HID = 768
ROWS = 4
PEERS = 32
LANES = 128
SP = ("sp_0", "sp_1")

ROOT_HALF = 0.7071067811865476
INV_ROOT_TAU = 0.3989422804014327
F32 = jnp.float32
BF16 = jnp.bfloat16


def fourier_constants():
    order = np.arange(128)
    live = (order < NLAT).astype(np.float64)
    value = np.minimum(order, NLAT - 1)
    phase = 2.0 * math.pi / NLON * ((np.arange(NLON)[:, None] * value[None, :]) % NLON)
    scaled = live * (2.0 * math.pi / NLON)
    forward = np.stack([np.cos(phase) * scaled, -np.sin(phase) * scaled], axis=1)
    factor = np.where(value == 0, 1.0, 2.0) * live / (2.0 * math.pi)
    inverse = np.stack([np.cos(phase) * factor, -np.sin(phase) * factor], axis=1)

    def arranged(table):
        table = table.reshape(NLON, 2, PEERS, ROWS).transpose(0, 2, 1, 3)
        return table.reshape(NLON, 256).astype(np.float32).astype(jnp.bfloat16)

    return arranged(forward), arranged(inverse)


def order_constants():
    table = np.zeros((PEERS, 3, 8, LANES), np.float32)
    for position in range(PEERS):
        for row in range(8):
            slot = position * ROWS + row % ROWS
            m = min(slot, NLAT - 1)
            log_start = 0.5 * (
                math.log((2.0 * m + 1.0) / (4.0 * math.pi))
                + math.lgamma(2.0 * m + 1.0)
                - 2.0 * math.lgamma(m + 1.0)
                - m * math.log(4.0)
            )
            table[position, 0, row] = m
            table[position, 1, row] = log_start
            table[position, 2, row] = float(slot < NLAT)
    return table


def tables_kernel(geo_ref, order_ref, ana_ref, syn_ref, work_ref):
    shape = (8, LANES)
    cosine = jnp.broadcast_to(geo_ref[0:1, :], shape)
    log_sine = jnp.broadcast_to(geo_ref[1:2, :], shape)
    weight = geo_ref[2:3, :]
    m = order_ref[0]
    keep = order_ref[2] * jnp.broadcast_to(geo_ref[3:4, :], shape)
    starting = jnp.exp(order_ref[1] + m * log_sine)
    squares = m * m
    previous = jnp.zeros(shape, F32)
    earlier = previous
    for degree in range(NLAT):
        upper = max(4.0 * degree * degree - 1.0, 0.0)
        lower = max(4.0 * (degree - 1.0) ** 2 - 1.0, 1.0)
        ratio_main = jnp.sqrt(upper / jnp.maximum(float(degree * degree) - squares, 1.0))
        ratio_back = jnp.sqrt(jnp.maximum((degree - 1.0) ** 2 - squares, 0.0) / lower)
        rising = ratio_main * (cosine * previous - ratio_back * earlier)
        current = jnp.where(m == float(degree), starting, jnp.where(m < float(degree), rising, 0.0))
        work_ref[degree * 8 : degree * 8 + 8, :] = current * keep
        previous, earlier = current, previous
    work_ref[NLAT * 8 :, :] = jnp.zeros((LANES * 8 - NLAT * 8, LANES), F32)
    for t in range(ROWS):
        table = work_ref[pl.ds(t, LANES, stride=8), :]
        syn_ref[t] = table.astype(BF16)
        ana_ref[t] = (table * weight).astype(BF16)


def to_blocks(out_ref, half, pair):
    blocks = [part.reshape(PEERS, 8, CH) for part in pair]
    out_ref[:, 16 * half : 16 * half + 16, :] = jnp.concatenate(blocks, axis=1).astype(BF16)


def from_blocks(block_ref, half):
    pair = block_ref[:, 16 * half : 16 * half + 16, :].astype(F32)
    return [pair[:, 8 * h : 8 * h + 8].reshape(256, CH).astype(BF16) for h in range(2)]


def matmul(left, right, dims=((1,), (0,))):
    return lax.dot_general(left, right, (dims, ((), ())), preferred_element_type=F32)


def coeffs_kernel(x_ref, forward_ref, out_ref):
    for half in range(2):
        to_blocks(out_ref, half, [matmul(forward_ref[...], x_ref[2 * half + h]) for h in range(2)])


def padded_filter(filt_ref):
    rest = jnp.zeros((LANES - NLAT, CH), F32)
    return [jnp.concatenate([filt_ref[part], rest], axis=0) for part in range(2)]


def spectral_kernel(arrived_ref, ana_ref, syn_ref, filt_ref, out_ref, *rest):
    spectra_ref = rest[0] if len(rest) == 3 else None
    came_ref, goes_ref = rest[-2:]
    came_ref[...] = arrived_ref[...].reshape(LANES * 8, CH).astype(F32)
    real, imag = padded_filter(filt_ref)
    for t in range(ROWS):
        parts = [came_ref[pl.ds(r * ROWS + t, LANES, stride=8), :] for r in range(2)]
        spectra = matmul(ana_ref[t], jnp.concatenate(parts, axis=1).astype(BF16))
        if spectra_ref is not None:
            spectra_ref[t] = spectra
        first, second = spectra[:, :CH], spectra[:, CH:]
        filtered = jnp.concatenate(
            [real * first - imag * second, real * second + imag * first], axis=1
        ).astype(BF16)
        values = matmul(syn_ref[t], filtered, ((0,), (0,)))
        for r in range(2):
            goes_ref[pl.ds(r * ROWS + t, LANES, stride=8), :] = values[:, r * CH : (r + 1) * CH]
    out_ref[...] = goes_ref[...].reshape(PEERS, 32, CH).astype(BF16)


def spectral_back_kernel(
    arrived_ref, spectra_ref, ana_ref, syn_ref, filt_ref, out_ref, grad_ref, came_ref, goes_ref
):
    came_ref[...] = arrived_ref[...].reshape(LANES * 8, CH).astype(F32)
    real, imag = padded_filter(filt_ref)
    total_real = jnp.zeros((LANES, CH), F32)
    total_imag = jnp.zeros((LANES, CH), F32)
    for t in range(ROWS):
        parts = [came_ref[pl.ds(r * ROWS + t, LANES, stride=8), :] for r in range(2)]
        grads = matmul(syn_ref[t], jnp.concatenate(parts, axis=1).astype(BF16))
        first, second = grads[:, :CH], grads[:, CH:]
        spectra = spectra_ref[t]
        s_first, s_second = spectra[:, :CH], spectra[:, CH:]
        total_real = total_real + (first * s_first + second * s_second)
        total_imag = total_imag + (second * s_first - first * s_second)
        grad_spectra = jnp.concatenate(
            [real * first + imag * second, real * second - imag * first], axis=1
        ).astype(BF16)
        coeffs = matmul(ana_ref[t], grad_spectra, ((0,), (0,)))
        for r in range(2):
            goes_ref[pl.ds(r * ROWS + t, LANES, stride=8), :] = coeffs[:, r * CH : (r + 1) * CH]
    out_ref[...] = goes_ref[...].reshape(PEERS, 32, CH).astype(BF16)
    grad_ref[0:LANES, :] = total_real.astype(BF16)
    grad_ref[LANES:, :] = total_imag.astype(BF16)


def live(cycle_ref, j):
    return jnp.where(cycle_ref[j] < NLAT, 1.0, 0.0).astype(F32)


def mlp_kernel(x_ref, values_ref, inverse_ref, expand_ref, reduce_ref, cycle_ref, out_ref):
    for half in range(2):
        values = from_blocks(values_ref, half)
        for h in range(2):
            j = 2 * half + h
            mixed = x_ref[j].astype(F32) + matmul(inverse_ref[...], values[h])
            pre = matmul(mixed.astype(BF16), expand_ref[...])
            hidden = (0.5 * pre * (1.0 + lax.erf(pre * ROOT_HALF))).astype(BF16)
            result = mixed + matmul(hidden, reduce_ref[...])
            out_ref[j] = (result * live(cycle_ref, j)).astype(BF16)


def mlp_back_kernel(
    x_ref,
    values_ref,
    cotangent_ref,
    inverse_ref,
    inverse_t_ref,
    expand_ref,
    reduce_ref,
    cycle_ref,
    out_ref,
    grad_mixed_ref,
    shares_ref,
    mixed_ref,
    masked_ref,
    hidden_ref,
    grad_pre_ref,
):
    for half in range(2):
        values = from_blocks(values_ref, half)
        grad_values = []
        for h in range(2):
            j = 2 * half + h
            rows = slice(j * NLON, (j + 1) * NLON)
            mixed = x_ref[j].astype(F32) + matmul(inverse_ref[...], values[h])
            mixed_b = mixed.astype(BF16)
            masked_f = cotangent_ref[j].astype(F32) * live(cycle_ref, j)
            masked = masked_f.astype(BF16)
            mixed_ref[rows, :] = mixed_b
            masked_ref[rows, :] = masked
            pre = matmul(mixed_b, expand_ref[...])
            normal = 0.5 * (1.0 + lax.erf(pre * ROOT_HALF))
            hidden_ref[rows, :] = (pre * normal).astype(BF16)
            slope = normal + pre * jnp.exp(-0.5 * pre * pre) * INV_ROOT_TAU
            grad_hidden = matmul(masked, reduce_ref[...], ((1,), (1,)))
            grad_pre = (grad_hidden * slope).astype(BF16)
            grad_pre_ref[rows, :] = grad_pre
            grad_mixed = masked_f + matmul(grad_pre, expand_ref[...], ((1,), (1,)))
            grad_mixed_ref[j] = grad_mixed
            grad_values.append(matmul(inverse_t_ref[...], grad_mixed.astype(BF16)))
        to_blocks(out_ref, half, grad_values)
    expand_grad = matmul(grad_pre_ref[...], mixed_ref[...], ((0,), (0,))).astype(BF16)
    reduce_grad = matmul(hidden_ref[...], masked_ref[...], ((0,), (0,))).astype(BF16)
    part = HID // 4
    for d in range(4):
        shares_ref[d, :part, :] = expand_grad[d * part : (d + 1) * part]
        shares_ref[d, part:, :] = reduce_grad[d * part : (d + 1) * part]


def input_grad_kernel(coeffs_ref, grad_mixed_ref, forward_ref, cycle_ref, out_ref):
    for half in range(2):
        values = from_blocks(coeffs_ref, half)
        for h in range(2):
            j = 2 * half + h
            total = grad_mixed_ref[j] + matmul(forward_ref[...], values[h])
            out_ref[j] = (total * live(cycle_ref, j)).astype(BF16)


def call(kernel, outs, args, scratch=(), flops=0, transcendentals=0, smem=()):
    specs = [
        pl.BlockSpec(memory_space=pltpu.SMEM if n in smem else pltpu.VMEM) for n in range(len(args))
    ]
    moved = sum(a.size * a.dtype.itemsize for a in (*args, *outs))
    return pl.pallas_call(
        kernel,
        out_shape=outs,
        in_specs=specs,
        out_specs=[pl.BlockSpec(memory_space=pltpu.VMEM)] * len(outs),
        scratch_shapes=list(scratch),
        compiler_params=pltpu.CompilerParams(vmem_limit_bytes=24 * 1024 * 1024),
        cost_estimate=pl.CostEstimate(
            flops=flops, bytes_accessed=moved, transcendentals=transcendentals
        ),
    )(*args)


BLOCKS = jax.ShapeDtypeStruct((PEERS, 32, CH), BF16)
TOKENS = jax.ShapeDtypeStruct((ROWS, NLON, CH), BF16)
SPECTRAL_SCRATCH = (pltpu.VMEM((LANES * 8, CH), F32), pltpu.VMEM((LANES * 8, CH), F32))


def exchange(blocks, axes):
    return lax.all_to_all(blocks, axes, split_axis=0, concat_axis=0, tiled=True)


def spread(block, axes, peers):
    return exchange(jnp.broadcast_to(block[None], (peers, *block.shape)), axes)


def total(blocks):
    return blocks.astype(F32).sum(axis=0)


def from_behind(block, axis, distance):
    devices = range(lax.axis_size(axis))
    route = [(i - distance, i) for i in devices if i - distance in devices]
    return lax.ppermute(block, axis, route)


def filter_total(part):
    halves = total(exchange(part.reshape(2, 128, CH), "sp_1"))
    quarters = total(exchange(halves.astype(BF16).reshape(4, 32, CH), "dp"))
    own = total(spread(quarters.astype(BF16), "sp_0", 16))
    return spread(own, ("sp_1", "dp"), 8).reshape(2, 128, CH)[:, :NLAT]


def share_total(shares):
    rows = 2 * HID // 4
    own = total(exchange(shares, "dp")).astype(BF16)
    piece = total(exchange(own.reshape(PEERS, rows // PEERS, CH), SP)).astype(BF16)
    both = spread(piece, SP, PEERS).astype(F32).reshape(2, HID // 4, CH)
    return both[0].T, both[1]


def on_device(
    forward_np,
    inverse_np,
    orders_np,
    fresh_input,
    saved_input,
    output_grad,
    expand_weight,
    reduce_weight,
    filter_weight,
    cycle_table,
):
    position = lax.axis_index(SP)
    fresh, saved, cotangent = fresh_input[0, 0], saved_input[0, 0], output_grad[0, 0]
    expand, contract, filt = expand_weight[0], reduce_weight[0], filter_weight[0]
    forward = jnp.asarray(forward_np)
    forward_t = jnp.asarray(np.ascontiguousarray(forward_np.T))
    inverse = jnp.asarray(inverse_np)
    inverse_t = jnp.asarray(np.ascontiguousarray(inverse_np.T))
    own_cycles = lax.dynamic_slice_in_dim(cycle_table, position * ROWS, ROWS)
    dft = 2 * ROWS * 256 * NLON * CH
    leg = 2 * 16 * 128 * 128 * CH
    mlp = 2 * ROWS * NLON * CH * HID

    saved_blocks = call(coeffs_kernel, [BLOCKS], [saved, forward_t], flops=dft)[0]
    saved_at_orders = exchange(saved_blocks, SP)
    fresh_blocks = call(coeffs_kernel, [BLOCKS], [fresh, forward_t], flops=dft)[0]
    fresh_at_orders = exchange(fresh_blocks, SP)

    lat_live = (cycle_table < NLAT).astype(F32)
    colatitude = math.pi * (jnp.minimum(cycle_table, NLAT - 1).astype(F32) + 0.5) / NLAT
    sine = jnp.sin(colatitude)
    geo = jnp.stack(
        [jnp.cos(colatitude), jnp.log(sine), math.pi / NLAT * sine * lat_live, lat_live]
    )
    order_rows = lax.dynamic_index_in_dim(jnp.asarray(orders_np), position, 0, keepdims=False)
    tables = jax.ShapeDtypeStruct((ROWS, LANES, LANES), BF16)
    ana, syn = call(
        tables_kernel,
        [tables, tables],
        [geo, order_rows],
        [pltpu.VMEM((LANES * 8, LANES), F32)],
        flops=4_000_000,
    )

    spectra_shape = jax.ShapeDtypeStruct((ROWS, LANES, 2 * CH), F32)
    saved_values, spectra = call(
        spectral_kernel,
        [BLOCKS, spectra_shape],
        [saved_at_orders, ana, syn, filt],
        SPECTRAL_SCRATCH,
        flops=leg,
    )
    saved_at_cycles = exchange(saved_values, SP)
    fresh_values = call(
        spectral_kernel, [BLOCKS], [fresh_at_orders, ana, syn, filt], SPECTRAL_SCRATCH, flops=leg
    )[0]
    fresh_at_cycles = exchange(fresh_values, SP)

    grad_values, grad_mixed, shares = call(
        mlp_back_kernel,
        [
            BLOCKS,
            jax.ShapeDtypeStruct((ROWS, NLON, CH), F32),
            jax.ShapeDtypeStruct((4, 2 * HID // 4, CH), BF16),
        ],
        [saved, saved_at_cycles, cotangent, inverse, inverse_t, expand, contract, own_cycles],
        [
            pltpu.VMEM((ROWS * NLON, CH), BF16),
            pltpu.VMEM((ROWS * NLON, CH), BF16),
            pltpu.VMEM((ROWS * NLON, HID), BF16),
            pltpu.VMEM((ROWS * NLON, HID), BF16),
        ],
        flops=5 * mlp + 2 * dft,
        transcendentals=2 * ROWS * NLON * HID,
        smem=(7,),
    )
    grads_at_orders = exchange(grad_values, SP)
    block = call(
        mlp_kernel,
        [TOKENS],
        [fresh, fresh_at_cycles, inverse, expand, contract, own_cycles],
        flops=2 * mlp + dft,
        transcendentals=ROWS * NLON * HID,
        smem=(5,),
    )[0]
    next_input = from_behind(block[None, None], "pipe", 1)
    expand_grad, reduce_grad = share_total(shares)

    grad_coeffs, filter_part = call(
        spectral_back_kernel,
        [BLOCKS, jax.ShapeDtypeStruct((256, CH), BF16)],
        [grads_at_orders, spectra, ana, syn, filt],
        SPECTRAL_SCRATCH,
        flops=leg,
    )
    coeffs_at_cycles = exchange(grad_coeffs, SP)
    filter_grad = filter_total(filter_part)
    input_grad = call(
        input_grad_kernel,
        [TOKENS],
        [coeffs_at_cycles, grad_mixed, forward, own_cycles],
        flops=dft,
        smem=(3,),
    )[0]
    sent_back = from_behind(input_grad[None, None], "pipe", -1)
    return (next_input, sent_back, expand_grad[None], reduce_grad[None], filter_grad[None])


def solution(mesh):
    finer = Mesh(
        mesh.devices.reshape(mesh.shape["pipe"], 16, 2, mesh.shape["dp"]),
        ("pipe", "sp_0", "sp_1", "dp"),
    )
    in_specs = (
        P("pipe", "dp", SP, None, None),
        P("pipe", "dp", SP, None, None),
        P("pipe", "dp", SP, None, None),
        P("pipe", None, None),
        P("pipe", None, None),
        P("pipe", None, None, None),
        P(),
    )
    out_specs = (
        P("pipe", "dp", SP, None, None),
        P("pipe", "dp", SP, None, None),
        P("pipe", None, "dp"),
        P("pipe", "dp", None),
        P("pipe", None, None, None),
    )
    forward, inverse = fourier_constants()
    program = functools.partial(on_device, forward, inverse, order_constants())
    return jax.shard_map(
        program, mesh=finer, in_specs=in_specs, out_specs=out_specs, check_vma=False
    )
```

```python
import functools
import math

import jax
import jax.numpy as jnp
import numpy as np
from jax import lax
from jax.experimental import pallas as pl
from jax.experimental.pallas import tpu as pltpu
from jax.sharding import Mesh
from jax.sharding import PartitionSpec as P

NLAT = 120
NLON = 240
CH = 128
HID = 768
ROWS = 4
PEERS = 32
LANES = 128
SP = ("sp_0", "sp_1")

ROOT_HALF = 0.7071067811865476
INV_ROOT_TAU = 0.3989422804014327
F32 = jnp.float32
BF16 = jnp.bfloat16


def fourier_constants():
    order = np.arange(128)
    live = (order < NLAT).astype(np.float64)
    value = np.minimum(order, NLAT - 1)
    phase = 2.0 * math.pi / NLON * ((np.arange(NLON)[:, None] * value[None, :]) % NLON)
    scaled = live * (2.0 * math.pi / NLON)
    forward = np.stack([np.cos(phase) * scaled, -np.sin(phase) * scaled], axis=1)
    factor = np.where(value == 0, 1.0, 2.0) * live / (2.0 * math.pi)
    inverse = np.stack([np.cos(phase) * factor, -np.sin(phase) * factor], axis=1)

    def arranged(table):
        table = table.reshape(NLON, 2, PEERS, ROWS).transpose(0, 2, 1, 3)
        return table.reshape(NLON, 256).astype(np.float32).astype(jnp.bfloat16)

    return arranged(forward), arranged(inverse)


def order_constants():
    table = np.zeros((PEERS, 3, 8, LANES), np.float32)
    for position in range(PEERS):
        for row in range(8):
            slot = position * ROWS + row % ROWS
            m = min(slot, NLAT - 1)
            log_start = 0.5 * (
                math.log((2.0 * m + 1.0) / (4.0 * math.pi))
                + math.lgamma(2.0 * m + 1.0)
                - 2.0 * math.lgamma(m + 1.0)
                - m * math.log(4.0)
            )
            table[position, 0, row] = m
            table[position, 1, row] = log_start
            table[position, 2, row] = float(slot < NLAT)
    return table


def tables_kernel(geo_ref, order_ref, ana_ref, syn_ref, work_ref):
    shape = (8, LANES)
    cosine = jnp.broadcast_to(geo_ref[0:1, :], shape)
    log_sine = jnp.broadcast_to(geo_ref[1:2, :], shape)
    weight = geo_ref[2:3, :]
    m = order_ref[0]
    keep = order_ref[2] * jnp.broadcast_to(geo_ref[3:4, :], shape)
    starting = jnp.exp(order_ref[1] + m * log_sine)
    squares = m * m
    previous = jnp.zeros(shape, F32)
    earlier = previous
    for degree in range(NLAT):
        upper = max(4.0 * degree * degree - 1.0, 0.0)
        lower = max(4.0 * (degree - 1.0) ** 2 - 1.0, 1.0)
        ratio_main = jnp.sqrt(upper / jnp.maximum(float(degree * degree) - squares, 1.0))
        ratio_back = jnp.sqrt(jnp.maximum((degree - 1.0) ** 2 - squares, 0.0) / lower)
        rising = ratio_main * (cosine * previous - ratio_back * earlier)
        current = jnp.where(m == float(degree), starting, jnp.where(m < float(degree), rising, 0.0))
        work_ref[degree * 8 : degree * 8 + 8, :] = current * keep
        previous, earlier = current, previous
    work_ref[NLAT * 8 :, :] = jnp.zeros((LANES * 8 - NLAT * 8, LANES), F32)
    for t in range(ROWS):
        table = work_ref[pl.ds(t, LANES, stride=8), :]
        syn_ref[t] = table.astype(BF16)
        ana_ref[t] = (table * weight).astype(BF16)


def to_blocks(out_ref, half, pair):
    blocks = [part.reshape(PEERS, 8, CH) for part in pair]
    out_ref[:, 16 * half : 16 * half + 16, :] = jnp.concatenate(blocks, axis=1).astype(BF16)


def from_blocks(block_ref, half):
    pair = block_ref[:, 16 * half : 16 * half + 16, :].astype(F32)
    return [pair[:, 8 * h : 8 * h + 8].reshape(256, CH).astype(BF16) for h in range(2)]


def matmul(left, right, dims=((1,), (0,))):
    return lax.dot_general(left, right, (dims, ((), ())), preferred_element_type=F32)


def coeffs_kernel(x_ref, forward_ref, out_ref):
    for half in range(2):
        to_blocks(out_ref, half, [matmul(forward_ref[...], x_ref[2 * half + h]) for h in range(2)])


def padded_filter(filt_ref):
    rest = jnp.zeros((LANES - NLAT, CH), F32)
    return [jnp.concatenate([filt_ref[part], rest], axis=0) for part in range(2)]


def spectral(came_ref, goes_ref, ana_ref, syn_ref, filt_ref, spectra_ref=None):
    real, imag = padded_filter(filt_ref)
    for t in range(ROWS):
        parts = [came_ref[pl.ds(r * ROWS + t, LANES, stride=8), :] for r in range(2)]
        spectra = matmul(ana_ref[t], jnp.concatenate(parts, axis=1).astype(BF16))
        if spectra_ref is not None:
            spectra_ref[t] = spectra
        first, second = spectra[:, :CH], spectra[:, CH:]
        filtered = jnp.concatenate(
            [real * first - imag * second, real * second + imag * first], axis=1
        ).astype(BF16)
        values = matmul(syn_ref[t], filtered, ((0,), (0,)))
        for r in range(2):
            goes_ref[pl.ds(r * ROWS + t, LANES, stride=8), :] = values[:, r * CH : (r + 1) * CH]


def saved_spectral_kernel(
    arrived_ref, ana_ref, syn_ref, filt_ref, beside_ref, out_ref, spectra_ref, came_ref, goes_ref
):
    out_ref[:, 32:, :] = beside_ref[...]
    came_ref[...] = arrived_ref[...].reshape(LANES * 8, CH).astype(F32)
    spectral(came_ref, goes_ref, ana_ref, syn_ref, filt_ref, spectra_ref)
    out_ref[:, :32, :] = goes_ref[...].reshape(PEERS, 32, CH).astype(BF16)


def fresh_spectral_kernel(arrived_ref, ana_ref, syn_ref, filt_ref, out_ref, came_ref, goes_ref):
    came_ref[...] = arrived_ref[:, 32:, :].reshape(LANES * 8, CH).astype(F32)
    spectral(came_ref, goes_ref, ana_ref, syn_ref, filt_ref)
    out_ref[...] = goes_ref[...].reshape(PEERS, 32, CH).astype(BF16)


def spectral_back_kernel(
    arrived_ref,
    spectra_ref,
    ana_ref,
    syn_ref,
    filt_ref,
    beside_ref,
    out_ref,
    grad_ref,
    came_ref,
    goes_ref,
):
    out_ref[:, 32:, :] = beside_ref[...]
    came_ref[...] = arrived_ref[...].reshape(LANES * 8, CH).astype(F32)
    real, imag = padded_filter(filt_ref)
    total_real = jnp.zeros((LANES, CH), F32)
    total_imag = jnp.zeros((LANES, CH), F32)
    for t in range(ROWS):
        parts = [came_ref[pl.ds(r * ROWS + t, LANES, stride=8), :] for r in range(2)]
        grads = matmul(syn_ref[t], jnp.concatenate(parts, axis=1).astype(BF16))
        first, second = grads[:, :CH], grads[:, CH:]
        spectra = spectra_ref[t]
        s_first, s_second = spectra[:, :CH], spectra[:, CH:]
        total_real = total_real + (first * s_first + second * s_second)
        total_imag = total_imag + (second * s_first - first * s_second)
        grad_spectra = jnp.concatenate(
            [real * first + imag * second, real * second - imag * first], axis=1
        ).astype(BF16)
        coeffs = matmul(ana_ref[t], grad_spectra, ((0,), (0,)))
        for r in range(2):
            goes_ref[pl.ds(r * ROWS + t, LANES, stride=8), :] = coeffs[:, r * CH : (r + 1) * CH]
    out_ref[:, :32, :] = goes_ref[...].reshape(PEERS, 32, CH).astype(BF16)
    grad_ref[:NLAT, :] = total_real[:NLAT]
    grad_ref[NLAT:, :] = total_imag[:NLAT]


def live(cycle_ref, j):
    return jnp.where(cycle_ref[j] < NLAT, 1.0, 0.0).astype(F32)


def mlp_kernel(x_ref, values_ref, inverse_ref, expand_ref, reduce_ref, cycle_ref, out_ref):
    for half in range(2):
        values = from_blocks(values_ref, 2 + half)
        for h in range(2):
            j = 2 * half + h
            mixed = x_ref[j].astype(F32) + matmul(inverse_ref[...], values[h])
            pre = matmul(mixed.astype(BF16), expand_ref[...])
            hidden = (0.5 * pre * (1.0 + lax.erf(pre * ROOT_HALF))).astype(BF16)
            result = mixed + matmul(hidden, reduce_ref[...])
            out_ref[j] = (result * live(cycle_ref, j)).astype(BF16)


def mlp_back_kernel(
    x_ref,
    values_ref,
    cotangent_ref,
    inverse_ref,
    inverse_t_ref,
    expand_ref,
    reduce_ref,
    cycle_ref,
    out_ref,
    grad_mixed_ref,
    shares_ref,
    mixed_ref,
    masked_ref,
    hidden_ref,
    grad_pre_ref,
):
    for half in range(2):
        values = from_blocks(values_ref, half)
        grad_values = []
        for h in range(2):
            j = 2 * half + h
            rows = slice(j * NLON, (j + 1) * NLON)
            mixed = x_ref[j].astype(F32) + matmul(inverse_ref[...], values[h])
            mixed_b = mixed.astype(BF16)
            masked_f = cotangent_ref[j].astype(F32) * live(cycle_ref, j)
            masked = masked_f.astype(BF16)
            mixed_ref[rows, :] = mixed_b
            masked_ref[rows, :] = masked
            pre = matmul(mixed_b, expand_ref[...])
            normal = 0.5 * (1.0 + lax.erf(pre * ROOT_HALF))
            hidden_ref[rows, :] = (pre * normal).astype(BF16)
            slope = normal + pre * jnp.exp(-0.5 * pre * pre) * INV_ROOT_TAU
            grad_hidden = matmul(masked, reduce_ref[...], ((1,), (1,)))
            grad_pre = (grad_hidden * slope).astype(BF16)
            grad_pre_ref[rows, :] = grad_pre
            grad_mixed = masked_f + matmul(grad_pre, expand_ref[...], ((1,), (1,)))
            grad_mixed_ref[j] = grad_mixed
            grad_values.append(matmul(inverse_t_ref[...], grad_mixed.astype(BF16)))
        to_blocks(out_ref, half, grad_values)
    expand_grad = matmul(grad_pre_ref[...], mixed_ref[...], ((0,), (0,))).astype(BF16)
    reduce_grad = matmul(hidden_ref[...], masked_ref[...], ((0,), (0,))).astype(BF16)
    part = HID // 4
    for d in range(4):
        shares_ref[d, :part, :] = expand_grad[d * part : (d + 1) * part]
        shares_ref[d, part:, :] = reduce_grad[d * part : (d + 1) * part]


def input_grad_kernel(coeffs_ref, grad_mixed_ref, forward_ref, cycle_ref, out_ref):
    for half in range(2):
        values = from_blocks(coeffs_ref, half)
        for h in range(2):
            j = 2 * half + h
            total = grad_mixed_ref[j] + matmul(forward_ref[...], values[h])
            out_ref[j] = (total * live(cycle_ref, j)).astype(BF16)


def call(kernel, outs, args, scratch=(), flops=0, transcendentals=0, smem=()):
    specs = [
        pl.BlockSpec(memory_space=pltpu.SMEM if n in smem else pltpu.VMEM) for n in range(len(args))
    ]
    moved = sum(a.size * a.dtype.itemsize for a in (*args, *outs))
    return pl.pallas_call(
        kernel,
        out_shape=outs,
        in_specs=specs,
        out_specs=[pl.BlockSpec(memory_space=pltpu.VMEM)] * len(outs),
        scratch_shapes=list(scratch),
        compiler_params=pltpu.CompilerParams(vmem_limit_bytes=24 * 1024 * 1024),
        cost_estimate=pl.CostEstimate(
            flops=flops, bytes_accessed=moved, transcendentals=transcendentals
        ),
    )(*args)


PAIRED = jax.ShapeDtypeStruct((PEERS, 64, CH), BF16)
BLOCKS = jax.ShapeDtypeStruct((PEERS, 32, CH), BF16)
TOKENS = jax.ShapeDtypeStruct((ROWS, NLON, CH), BF16)
SPECTRAL_SCRATCH = (pltpu.VMEM((LANES * 8, CH), F32), pltpu.VMEM((LANES * 8, CH), F32))


def exchange(blocks, axes):
    return lax.all_to_all(blocks, axes, split_axis=0, concat_axis=0, tiled=True)


def spread(block, axes, peers):
    return exchange(jnp.broadcast_to(block[None], (peers, *block.shape)), axes)


def total(blocks):
    return blocks.astype(F32).sum(axis=0)


def from_behind(block, axis, distance):
    devices = range(lax.axis_size(axis))
    route = [(i - distance, i) for i in devices if i - distance in devices]
    return lax.ppermute(block, axis, route)


def around(block, axis, distance):
    count = lax.axis_size(axis)
    return lax.ppermute(block, axis, [(i, (i + distance) % count) for i in range(count)])


def scattered_total(blocks, axis):
    count = lax.axis_size(axis)
    me = lax.axis_index(axis)

    def block_of(distance):
        return lax.dynamic_index_in_dim(blocks, (me + distance) % count, 0, keepdims=False)

    came = [around(block_of(k), axis, k) for k in range(1, count)]
    return sum((block.astype(F32) for block in came), block_of(0).astype(F32))


def shares_half(shares):
    own = scattered_total(shares, "dp").astype(BF16)
    return scattered_total(own.reshape(2, HID // 4, CH), "sp_1").astype(BF16)


def gradient_totals(half, filter_part):
    rows = HID // 4
    quarter = scattered_total(filter_part.reshape(4, NLAT // 2, CH), "dp").astype(BF16)
    mine = total(lax.all_gather(jnp.concatenate([half, quarter]), "sp_0"))
    other = around(mine, "sp_1", 1)
    first = lax.axis_index("sp_1") == 0
    filter_own = mine[rows:] + other[rows:]
    filter_grad = spread(filter_own, "dp", 4).reshape(2, NLAT, CH)
    expand_grad = jnp.where(first, mine[:rows], other[:rows]).T
    return expand_grad, jnp.where(first, other[:rows], mine[:rows]), filter_grad


def on_device(
    forward_np,
    inverse_np,
    orders_np,
    fresh_input,
    saved_input,
    output_grad,
    expand_weight,
    reduce_weight,
    filter_weight,
    cycle_table,
):
    position = lax.axis_index(SP)
    fresh, saved, cotangent = fresh_input[0, 0], saved_input[0, 0], output_grad[0, 0]
    expand, contract, filt = expand_weight[0], reduce_weight[0], filter_weight[0]
    forward = jnp.asarray(forward_np)
    forward_t = jnp.asarray(np.ascontiguousarray(forward_np.T))
    inverse = jnp.asarray(inverse_np)
    inverse_t = jnp.asarray(np.ascontiguousarray(inverse_np.T))
    own_cycles = lax.dynamic_slice_in_dim(cycle_table, position * ROWS, ROWS)
    dft = 2 * ROWS * 256 * NLON * CH
    leg = 2 * 16 * 128 * 128 * CH
    mlp = 2 * ROWS * NLON * CH * HID

    saved_blocks = call(coeffs_kernel, [BLOCKS], [saved, forward_t], flops=dft)[0]
    saved_at_orders = exchange(saved_blocks, SP)
    fresh_blocks = call(coeffs_kernel, [BLOCKS], [fresh, forward_t], flops=dft)[0]

    lat_live = (cycle_table < NLAT).astype(F32)
    colatitude = math.pi * (jnp.minimum(cycle_table, NLAT - 1).astype(F32) + 0.5) / NLAT
    sine = jnp.sin(colatitude)
    geo = jnp.stack(
        [jnp.cos(colatitude), jnp.log(sine), math.pi / NLAT * sine * lat_live, lat_live]
    )
    order_rows = lax.dynamic_index_in_dim(jnp.asarray(orders_np), position, 0, keepdims=False)
    tables = jax.ShapeDtypeStruct((ROWS, LANES, LANES), BF16)
    ana, syn = call(
        tables_kernel,
        [tables, tables],
        [geo, order_rows],
        [pltpu.VMEM((LANES * 8, LANES), F32)],
        flops=4_000_000,
    )

    spectra_shape = jax.ShapeDtypeStruct((ROWS, LANES, 2 * CH), F32)
    values_fresh, spectra = call(
        saved_spectral_kernel,
        [PAIRED, spectra_shape],
        [saved_at_orders, ana, syn, filt, fresh_blocks],
        SPECTRAL_SCRATCH,
        flops=leg,
    )
    values_fresh = exchange(values_fresh, SP)

    grad_values, grad_mixed, shares = call(
        mlp_back_kernel,
        [
            BLOCKS,
            jax.ShapeDtypeStruct((ROWS, NLON, CH), F32),
            jax.ShapeDtypeStruct((4, 2 * HID // 4, CH), BF16),
        ],
        [saved, values_fresh, cotangent, inverse, inverse_t, expand, contract, own_cycles],
        [
            pltpu.VMEM((ROWS * NLON, CH), BF16),
            pltpu.VMEM((ROWS * NLON, CH), BF16),
            pltpu.VMEM((ROWS * NLON, HID), BF16),
            pltpu.VMEM((ROWS * NLON, HID), BF16),
        ],
        flops=5 * mlp + 2 * dft,
        transcendentals=2 * ROWS * NLON * HID,
        smem=(7,),
    )
    grads_at_orders = exchange(grad_values, SP)
    fresh_values = call(
        fresh_spectral_kernel, [BLOCKS], [values_fresh, ana, syn, filt], SPECTRAL_SCRATCH, flops=leg
    )[0]
    half = shares_half(shares)

    coeffs_fresh, filter_part = call(
        spectral_back_kernel,
        [PAIRED, jax.ShapeDtypeStruct((2 * NLAT, CH), F32)],
        [grads_at_orders, spectra, ana, syn, filt, fresh_values],
        SPECTRAL_SCRATCH,
        flops=leg,
    )
    coeffs_fresh = exchange(coeffs_fresh, SP)
    expand_grad, reduce_grad, filter_grad = gradient_totals(half, filter_part)
    input_grad = call(
        input_grad_kernel,
        [TOKENS],
        [coeffs_fresh, grad_mixed, forward, own_cycles],
        flops=dft,
        smem=(3,),
    )[0]
    sent_back = from_behind(input_grad[None, None], "pipe", -1)
    block = call(
        mlp_kernel,
        [TOKENS],
        [fresh, coeffs_fresh, inverse, expand, contract, own_cycles],
        flops=2 * mlp + dft,
        transcendentals=ROWS * NLON * HID,
        smem=(5,),
    )[0]
    next_input = from_behind(block[None, None], "pipe", 1)
    return (next_input, sent_back, expand_grad[None], reduce_grad[None], filter_grad[None])


def solution(mesh):
    finer = Mesh(
        mesh.devices.reshape(mesh.shape["pipe"], 16, 2, mesh.shape["dp"]),
        ("pipe", "sp_0", "sp_1", "dp"),
    )
    in_specs = (
        P("pipe", "dp", SP, None, None),
        P("pipe", "dp", SP, None, None),
        P("pipe", "dp", SP, None, None),
        P("pipe", None, None),
        P("pipe", None, None),
        P("pipe", None, None, None),
        P(),
    )
    out_specs = (
        P("pipe", "dp", SP, None, None),
        P("pipe", "dp", SP, None, None),
        P("pipe", None, "dp"),
        P("pipe", "dp", None),
        P("pipe", None, None, None),
    )
    forward, inverse = fourier_constants()
    program = functools.partial(on_device, forward, inverse, order_constants())
    return jax.shard_map(
        program, mesh=finer, in_specs=in_specs, out_specs=out_specs, check_vma=False
    )
```

```python
import functools
import math

import jax
import jax.numpy as jnp
import numpy as np
from jax import lax
from jax.experimental import pallas as pl
from jax.experimental.pallas import tpu as pltpu
from jax.sharding import Mesh
from jax.sharding import PartitionSpec as P

NLAT = 120
NLON = 240
CH = 128
HID = 768
ROWS = 4
PEERS = 32
LANES = 128
SP = ("sp_0", "sp_1")

ROOT_HALF = 0.7071067811865476
INV_ROOT_TAU = 0.3989422804014327
F32 = jnp.float32
BF16 = jnp.bfloat16


def fourier_constants():
    order = np.arange(128)
    live = (order < NLAT).astype(np.float64)
    value = np.minimum(order, NLAT - 1)
    phase = 2.0 * math.pi / NLON * ((np.arange(NLON)[:, None] * value[None, :]) % NLON)
    scaled = live * (2.0 * math.pi / NLON)
    forward = np.stack([np.cos(phase) * scaled, -np.sin(phase) * scaled], axis=1)
    factor = np.where(value == 0, 1.0, 2.0) * live / (2.0 * math.pi)
    inverse = np.stack([np.cos(phase) * factor, -np.sin(phase) * factor], axis=1)

    def arranged(table):
        table = table.reshape(NLON, 2, PEERS, ROWS).transpose(0, 2, 1, 3)
        return table.reshape(NLON, 256).astype(np.float32).astype(jnp.bfloat16)

    return arranged(forward), arranged(inverse)


def order_constants():
    table = np.zeros((PEERS, 3, 8, LANES), np.float32)
    for position in range(PEERS):
        for row in range(8):
            slot = position * ROWS + row % ROWS
            m = min(slot, NLAT - 1)
            log_start = 0.5 * (
                math.log((2.0 * m + 1.0) / (4.0 * math.pi))
                + math.lgamma(2.0 * m + 1.0)
                - 2.0 * math.lgamma(m + 1.0)
                - m * math.log(4.0)
            )
            table[position, 0, row] = m
            table[position, 1, row] = log_start
            table[position, 2, row] = float(slot < NLAT)
    return table


def tables_kernel(geo_ref, order_ref, ana_ref, syn_ref, work_ref):
    shape = (8, LANES)
    cosine = jnp.broadcast_to(geo_ref[0:1, :], shape)
    log_sine = jnp.broadcast_to(geo_ref[1:2, :], shape)
    weight = geo_ref[2:3, :]
    m = order_ref[0]
    keep = order_ref[2] * jnp.broadcast_to(geo_ref[3:4, :], shape)
    starting = jnp.exp(order_ref[1] + m * log_sine)
    squares = m * m
    previous = jnp.zeros(shape, F32)
    earlier = previous
    for degree in range(NLAT):
        upper = max(4.0 * degree * degree - 1.0, 0.0)
        lower = max(4.0 * (degree - 1.0) ** 2 - 1.0, 1.0)
        ratio_main = jnp.sqrt(upper / jnp.maximum(float(degree * degree) - squares, 1.0))
        ratio_back = jnp.sqrt(jnp.maximum((degree - 1.0) ** 2 - squares, 0.0) / lower)
        rising = ratio_main * (cosine * previous - ratio_back * earlier)
        current = jnp.where(m == float(degree), starting, jnp.where(m < float(degree), rising, 0.0))
        work_ref[degree * 8 : degree * 8 + 8, :] = current * keep
        previous, earlier = current, previous
    work_ref[NLAT * 8 :, :] = jnp.zeros((LANES * 8 - NLAT * 8, LANES), F32)
    for t in range(ROWS):
        table = work_ref[pl.ds(t, LANES, stride=8), :]
        syn_ref[t] = table.astype(BF16)
        ana_ref[t] = (table * weight).astype(BF16)


def to_blocks(out_ref, half, pair):
    blocks = [part.reshape(PEERS, 8, CH) for part in pair]
    out_ref[:, 16 * half : 16 * half + 16, :] = jnp.concatenate(blocks, axis=1).astype(BF16)


def from_blocks(block_ref, half):
    pair = block_ref[:, 16 * half : 16 * half + 16, :].astype(F32)
    return [pair[:, 8 * h : 8 * h + 8].reshape(256, CH).astype(BF16) for h in range(2)]


def matmul(left, right, dims=((1,), (0,))):
    return lax.dot_general(left, right, (dims, ((), ())), preferred_element_type=F32)


def coeffs_kernel(x_ref, forward_ref, out_ref):
    for half in range(2):
        to_blocks(out_ref, half, [matmul(forward_ref[...], x_ref[2 * half + h]) for h in range(2)])


def padded_filter(filt_ref):
    rest = jnp.zeros((LANES - NLAT, CH), F32)
    return [jnp.concatenate([filt_ref[part], rest], axis=0) for part in range(2)]


def spectral(came_ref, goes_ref, ana_ref, syn_ref, filt_ref, spectra_ref=None):
    real, imag = padded_filter(filt_ref)
    for t in range(ROWS):
        parts = [came_ref[pl.ds(r * ROWS + t, LANES, stride=8), :] for r in range(2)]
        spectra = matmul(ana_ref[t], jnp.concatenate(parts, axis=1).astype(BF16))
        if spectra_ref is not None:
            spectra_ref[t] = spectra
        first, second = spectra[:, :CH], spectra[:, CH:]
        filtered = jnp.concatenate(
            [real * first - imag * second, real * second + imag * first], axis=1
        ).astype(BF16)
        values = matmul(syn_ref[t], filtered, ((0,), (0,)))
        for r in range(2):
            goes_ref[pl.ds(r * ROWS + t, LANES, stride=8), :] = values[:, r * CH : (r + 1) * CH]


def saved_spectral_kernel(
    arrived_ref, ana_ref, syn_ref, filt_ref, beside_ref, out_ref, spectra_ref, came_ref, goes_ref
):
    out_ref[:, 32:, :] = beside_ref[...]
    came_ref[...] = arrived_ref[...].reshape(LANES * 8, CH).astype(F32)
    spectral(came_ref, goes_ref, ana_ref, syn_ref, filt_ref, spectra_ref)
    out_ref[:, :32, :] = goes_ref[...].reshape(PEERS, 32, CH).astype(BF16)


def fresh_spectral_kernel(arrived_ref, ana_ref, syn_ref, filt_ref, out_ref, came_ref, goes_ref):
    came_ref[...] = arrived_ref[:, 32:, :].reshape(LANES * 8, CH).astype(F32)
    spectral(came_ref, goes_ref, ana_ref, syn_ref, filt_ref)
    out_ref[...] = goes_ref[...].reshape(PEERS, 32, CH).astype(BF16)


def spectral_back_kernel(
    arrived_ref,
    spectra_ref,
    ana_ref,
    syn_ref,
    filt_ref,
    beside_ref,
    shares_ref,
    out_ref,
    grad_ref,
    came_ref,
    goes_ref,
):
    out_ref[:, 32:64, :] = beside_ref[...]
    out_ref[:, 64:, :] = shares_ref[...]
    came_ref[...] = arrived_ref[...].reshape(LANES * 8, CH).astype(F32)
    real, imag = padded_filter(filt_ref)
    total_real = jnp.zeros((LANES, CH), F32)
    total_imag = jnp.zeros((LANES, CH), F32)
    for t in range(ROWS):
        parts = [came_ref[pl.ds(r * ROWS + t, LANES, stride=8), :] for r in range(2)]
        grads = matmul(syn_ref[t], jnp.concatenate(parts, axis=1).astype(BF16))
        first, second = grads[:, :CH], grads[:, CH:]
        spectra = spectra_ref[t]
        s_first, s_second = spectra[:, :CH], spectra[:, CH:]
        total_real = total_real + (first * s_first + second * s_second)
        total_imag = total_imag + (second * s_first - first * s_second)
        grad_spectra = jnp.concatenate(
            [real * first + imag * second, real * second - imag * first], axis=1
        ).astype(BF16)
        coeffs = matmul(ana_ref[t], grad_spectra, ((0,), (0,)))
        for r in range(2):
            goes_ref[pl.ds(r * ROWS + t, LANES, stride=8), :] = coeffs[:, r * CH : (r + 1) * CH]
    out_ref[:, :32, :] = goes_ref[...].reshape(PEERS, 32, CH).astype(BF16)
    grad_ref[...] = jnp.concatenate([total_real[:NLAT], total_imag[:NLAT]], axis=0).astype(BF16)


def live(cycle_ref, j):
    return jnp.where(cycle_ref[j] < NLAT, 1.0, 0.0).astype(F32)


def mlp_kernel(x_ref, values_ref, inverse_ref, expand_ref, reduce_ref, cycle_ref, out_ref):
    for half in range(2):
        values = from_blocks(values_ref, 2 + half)
        for h in range(2):
            j = 2 * half + h
            mixed = x_ref[j].astype(F32) + matmul(inverse_ref[...], values[h])
            pre = matmul(mixed.astype(BF16), expand_ref[...])
            hidden = (0.5 * pre * (1.0 + lax.erf(pre * ROOT_HALF))).astype(BF16)
            result = mixed + matmul(hidden, reduce_ref[...])
            out_ref[j] = (result * live(cycle_ref, j)).astype(BF16)


def mlp_back_kernel(
    x_ref,
    values_ref,
    cotangent_ref,
    inverse_ref,
    inverse_t_ref,
    expand_ref,
    reduce_ref,
    cycle_ref,
    out_ref,
    grad_mixed_ref,
    shares_ref,
    mixed_ref,
    masked_ref,
    hidden_ref,
    grad_pre_ref,
):
    for half in range(2):
        values = from_blocks(values_ref, half)
        grad_values = []
        for h in range(2):
            j = 2 * half + h
            rows = slice(j * NLON, (j + 1) * NLON)
            mixed = x_ref[j].astype(F32) + matmul(inverse_ref[...], values[h])
            mixed_b = mixed.astype(BF16)
            masked_f = cotangent_ref[j].astype(F32) * live(cycle_ref, j)
            masked = masked_f.astype(BF16)
            mixed_ref[rows, :] = mixed_b
            masked_ref[rows, :] = masked
            pre = matmul(mixed_b, expand_ref[...])
            normal = 0.5 * (1.0 + lax.erf(pre * ROOT_HALF))
            hidden_ref[rows, :] = (pre * normal).astype(BF16)
            slope = normal + pre * jnp.exp(-0.5 * pre * pre) * INV_ROOT_TAU
            grad_hidden = matmul(masked, reduce_ref[...], ((1,), (1,)))
            grad_pre = (grad_hidden * slope).astype(BF16)
            grad_pre_ref[rows, :] = grad_pre
            grad_mixed = masked_f + matmul(grad_pre, expand_ref[...], ((1,), (1,)))
            grad_mixed_ref[j] = grad_mixed
            grad_values.append(matmul(inverse_t_ref[...], grad_mixed.astype(BF16)))
        to_blocks(out_ref, half, grad_values)
    expand_grad = matmul(grad_pre_ref[...], mixed_ref[...], ((0,), (0,))).astype(BF16)
    reduce_grad = matmul(hidden_ref[...], masked_ref[...], ((0,), (0,))).astype(BF16)
    part = HID // 4
    for d in range(4):
        shares_ref[d, :part, :] = expand_grad[d * part : (d + 1) * part]
        shares_ref[d, part:, :] = reduce_grad[d * part : (d + 1) * part]


def input_grad_kernel(coeffs_ref, grad_mixed_ref, forward_ref, cycle_ref, out_ref):
    for half in range(2):
        values = from_blocks(coeffs_ref, half)
        for h in range(2):
            j = 2 * half + h
            total = grad_mixed_ref[j] + matmul(forward_ref[...], values[h])
            out_ref[j] = (total * live(cycle_ref, j)).astype(BF16)


def share_piece_kernel(arrived_ref, out_ref):
    piece = arrived_ref[:, 64:, :].astype(F32).sum(axis=0).astype(BF16)
    out_ref[...] = jnp.broadcast_to(piece[None], out_ref.shape)


def share_result_kernel(pieces_ref, expand_ref, reduce_ref):
    half = PEERS // 2
    for p in range(PEERS):
        target = expand_ref if p < half else reduce_ref
        target[(p % half) * 12 : (p % half) * 12 + 12, :] = pieces_ref[p].astype(F32)[:12]


def call(kernel, outs, args, scratch=(), flops=0, transcendentals=0, smem=()):
    specs = [
        pl.BlockSpec(memory_space=pltpu.SMEM if n in smem else pltpu.VMEM) for n in range(len(args))
    ]
    moved = sum(a.size * a.dtype.itemsize for a in (*args, *outs))
    return pl.pallas_call(
        kernel,
        out_shape=outs,
        in_specs=specs,
        out_specs=[pl.BlockSpec(memory_space=pltpu.VMEM)] * len(outs),
        scratch_shapes=list(scratch),
        compiler_params=pltpu.CompilerParams(vmem_limit_bytes=24 * 1024 * 1024),
        cost_estimate=pl.CostEstimate(
            flops=flops, bytes_accessed=moved, transcendentals=transcendentals
        ),
    )(*args)


PAIRED = jax.ShapeDtypeStruct((PEERS, 64, CH), BF16)
TRIPLE = jax.ShapeDtypeStruct((PEERS, 80, CH), BF16)
SHARES = jax.ShapeDtypeStruct((PEERS, 16, CH), BF16)
BLOCKS = jax.ShapeDtypeStruct((PEERS, 32, CH), BF16)
TOKENS = jax.ShapeDtypeStruct((ROWS, NLON, CH), BF16)
SPECTRAL_SCRATCH = (pltpu.VMEM((LANES * 8, CH), F32), pltpu.VMEM((LANES * 8, CH), F32))


def exchange(blocks, axes):
    return lax.all_to_all(blocks, axes, split_axis=0, concat_axis=0, tiled=True)


def total(blocks):
    return blocks.astype(F32).sum(axis=0)


def from_behind(block, axis, distance):
    devices = range(lax.axis_size(axis))
    route = [(i - distance, i) for i in devices if i - distance in devices]
    return lax.ppermute(block, axis, route)


def around(block, axis, distance):
    count = lax.axis_size(axis)
    return lax.ppermute(block, axis, [(i, (i + distance) % count) for i in range(count)])


def scattered_total(blocks, axis):
    count = lax.axis_size(axis)
    me = lax.axis_index(axis)

    def block_of(distance):
        return lax.dynamic_index_in_dim(blocks, (me + distance) % count, 0, keepdims=False)

    came = [around(block_of(k), axis, k) for k in range(1, count)]
    return sum((block.astype(F32) for block in came), block_of(0).astype(F32))


def share_blocks_of(shares):
    own = scattered_total(shares, "dp").astype(BF16).reshape(PEERS, 12, CH)
    return jnp.pad(own, ((0, 0), (0, 4), (0, 0)))


def filter_total(part):
    over_dp = total(lax.all_gather(part, "dp")).astype(BF16)
    half = scattered_total(over_dp.reshape(2, NLAT, CH), "sp_1").astype(BF16)
    mine = total(lax.all_gather(half, "sp_0"))
    other = around(mine, "sp_1", 1)
    first = lax.axis_index("sp_1") == 0
    return jnp.stack([jnp.where(first, mine, other), jnp.where(first, other, mine)])


def on_device(
    forward_np,
    inverse_np,
    orders_np,
    fresh_input,
    saved_input,
    output_grad,
    expand_weight,
    reduce_weight,
    filter_weight,
    cycle_table,
):
    position = lax.axis_index(SP)
    fresh, saved, cotangent = fresh_input[0, 0], saved_input[0, 0], output_grad[0, 0]
    expand, contract, filt = expand_weight[0], reduce_weight[0], filter_weight[0]
    forward = jnp.asarray(forward_np)
    forward_t = jnp.asarray(np.ascontiguousarray(forward_np.T))
    inverse = jnp.asarray(inverse_np)
    inverse_t = jnp.asarray(np.ascontiguousarray(inverse_np.T))
    own_cycles = lax.dynamic_slice_in_dim(cycle_table, position * ROWS, ROWS)
    dft = 2 * ROWS * 256 * NLON * CH
    leg = 2 * 16 * 128 * 128 * CH
    mlp = 2 * ROWS * NLON * CH * HID

    saved_blocks = call(coeffs_kernel, [BLOCKS], [saved, forward_t], flops=dft)[0]
    saved_at_orders = exchange(saved_blocks, SP)
    fresh_blocks = call(coeffs_kernel, [BLOCKS], [fresh, forward_t], flops=dft)[0]

    lat_live = (cycle_table < NLAT).astype(F32)
    colatitude = math.pi * (jnp.minimum(cycle_table, NLAT - 1).astype(F32) + 0.5) / NLAT
    sine = jnp.sin(colatitude)
    geo = jnp.stack(
        [jnp.cos(colatitude), jnp.log(sine), math.pi / NLAT * sine * lat_live, lat_live]
    )
    order_rows = lax.dynamic_index_in_dim(jnp.asarray(orders_np), position, 0, keepdims=False)
    tables = jax.ShapeDtypeStruct((ROWS, LANES, LANES), BF16)
    ana, syn = call(
        tables_kernel,
        [tables, tables],
        [geo, order_rows],
        [pltpu.VMEM((LANES * 8, LANES), F32)],
        flops=4_000_000,
    )

    spectra_shape = jax.ShapeDtypeStruct((ROWS, LANES, 2 * CH), F32)
    values_fresh, spectra = call(
        saved_spectral_kernel,
        [PAIRED, spectra_shape],
        [saved_at_orders, ana, syn, filt, fresh_blocks],
        SPECTRAL_SCRATCH,
        flops=leg,
    )
    values_fresh = exchange(values_fresh, SP)

    grad_values, grad_mixed, shares = call(
        mlp_back_kernel,
        [
            BLOCKS,
            jax.ShapeDtypeStruct((ROWS, NLON, CH), F32),
            jax.ShapeDtypeStruct((4, 2 * HID // 4, CH), BF16),
        ],
        [saved, values_fresh, cotangent, inverse, inverse_t, expand, contract, own_cycles],
        [
            pltpu.VMEM((ROWS * NLON, CH), BF16),
            pltpu.VMEM((ROWS * NLON, CH), BF16),
            pltpu.VMEM((ROWS * NLON, HID), BF16),
            pltpu.VMEM((ROWS * NLON, HID), BF16),
        ],
        flops=5 * mlp + 2 * dft,
        transcendentals=2 * ROWS * NLON * HID,
        smem=(7,),
    )
    grads_at_orders = exchange(grad_values, SP)
    fresh_values = call(
        fresh_spectral_kernel, [BLOCKS], [values_fresh, ana, syn, filt], SPECTRAL_SCRATCH, flops=leg
    )[0]
    share_blocks = share_blocks_of(shares)

    coeffs_fresh, filter_part = call(
        spectral_back_kernel,
        [TRIPLE, jax.ShapeDtypeStruct((2 * NLAT, CH), BF16)],
        [grads_at_orders, spectra, ana, syn, filt, fresh_values, share_blocks],
        SPECTRAL_SCRATCH,
        flops=leg,
    )
    coeffs_fresh = exchange(coeffs_fresh, SP)
    filter_grad = filter_total(filter_part)
    pieces = call(share_piece_kernel, [SHARES], [coeffs_fresh])[0]
    pieces = exchange(pieces, SP)
    input_grad = call(
        input_grad_kernel,
        [TOKENS],
        [coeffs_fresh, grad_mixed, forward, own_cycles],
        flops=dft,
        smem=(3,),
    )[0]
    sent_back = from_behind(input_grad[None, None], "pipe", -1)
    block = call(
        mlp_kernel,
        [TOKENS],
        [fresh, coeffs_fresh, inverse, expand, contract, own_cycles],
        flops=2 * mlp + dft,
        transcendentals=ROWS * NLON * HID,
        smem=(5,),
    )[0]
    next_input = from_behind(block[None, None], "pipe", 1)
    part = jax.ShapeDtypeStruct((HID // 4, CH), F32)
    expand_grad, reduce_grad = call(share_result_kernel, [part, part], [pieces])
    return (next_input, sent_back, expand_grad.T[None], reduce_grad[None], filter_grad[None])


def solution(mesh):
    finer = Mesh(
        mesh.devices.reshape(mesh.shape["pipe"], 16, 2, mesh.shape["dp"]),
        ("pipe", "sp_0", "sp_1", "dp"),
    )
    in_specs = (
        P("pipe", "dp", SP, None, None),
        P("pipe", "dp", SP, None, None),
        P("pipe", "dp", SP, None, None),
        P("pipe", None, None),
        P("pipe", None, None),
        P("pipe", None, None, None),
        P(),
    )
    out_specs = (
        P("pipe", "dp", SP, None, None),
        P("pipe", "dp", SP, None, None),
        P("pipe", None, "dp"),
        P("pipe", "dp", None),
        P("pipe", None, None, None),
    )
    forward, inverse = fourier_constants()
    program = functools.partial(on_device, forward, inverse, order_constants())
    return jax.shard_map(
        program, mesh=finer, in_specs=in_specs, out_specs=out_specs, check_vma=False
    )
```

```python
import functools
import math

import jax
import jax.numpy as jnp
import numpy as np
from jax import lax
from jax.experimental import pallas as pl
from jax.experimental.pallas import tpu as pltpu
from jax.sharding import Mesh
from jax.sharding import PartitionSpec as P

NLAT = 120
NLON = 240
CH = 128
HID = 768
ROWS = 4
PEERS = 32
LANES = 128
SP = ("sp_0", "sp_1")

ROOT_HALF = 0.7071067811865476
INV_ROOT_TAU = 0.3989422804014327
F32 = jnp.float32
BF16 = jnp.bfloat16


def fourier_constants():
    order = np.arange(128)
    live = (order < NLAT).astype(np.float64)
    value = np.minimum(order, NLAT - 1)
    phase = 2.0 * math.pi / NLON * ((np.arange(NLON)[:, None] * value[None, :]) % NLON)
    scaled = live * (2.0 * math.pi / NLON)
    forward = np.stack([np.cos(phase) * scaled, -np.sin(phase) * scaled], axis=1)
    factor = np.where(value == 0, 1.0, 2.0) * live / (2.0 * math.pi)
    inverse = np.stack([np.cos(phase) * factor, -np.sin(phase) * factor], axis=1)

    def arranged(table):
        table = table.reshape(NLON, 2, PEERS, ROWS).transpose(0, 2, 1, 3)
        return table.reshape(NLON, 256).astype(np.float32).astype(jnp.bfloat16)

    return arranged(forward), arranged(inverse)


def order_constants():
    table = np.zeros((PEERS, 3, 8, LANES), np.float32)
    for position in range(PEERS):
        for row in range(8):
            slot = position * ROWS + row % ROWS
            m = min(slot, NLAT - 1)
            log_start = 0.5 * (
                math.log((2.0 * m + 1.0) / (4.0 * math.pi))
                + math.lgamma(2.0 * m + 1.0)
                - 2.0 * math.lgamma(m + 1.0)
                - m * math.log(4.0)
            )
            table[position, 0, row] = m
            table[position, 1, row] = log_start
            table[position, 2, row] = float(slot < NLAT)
    return table


def tables_kernel(geo_ref, order_ref, ana_ref, syn_ref, work_ref):
    shape = (8, LANES)
    cosine = jnp.broadcast_to(geo_ref[0:1, :], shape)
    log_sine = jnp.broadcast_to(geo_ref[1:2, :], shape)
    weight = geo_ref[2:3, :]
    m = order_ref[0]
    keep = order_ref[2] * jnp.broadcast_to(geo_ref[3:4, :], shape)
    starting = jnp.exp(order_ref[1] + m * log_sine)
    squares = m * m
    previous = jnp.zeros(shape, F32)
    earlier = previous
    for degree in range(NLAT):
        upper = max(4.0 * degree * degree - 1.0, 0.0)
        lower = max(4.0 * (degree - 1.0) ** 2 - 1.0, 1.0)
        ratio_main = jnp.sqrt(upper / jnp.maximum(float(degree * degree) - squares, 1.0))
        ratio_back = jnp.sqrt(jnp.maximum((degree - 1.0) ** 2 - squares, 0.0) / lower)
        rising = ratio_main * (cosine * previous - ratio_back * earlier)
        current = jnp.where(m == float(degree), starting, jnp.where(m < float(degree), rising, 0.0))
        work_ref[degree * 8 : degree * 8 + 8, :] = current * keep
        previous, earlier = current, previous
    work_ref[NLAT * 8 :, :] = jnp.zeros((LANES * 8 - NLAT * 8, LANES), F32)
    for t in range(ROWS):
        table = work_ref[pl.ds(t, LANES, stride=8), :]
        syn_ref[t] = table.astype(BF16)
        ana_ref[t] = (table * weight).astype(BF16)


def to_blocks(out_ref, half, pair):
    blocks = [part.reshape(PEERS, 8, CH) for part in pair]
    out_ref[:, 16 * half : 16 * half + 16, :] = jnp.concatenate(blocks, axis=1).astype(BF16)


def from_blocks(block_ref, half):
    pair = block_ref[:, 16 * half : 16 * half + 16, :].astype(F32)
    return [pair[:, 8 * h : 8 * h + 8].reshape(256, CH).astype(BF16) for h in range(2)]


def matmul(left, right, dims=((1,), (0,))):
    return lax.dot_general(left, right, (dims, ((), ())), preferred_element_type=F32)


def coeffs_kernel(x_ref, forward_ref, out_ref):
    for half in range(2):
        to_blocks(out_ref, half, [matmul(forward_ref[...], x_ref[2 * half + h]) for h in range(2)])


def padded_filter(filt_ref):
    rest = jnp.zeros((LANES - NLAT, CH), F32)
    return [jnp.concatenate([filt_ref[part], rest], axis=0) for part in range(2)]


def spectral(came_ref, goes_ref, ana_ref, syn_ref, filt_ref, spectra_ref=None):
    real, imag = padded_filter(filt_ref)
    for t in range(ROWS):
        parts = [came_ref[pl.ds(r * ROWS + t, LANES, stride=8), :] for r in range(2)]
        spectra = matmul(ana_ref[t], jnp.concatenate(parts, axis=1).astype(BF16))
        if spectra_ref is not None:
            spectra_ref[t] = spectra
        first, second = spectra[:, :CH], spectra[:, CH:]
        filtered = jnp.concatenate(
            [real * first - imag * second, real * second + imag * first], axis=1
        ).astype(BF16)
        values = matmul(syn_ref[t], filtered, ((0,), (0,)))
        for r in range(2):
            goes_ref[pl.ds(r * ROWS + t, LANES, stride=8), :] = values[:, r * CH : (r + 1) * CH]


def saved_spectral_kernel(
    arrived_ref, ana_ref, syn_ref, filt_ref, beside_ref, out_ref, spectra_ref, came_ref, goes_ref
):
    out_ref[:, 32:, :] = beside_ref[...]
    came_ref[...] = arrived_ref[...].reshape(LANES * 8, CH).astype(F32)
    spectral(came_ref, goes_ref, ana_ref, syn_ref, filt_ref, spectra_ref)
    out_ref[:, :32, :] = goes_ref[...].reshape(PEERS, 32, CH).astype(BF16)


def fresh_spectral_kernel(arrived_ref, ana_ref, syn_ref, filt_ref, out_ref, came_ref, goes_ref):
    came_ref[...] = arrived_ref[:, 32:, :].reshape(LANES * 8, CH).astype(F32)
    spectral(came_ref, goes_ref, ana_ref, syn_ref, filt_ref)
    out_ref[...] = goes_ref[...].reshape(PEERS, 32, CH).astype(BF16)


def spectral_back_kernel(
    arrived_ref,
    spectra_ref,
    ana_ref,
    syn_ref,
    filt_ref,
    beside_ref,
    shares_ref,
    out_ref,
    came_ref,
    goes_ref,
):
    out_ref[:, 32:64, :] = beside_ref[...]
    came_ref[...] = arrived_ref[...].reshape(LANES * 8, CH).astype(F32)
    real, imag = padded_filter(filt_ref)
    total_real = jnp.zeros((LANES, CH), F32)
    total_imag = jnp.zeros((LANES, CH), F32)
    for t in range(ROWS):
        parts = [came_ref[pl.ds(r * ROWS + t, LANES, stride=8), :] for r in range(2)]
        grads = matmul(syn_ref[t], jnp.concatenate(parts, axis=1).astype(BF16))
        first, second = grads[:, :CH], grads[:, CH:]
        spectra = spectra_ref[t]
        s_first, s_second = spectra[:, :CH], spectra[:, CH:]
        total_real = total_real + (first * s_first + second * s_second)
        total_imag = total_imag + (second * s_first - first * s_second)
        grad_spectra = jnp.concatenate(
            [real * first + imag * second, real * second - imag * first], axis=1
        ).astype(BF16)
        coeffs = matmul(ana_ref[t], grad_spectra, ((0,), (0,)))
        for r in range(2):
            goes_ref[pl.ds(r * ROWS + t, LANES, stride=8), :] = coeffs[:, r * CH : (r + 1) * CH]
    out_ref[:, :32, :] = goes_ref[...].reshape(PEERS, 32, CH).astype(BF16)
    filter_part = jnp.concatenate([total_real, total_imag], axis=0).reshape(PEERS, 8, CH)
    sums = jnp.concatenate([shares_ref[...].astype(F32), filter_part], axis=1)
    out_ref[:, 64:, :] = sums.astype(BF16)


def live(cycle_ref, j):
    return jnp.where(cycle_ref[j] < NLAT, 1.0, 0.0).astype(F32)


def mlp_kernel(x_ref, values_ref, inverse_ref, expand_ref, reduce_ref, cycle_ref, out_ref):
    for half in range(2):
        values = from_blocks(values_ref, 2 + half)
        for h in range(2):
            j = 2 * half + h
            mixed = x_ref[j].astype(F32) + matmul(inverse_ref[...], values[h])
            pre = matmul(mixed.astype(BF16), expand_ref[...])
            hidden = (0.5 * pre * (1.0 + lax.erf(pre * ROOT_HALF))).astype(BF16)
            result = mixed + matmul(hidden, reduce_ref[...])
            out_ref[j] = (result * live(cycle_ref, j)).astype(BF16)


def mlp_back_kernel(
    x_ref,
    values_ref,
    cotangent_ref,
    inverse_ref,
    inverse_t_ref,
    expand_ref,
    reduce_ref,
    cycle_ref,
    out_ref,
    grad_mixed_ref,
    shares_ref,
    mixed_ref,
    masked_ref,
    hidden_ref,
    grad_pre_ref,
):
    for half in range(2):
        values = from_blocks(values_ref, half)
        grad_values = []
        for h in range(2):
            j = 2 * half + h
            rows = slice(j * NLON, (j + 1) * NLON)
            mixed = x_ref[j].astype(F32) + matmul(inverse_ref[...], values[h])
            mixed_b = mixed.astype(BF16)
            masked_f = cotangent_ref[j].astype(F32) * live(cycle_ref, j)
            masked = masked_f.astype(BF16)
            mixed_ref[rows, :] = mixed_b
            masked_ref[rows, :] = masked
            pre = matmul(mixed_b, expand_ref[...])
            normal = 0.5 * (1.0 + lax.erf(pre * ROOT_HALF))
            hidden_ref[rows, :] = (pre * normal).astype(BF16)
            slope = normal + pre * jnp.exp(-0.5 * pre * pre) * INV_ROOT_TAU
            grad_hidden = matmul(masked, reduce_ref[...], ((1,), (1,)))
            grad_pre = (grad_hidden * slope).astype(BF16)
            grad_pre_ref[rows, :] = grad_pre
            grad_mixed = masked_f + matmul(grad_pre, expand_ref[...], ((1,), (1,)))
            grad_mixed_ref[j] = grad_mixed
            grad_values.append(matmul(inverse_t_ref[...], grad_mixed.astype(BF16)))
        to_blocks(out_ref, half, grad_values)
    expand_grad = matmul(grad_pre_ref[...], mixed_ref[...], ((0,), (0,))).astype(BF16)
    reduce_grad = matmul(hidden_ref[...], masked_ref[...], ((0,), (0,))).astype(BF16)
    part = HID // 4
    for d in range(4):
        shares_ref[d, :part, :] = expand_grad[d * part : (d + 1) * part]
        shares_ref[d, part:, :] = reduce_grad[d * part : (d + 1) * part]


def input_grad_kernel(coeffs_ref, grad_mixed_ref, forward_ref, cycle_ref, out_ref):
    for half in range(2):
        values = from_blocks(coeffs_ref, half)
        for h in range(2):
            j = 2 * half + h
            total = grad_mixed_ref[j] + matmul(forward_ref[...], values[h])
            out_ref[j] = (total * live(cycle_ref, j)).astype(BF16)


def piece_kernel(arrived_ref, share_ref, filter_ref):
    piece = arrived_ref[:, 64:, :].astype(F32).sum(axis=0)
    share_ref[...] = piece[:16]
    filter_ref[...] = jnp.broadcast_to(piece[16:][None], filter_ref.shape)


def spread_kernel(share_ref, filter_ref, out_ref):
    piece = jnp.concatenate([share_ref[...], filter_ref[...].sum(axis=0)], axis=0)
    out_ref[...] = jnp.broadcast_to(piece[None], out_ref.shape).astype(BF16)


def result_kernel(pieces_ref, expand_ref, reduce_ref, filter_ref):
    half = PEERS // 2
    for p in range(PEERS):
        side, at = divmod(p, half)
        piece = pieces_ref[p].astype(F32)
        (reduce_ref if side else expand_ref)[at * 12 : at * 12 + 12, :] = piece[:12]
        if at < NLAT // 8:
            filter_ref[side, at * 8 : at * 8 + 8, :] = piece[16:]


def call(kernel, outs, args, scratch=(), flops=0, transcendentals=0, smem=()):
    specs = [
        pl.BlockSpec(memory_space=pltpu.SMEM if n in smem else pltpu.VMEM) for n in range(len(args))
    ]
    moved = sum(a.size * a.dtype.itemsize for a in (*args, *outs))
    return pl.pallas_call(
        kernel,
        out_shape=outs,
        in_specs=specs,
        out_specs=[pl.BlockSpec(memory_space=pltpu.VMEM)] * len(outs),
        scratch_shapes=list(scratch),
        compiler_params=pltpu.CompilerParams(vmem_limit_bytes=24 * 1024 * 1024),
        cost_estimate=pl.CostEstimate(
            flops=flops, bytes_accessed=moved, transcendentals=transcendentals
        ),
    )(*args)


PAIRED = jax.ShapeDtypeStruct((PEERS, 64, CH), BF16)
TRIPLE = jax.ShapeDtypeStruct((PEERS, 88, CH), BF16)
BLOCKS = jax.ShapeDtypeStruct((PEERS, 32, CH), BF16)
TOKENS = jax.ShapeDtypeStruct((ROWS, NLON, CH), BF16)
SPECTRAL_SCRATCH = (pltpu.VMEM((LANES * 8, CH), F32), pltpu.VMEM((LANES * 8, CH), F32))


def exchange(blocks, axes):
    return lax.all_to_all(blocks, axes, split_axis=0, concat_axis=0, tiled=True)


def from_behind(block, axis, distance):
    devices = range(lax.axis_size(axis))
    route = [(i - distance, i) for i in devices if i - distance in devices]
    return lax.ppermute(block, axis, route)


def around(block, axis, distance):
    count = lax.axis_size(axis)
    return lax.ppermute(block, axis, [(i, (i + distance) % count) for i in range(count)])


def scattered_total(blocks, axis):
    count = lax.axis_size(axis)
    me = lax.axis_index(axis)

    def block_of(distance):
        return lax.dynamic_index_in_dim(blocks, (me + distance) % count, 0, keepdims=False)

    came = [around(block_of(k), axis, k) for k in range(1, count)]
    return sum((block.astype(F32) for block in came), block_of(0).astype(F32))


def share_blocks_of(shares):
    own = scattered_total(shares, "dp").astype(BF16).reshape(PEERS, 12, CH)
    return jnp.pad(own, ((0, 0), (0, 4), (0, 0)))


def on_device(
    forward_np,
    inverse_np,
    orders_np,
    fresh_input,
    saved_input,
    output_grad,
    expand_weight,
    reduce_weight,
    filter_weight,
    cycle_table,
):
    position = lax.axis_index(SP)
    fresh, saved, cotangent = fresh_input[0, 0], saved_input[0, 0], output_grad[0, 0]
    expand, contract, filt = expand_weight[0], reduce_weight[0], filter_weight[0]
    forward = jnp.asarray(forward_np)
    forward_t = jnp.asarray(np.ascontiguousarray(forward_np.T))
    inverse = jnp.asarray(inverse_np)
    inverse_t = jnp.asarray(np.ascontiguousarray(inverse_np.T))
    own_cycles = lax.dynamic_slice_in_dim(cycle_table, position * ROWS, ROWS)
    dft = 2 * ROWS * 256 * NLON * CH
    leg = 2 * 16 * 128 * 128 * CH
    mlp = 2 * ROWS * NLON * CH * HID

    saved_blocks = call(coeffs_kernel, [BLOCKS], [saved, forward_t], flops=dft)[0]
    saved_at_orders = exchange(saved_blocks, SP)
    fresh_blocks = call(coeffs_kernel, [BLOCKS], [fresh, forward_t], flops=dft)[0]

    lat_live = (cycle_table < NLAT).astype(F32)
    colatitude = math.pi * (jnp.minimum(cycle_table, NLAT - 1).astype(F32) + 0.5) / NLAT
    sine = jnp.sin(colatitude)
    geo = jnp.stack(
        [jnp.cos(colatitude), jnp.log(sine), math.pi / NLAT * sine * lat_live, lat_live]
    )
    order_rows = lax.dynamic_index_in_dim(jnp.asarray(orders_np), position, 0, keepdims=False)
    tables = jax.ShapeDtypeStruct((ROWS, LANES, LANES), BF16)
    ana, syn = call(
        tables_kernel,
        [tables, tables],
        [geo, order_rows],
        [pltpu.VMEM((LANES * 8, LANES), F32)],
        flops=4_000_000,
    )

    spectra_shape = jax.ShapeDtypeStruct((ROWS, LANES, 2 * CH), F32)
    values_fresh, spectra = call(
        saved_spectral_kernel,
        [PAIRED, spectra_shape],
        [saved_at_orders, ana, syn, filt, fresh_blocks],
        SPECTRAL_SCRATCH,
        flops=leg,
    )
    values_fresh = exchange(values_fresh, SP)

    grad_values, grad_mixed, shares = call(
        mlp_back_kernel,
        [
            BLOCKS,
            jax.ShapeDtypeStruct((ROWS, NLON, CH), F32),
            jax.ShapeDtypeStruct((4, 2 * HID // 4, CH), BF16),
        ],
        [saved, values_fresh, cotangent, inverse, inverse_t, expand, contract, own_cycles],
        [
            pltpu.VMEM((ROWS * NLON, CH), BF16),
            pltpu.VMEM((ROWS * NLON, CH), BF16),
            pltpu.VMEM((ROWS * NLON, HID), BF16),
            pltpu.VMEM((ROWS * NLON, HID), BF16),
        ],
        flops=5 * mlp + 2 * dft,
        transcendentals=2 * ROWS * NLON * HID,
        smem=(7,),
    )
    grads_at_orders = exchange(grad_values, SP)
    fresh_values = call(
        fresh_spectral_kernel, [BLOCKS], [values_fresh, ana, syn, filt], SPECTRAL_SCRATCH, flops=leg
    )[0]
    share_blocks = share_blocks_of(shares)

    coeffs_fresh = call(
        spectral_back_kernel,
        [TRIPLE],
        [grads_at_orders, spectra, ana, syn, filt, fresh_values, share_blocks],
        SPECTRAL_SCRATCH,
        flops=leg,
    )[0]
    coeffs_fresh = exchange(coeffs_fresh, SP)
    share, filter_piece = call(
        piece_kernel,
        [jax.ShapeDtypeStruct((16, CH), F32), jax.ShapeDtypeStruct((4, 8, CH), F32)],
        [coeffs_fresh],
    )
    filter_piece = exchange(filter_piece, "dp")
    pieces = call(
        spread_kernel, [jax.ShapeDtypeStruct((PEERS, 24, CH), BF16)], [share, filter_piece]
    )[0]
    pieces = exchange(pieces, SP)
    input_grad = call(
        input_grad_kernel,
        [TOKENS],
        [coeffs_fresh, grad_mixed, forward, own_cycles],
        flops=dft,
        smem=(3,),
    )[0]
    sent_back = from_behind(input_grad[None, None], "pipe", -1)
    block = call(
        mlp_kernel,
        [TOKENS],
        [fresh, coeffs_fresh, inverse, expand, contract, own_cycles],
        flops=2 * mlp + dft,
        transcendentals=ROWS * NLON * HID,
        smem=(5,),
    )[0]
    next_input = from_behind(block[None, None], "pipe", 1)
    part = jax.ShapeDtypeStruct((HID // 4, CH), F32)
    expand_grad, reduce_grad, filter_grad = call(
        result_kernel, [part, part, jax.ShapeDtypeStruct((2, NLAT, CH), F32)], [pieces]
    )
    return (next_input, sent_back, expand_grad.T[None], reduce_grad[None], filter_grad[None])


def solution(mesh):
    finer = Mesh(
        mesh.devices.reshape(mesh.shape["pipe"], 16, 2, mesh.shape["dp"]),
        ("pipe", "sp_0", "sp_1", "dp"),
    )
    in_specs = (
        P("pipe", "dp", SP, None, None),
        P("pipe", "dp", SP, None, None),
        P("pipe", "dp", SP, None, None),
        P("pipe", None, None),
        P("pipe", None, None),
        P("pipe", None, None, None),
        P(),
    )
    out_specs = (
        P("pipe", "dp", SP, None, None),
        P("pipe", "dp", SP, None, None),
        P("pipe", None, "dp"),
        P("pipe", "dp", None),
        P("pipe", None, None, None),
    )
    forward, inverse = fourier_constants()
    program = functools.partial(on_device, forward, inverse, order_constants())
    return jax.shard_map(
        program, mesh=finer, in_specs=in_specs, out_specs=out_specs, check_vma=False
    )
```

```python
import functools
import math

import jax
import jax.numpy as jnp
import numpy as np
from jax import lax
from jax.experimental import pallas as pl
from jax.experimental.pallas import tpu as pltpu
from jax.sharding import Mesh
from jax.sharding import PartitionSpec as P

NLAT = 120
NLON = 240
CH = 128
HID = 768
ROWS = 4
PEERS = 32
LANES = 128
SP = ("sp_0", "sp_1")

ROOT_HALF = 0.7071067811865476
INV_ROOT_TAU = 0.3989422804014327
F32 = jnp.float32
BF16 = jnp.bfloat16


def fourier_constants():
    order = np.arange(128)
    live = (order < NLAT).astype(np.float64)
    value = np.minimum(order, NLAT - 1)
    phase = 2.0 * math.pi / NLON * ((np.arange(NLON)[:, None] * value[None, :]) % NLON)
    scaled = live * (2.0 * math.pi / NLON)
    forward = np.stack([np.cos(phase) * scaled, -np.sin(phase) * scaled], axis=1)
    factor = np.where(value == 0, 1.0, 2.0) * live / (2.0 * math.pi)
    inverse = np.stack([np.cos(phase) * factor, -np.sin(phase) * factor], axis=1)

    def arranged(table):
        table = table.reshape(NLON, 2, PEERS, ROWS).transpose(0, 2, 1, 3)
        return table.reshape(NLON, 256).astype(np.float32).astype(jnp.bfloat16)

    return arranged(forward), arranged(inverse)


def order_constants():
    table = np.zeros((PEERS, 3, 8, LANES), np.float32)
    for position in range(PEERS):
        for row in range(8):
            slot = position * ROWS + row % ROWS
            m = min(slot, NLAT - 1)
            log_start = 0.5 * (
                math.log((2.0 * m + 1.0) / (4.0 * math.pi))
                + math.lgamma(2.0 * m + 1.0)
                - 2.0 * math.lgamma(m + 1.0)
                - m * math.log(4.0)
            )
            table[position, 0, row] = m
            table[position, 1, row] = log_start
            table[position, 2, row] = float(slot < NLAT)
    return table


def tables_kernel(geo_ref, order_ref, ana_ref, syn_ref, work_ref):
    shape = (8, LANES)
    cosine = jnp.broadcast_to(geo_ref[0:1, :], shape)
    log_sine = jnp.broadcast_to(geo_ref[1:2, :], shape)
    weight = geo_ref[2:3, :]
    m = order_ref[0]
    keep = order_ref[2] * jnp.broadcast_to(geo_ref[3:4, :], shape)
    starting = jnp.exp(order_ref[1] + m * log_sine)
    squares = m * m
    previous = jnp.zeros(shape, F32)
    earlier = previous
    for degree in range(NLAT):
        upper = max(4.0 * degree * degree - 1.0, 0.0)
        lower = max(4.0 * (degree - 1.0) ** 2 - 1.0, 1.0)
        ratio_main = jnp.sqrt(upper / jnp.maximum(float(degree * degree) - squares, 1.0))
        ratio_back = jnp.sqrt(jnp.maximum((degree - 1.0) ** 2 - squares, 0.0) / lower)
        rising = ratio_main * (cosine * previous - ratio_back * earlier)
        current = jnp.where(m == float(degree), starting, jnp.where(m < float(degree), rising, 0.0))
        work_ref[degree * 8 : degree * 8 + 8, :] = current * keep
        previous, earlier = current, previous
    work_ref[NLAT * 8 :, :] = jnp.zeros((LANES * 8 - NLAT * 8, LANES), F32)
    for t in range(ROWS):
        table = work_ref[pl.ds(t, LANES, stride=8), :]
        syn_ref[t] = table.astype(BF16)
        ana_ref[t] = (table * weight).astype(BF16)


def to_blocks(out_ref, half, pair):
    blocks = [part.reshape(PEERS, 8, CH) for part in pair]
    out_ref[:, 16 * half : 16 * half + 16, :] = jnp.concatenate(blocks, axis=1).astype(BF16)


def from_blocks(block_ref, half):
    pair = block_ref[:, 16 * half : 16 * half + 16, :].astype(F32)
    return [pair[:, 8 * h : 8 * h + 8].reshape(256, CH).astype(BF16) for h in range(2)]


def matmul(left, right, dims=((1,), (0,))):
    return lax.dot_general(left, right, (dims, ((), ())), preferred_element_type=F32)


def coeffs_kernel(x_ref, forward_ref, out_ref):
    for half in range(2):
        to_blocks(out_ref, half, [matmul(forward_ref[...], x_ref[2 * half + h]) for h in range(2)])


def padded_filter(filt_ref):
    rest = jnp.zeros((LANES - NLAT, CH), F32)
    return [jnp.concatenate([filt_ref[part], rest], axis=0) for part in range(2)]


def spectral(came_ref, goes_ref, ana_ref, syn_ref, filt_ref, spectra_ref=None):
    real, imag = padded_filter(filt_ref)
    for t in range(ROWS):
        parts = [came_ref[pl.ds(r * ROWS + t, LANES, stride=8), :] for r in range(2)]
        spectra = matmul(ana_ref[t], jnp.concatenate(parts, axis=1).astype(BF16))
        if spectra_ref is not None:
            spectra_ref[t] = spectra
        first, second = spectra[:, :CH], spectra[:, CH:]
        filtered = jnp.concatenate(
            [real * first - imag * second, real * second + imag * first], axis=1
        ).astype(BF16)
        values = matmul(syn_ref[t], filtered, ((0,), (0,)))
        for r in range(2):
            goes_ref[pl.ds(r * ROWS + t, LANES, stride=8), :] = values[:, r * CH : (r + 1) * CH]


def saved_spectral_kernel(
    arrived_ref, ana_ref, syn_ref, filt_ref, beside_ref, out_ref, spectra_ref, came_ref, goes_ref
):
    out_ref[:, 32:, :] = beside_ref[...]
    came_ref[...] = arrived_ref[...].reshape(LANES * 8, CH).astype(F32)
    spectral(came_ref, goes_ref, ana_ref, syn_ref, filt_ref, spectra_ref)
    out_ref[:, :32, :] = goes_ref[...].reshape(PEERS, 32, CH).astype(BF16)


def fresh_spectral_kernel(arrived_ref, ana_ref, syn_ref, filt_ref, out_ref, came_ref, goes_ref):
    came_ref[...] = arrived_ref[:, 32:, :].reshape(LANES * 8, CH).astype(F32)
    spectral(came_ref, goes_ref, ana_ref, syn_ref, filt_ref)
    out_ref[...] = goes_ref[...].reshape(PEERS, 32, CH).astype(BF16)


def spectral_back_kernel(
    arrived_ref,
    spectra_ref,
    ana_ref,
    syn_ref,
    filt_ref,
    beside_ref,
    shares_ref,
    out_ref,
    came_ref,
    goes_ref,
):
    out_ref[:, 32:64, :] = beside_ref[...]
    came_ref[...] = arrived_ref[...].reshape(LANES * 8, CH).astype(F32)
    real, imag = padded_filter(filt_ref)
    total_real = jnp.zeros((LANES, CH), F32)
    total_imag = jnp.zeros((LANES, CH), F32)
    for t in range(ROWS):
        parts = [came_ref[pl.ds(r * ROWS + t, LANES, stride=8), :] for r in range(2)]
        grads = matmul(syn_ref[t], jnp.concatenate(parts, axis=1).astype(BF16))
        first, second = grads[:, :CH], grads[:, CH:]
        spectra = spectra_ref[t]
        s_first, s_second = spectra[:, :CH], spectra[:, CH:]
        total_real = total_real + (first * s_first + second * s_second)
        total_imag = total_imag + (second * s_first - first * s_second)
        grad_spectra = jnp.concatenate(
            [real * first + imag * second, real * second - imag * first], axis=1
        ).astype(BF16)
        coeffs = matmul(ana_ref[t], grad_spectra, ((0,), (0,)))
        for r in range(2):
            goes_ref[pl.ds(r * ROWS + t, LANES, stride=8), :] = coeffs[:, r * CH : (r + 1) * CH]
    out_ref[:, :32, :] = goes_ref[...].reshape(PEERS, 32, CH).astype(BF16)
    filter_part = jnp.concatenate([total_real, total_imag], axis=0).reshape(PEERS, 8, CH)
    sums = jnp.concatenate([shares_ref[...].astype(F32), filter_part], axis=1)
    out_ref[:, 64:, :] = sums.astype(BF16)


def live(cycle_ref, j):
    return jnp.where(cycle_ref[j] < NLAT, 1.0, 0.0).astype(F32)


def mlp_kernel(x_ref, values_ref, inverse_ref, expand_ref, reduce_ref, cycle_ref, out_ref):
    for half in range(2):
        values = from_blocks(values_ref, 2 + half)
        for h in range(2):
            j = 2 * half + h
            mixed = x_ref[j].astype(F32) + matmul(inverse_ref[...], values[h])
            pre = matmul(mixed.astype(BF16), expand_ref[...])
            hidden = (0.5 * pre * (1.0 + lax.erf(pre * ROOT_HALF))).astype(BF16)
            result = mixed + matmul(hidden, reduce_ref[...])
            out_ref[j] = (result * live(cycle_ref, j)).astype(BF16)


def mlp_back_kernel(
    x_ref,
    values_ref,
    cotangent_ref,
    inverse_ref,
    inverse_t_ref,
    expand_ref,
    reduce_ref,
    cycle_ref,
    out_ref,
    grad_mixed_ref,
    mixed_ref,
    masked_ref,
    hidden_ref,
    grad_pre_ref,
):
    for half in range(2):
        values = from_blocks(values_ref, half)
        grad_values = []
        for h in range(2):
            j = 2 * half + h
            rows = slice(j * NLON, (j + 1) * NLON)
            mixed = x_ref[j].astype(F32) + matmul(inverse_ref[...], values[h])
            mixed_b = mixed.astype(BF16)
            masked_f = cotangent_ref[j].astype(F32) * live(cycle_ref, j)
            masked = masked_f.astype(BF16)
            mixed_ref[rows, :] = mixed_b
            masked_ref[rows, :] = masked
            pre = matmul(mixed_b, expand_ref[...])
            normal = 0.5 * (1.0 + lax.erf(pre * ROOT_HALF))
            hidden_ref[rows, :] = (pre * normal).astype(BF16)
            slope = normal + pre * jnp.exp(-0.5 * pre * pre) * INV_ROOT_TAU
            grad_hidden = matmul(masked, reduce_ref[...], ((1,), (1,)))
            grad_pre = (grad_hidden * slope).astype(BF16)
            grad_pre_ref[rows, :] = grad_pre
            grad_mixed = masked_f + matmul(grad_pre, expand_ref[...], ((1,), (1,)))
            grad_mixed_ref[j] = grad_mixed
            grad_values.append(matmul(inverse_t_ref[...], grad_mixed.astype(BF16)))
        to_blocks(out_ref, half, grad_values)


def weight_grads_kernel(mixed_ref, masked_ref, hidden_ref, grad_pre_ref, out_ref):
    quarter = HID // 4
    pairs = ((grad_pre_ref, mixed_ref), (hidden_ref, masked_ref))
    for side, (wide_ref, narrow_ref) in enumerate(pairs):
        grad = matmul(wide_ref[...], narrow_ref[...], ((0,), (0,))).astype(BF16)
        for d in range(4):
            out_ref[side, d] = grad[d * quarter : (d + 1) * quarter]


def input_grad_kernel(coeffs_ref, grad_mixed_ref, forward_ref, cycle_ref, out_ref):
    for half in range(2):
        values = from_blocks(coeffs_ref, half)
        for h in range(2):
            j = 2 * half + h
            total = grad_mixed_ref[j] + matmul(forward_ref[...], values[h])
            out_ref[j] = (total * live(cycle_ref, j)).astype(BF16)


def piece_kernel(arrived_ref, share_ref, filter_ref):
    came = arrived_ref[:, 64:, :].astype(F32).reshape(PEERS // 2, 2, 16, CH)
    sums = came.sum(axis=0)
    share_ref[0] = sums[0, :8]
    share_ref[1] = sums[1, :8]
    filter_ref[...] = jnp.broadcast_to((sums[0, 8:] + sums[1, 8:])[None], filter_ref.shape)


def spread_kernel(share_ref, filter_ref, out_ref):
    piece = jnp.concatenate([share_ref[0], share_ref[1], filter_ref[...].sum(axis=0)], axis=0)
    out_ref[...] = jnp.broadcast_to(piece[None], out_ref.shape).astype(BF16)


def result_kernel(
    pieces_ref,
    other_ref,
    core_ref,
    next_ref,
    back_ref,
    expand_ref,
    reduce_ref,
    filter_ref,
    next_out_ref,
    back_out_ref,
):
    next_out_ref[...] = next_ref[...]
    back_out_ref[...] = back_ref[...]
    first = core_ref[0] == 0
    for p in range(PEERS):
        mine, other = pieces_ref[p // 2].astype(F32), other_ref[p // 2].astype(F32)
        piece = jnp.where(first, mine, other) if p % 2 == 0 else jnp.where(first, other, mine)
        expand_ref[p * 6 : p * 6 + 6, :] = piece[:6]
        reduce_ref[p * 6 : p * 6 + 6, :] = piece[8:14]
        side, at = divmod(p, PEERS // 2)
        if at < NLAT // 8:
            filter_ref[side, at * 8 : at * 8 + 8, :] = piece[16:]


def call(kernel, outs, args, scratch=(), flops=0, transcendentals=0, smem=()):
    specs = [
        pl.BlockSpec(memory_space=pltpu.SMEM if n in smem else pltpu.VMEM) for n in range(len(args))
    ]
    moved = sum(a.size * a.dtype.itemsize for a in (*args, *outs))
    return pl.pallas_call(
        kernel,
        out_shape=outs,
        in_specs=specs,
        out_specs=[pl.BlockSpec(memory_space=pltpu.VMEM)] * len(outs),
        scratch_shapes=list(scratch),
        compiler_params=pltpu.CompilerParams(vmem_limit_bytes=24 * 1024 * 1024),
        cost_estimate=pl.CostEstimate(
            flops=flops, bytes_accessed=moved, transcendentals=transcendentals
        ),
    )(*args)


PAIRED = jax.ShapeDtypeStruct((PEERS, 64, CH), BF16)
TRIPLE = jax.ShapeDtypeStruct((PEERS, 80, CH), BF16)
BLOCKS = jax.ShapeDtypeStruct((PEERS, 32, CH), BF16)
TOKENS = jax.ShapeDtypeStruct((ROWS, NLON, CH), BF16)
SPECTRAL_SCRATCH = (pltpu.VMEM((LANES * 8, CH), F32), pltpu.VMEM((LANES * 8, CH), F32))


CORE_SWAP = [(0, 1), (1, 0)]


def exchange(blocks, axes):
    return lax.all_to_all(blocks, axes, split_axis=0, concat_axis=0, tiled=True)


def from_behind(block, axis, distance):
    devices = range(lax.axis_size(axis))
    route = [(i - distance, i) for i in devices if i - distance in devices]
    return lax.ppermute(block, axis, route)


def halved(blocks, axis, route, kept):
    mine = lax.dynamic_index_in_dim(blocks, kept, 0, keepdims=False)
    sent = lax.dynamic_index_in_dim(blocks, 1 - kept, 0, keepdims=False)
    came = lax.ppermute(sent, axis, route)
    return (mine.astype(F32) + came.astype(F32)).astype(BF16)


def around(block, axis, distance):
    count = lax.axis_size(axis)
    return lax.ppermute(block, axis, [(i, (i + distance) % count) for i in range(count)])


def scattered_total(blocks, axis):
    count = lax.axis_size(axis)
    me = lax.axis_index(axis)

    def block_of(distance):
        return lax.dynamic_index_in_dim(blocks, (me + distance) % count, 0, keepdims=False)

    came = [around(block_of(k), axis, k) for k in range(1, count)]
    return sum((block.astype(F32) for block in came), block_of(0).astype(F32))


def share_blocks_of(shares):
    kept = halved(shares, "sp_1", CORE_SWAP, lax.axis_index("sp_1"))
    kept = scattered_total(kept, "dp").astype(BF16)
    return jnp.pad(kept.reshape(PEERS, 6, CH), ((0, 0), (0, 2), (0, 0)))


def on_device(
    forward_np,
    inverse_np,
    orders_np,
    fresh_input,
    saved_input,
    output_grad,
    expand_weight,
    reduce_weight,
    filter_weight,
    cycle_table,
):
    position = lax.axis_index(SP)
    fresh, saved, cotangent = fresh_input[0, 0], saved_input[0, 0], output_grad[0, 0]
    expand, contract, filt = expand_weight[0], reduce_weight[0], filter_weight[0]
    forward = jnp.asarray(forward_np)
    forward_t = jnp.asarray(np.ascontiguousarray(forward_np.T))
    inverse = jnp.asarray(inverse_np)
    inverse_t = jnp.asarray(np.ascontiguousarray(inverse_np.T))
    own_cycles = lax.dynamic_slice_in_dim(cycle_table, position * ROWS, ROWS)
    dft = 2 * ROWS * 256 * NLON * CH
    leg = 2 * 16 * 128 * 128 * CH
    mlp = 2 * ROWS * NLON * CH * HID

    saved_blocks = call(coeffs_kernel, [BLOCKS], [saved, forward_t], flops=dft)[0]
    saved_at_orders = exchange(saved_blocks, SP)
    fresh_blocks = call(coeffs_kernel, [BLOCKS], [fresh, forward_t], flops=dft)[0]

    lat_live = (cycle_table < NLAT).astype(F32)
    colatitude = math.pi * (jnp.minimum(cycle_table, NLAT - 1).astype(F32) + 0.5) / NLAT
    sine = jnp.sin(colatitude)
    geo = jnp.stack(
        [jnp.cos(colatitude), jnp.log(sine), math.pi / NLAT * sine * lat_live, lat_live]
    )
    order_rows = lax.dynamic_index_in_dim(jnp.asarray(orders_np), position, 0, keepdims=False)
    tables = jax.ShapeDtypeStruct((ROWS, LANES, LANES), BF16)
    ana, syn = call(
        tables_kernel,
        [tables, tables],
        [geo, order_rows],
        [pltpu.VMEM((LANES * 8, LANES), F32)],
        flops=4_000_000,
    )

    spectra_shape = jax.ShapeDtypeStruct((ROWS, LANES, 2 * CH), F32)
    values_fresh, spectra = call(
        saved_spectral_kernel,
        [PAIRED, spectra_shape],
        [saved_at_orders, ana, syn, filt, fresh_blocks],
        SPECTRAL_SCRATCH,
        flops=leg,
    )
    values_fresh = exchange(values_fresh, SP)

    narrow = jax.ShapeDtypeStruct((ROWS * NLON, CH), BF16)
    wide = jax.ShapeDtypeStruct((ROWS * NLON, HID), BF16)
    grad_values, grad_mixed, *grad_operands = call(
        mlp_back_kernel,
        [BLOCKS, jax.ShapeDtypeStruct((ROWS, NLON, CH), F32), narrow, narrow, wide, wide],
        [saved, values_fresh, cotangent, inverse, inverse_t, expand, contract, own_cycles],
        flops=3 * mlp + 2 * dft,
        transcendentals=2 * ROWS * NLON * HID,
        smem=(7,),
    )
    grads_at_orders = exchange(grad_values, SP)
    fresh_values = call(
        fresh_spectral_kernel, [BLOCKS], [values_fresh, ana, syn, filt], SPECTRAL_SCRATCH, flops=leg
    )[0]
    shares = call(
        weight_grads_kernel,
        [jax.ShapeDtypeStruct((2, 4, HID // 4, CH), BF16)],
        grad_operands,
        flops=2 * mlp,
    )[0]
    share_blocks = share_blocks_of(shares)

    coeffs_fresh = call(
        spectral_back_kernel,
        [TRIPLE],
        [grads_at_orders, spectra, ana, syn, filt, fresh_values, share_blocks],
        SPECTRAL_SCRATCH,
        flops=leg,
    )[0]
    coeffs_fresh = exchange(coeffs_fresh, SP)
    share, filter_piece = call(
        piece_kernel,
        [jax.ShapeDtypeStruct((2, 8, CH), F32), jax.ShapeDtypeStruct((4, 8, CH), F32)],
        [coeffs_fresh],
    )
    filter_piece = exchange(filter_piece, "dp")
    input_grad = call(
        input_grad_kernel,
        [TOKENS],
        [coeffs_fresh, grad_mixed, forward, own_cycles],
        flops=dft,
        smem=(3,),
    )[0]
    filter_piece, _ = lax.optimization_barrier((filter_piece, input_grad))
    pieces = call(
        spread_kernel, [jax.ShapeDtypeStruct((PEERS // 2, 24, CH), BF16)], [share, filter_piece]
    )[0]
    pieces = exchange(pieces, "sp_0")
    other_pieces = lax.ppermute(pieces, "sp_1", CORE_SWAP)
    sent_back = from_behind(input_grad, "pipe", -1)
    block = call(
        mlp_kernel,
        [TOKENS],
        [fresh, coeffs_fresh, inverse, expand, contract, own_cycles],
        flops=2 * mlp + dft,
        transcendentals=ROWS * NLON * HID,
        smem=(5,),
    )[0]
    next_input = from_behind(block, "pipe", 1)
    part = jax.ShapeDtypeStruct((HID // 4, CH), F32)
    core = lax.axis_index("sp_1").astype(jnp.int32)[None]
    expand_grad, reduce_grad, filter_grad, next_input, sent_back = call(
        result_kernel,
        [part, part, jax.ShapeDtypeStruct((2, NLAT, CH), F32), TOKENS, TOKENS],
        [pieces, other_pieces, core, next_input, sent_back],
        smem=(2,),
    )
    return (
        next_input[None, None],
        sent_back[None, None],
        expand_grad.T[None],
        reduce_grad[None],
        filter_grad[None],
    )


def solution(mesh):
    finer = Mesh(
        mesh.devices.reshape(mesh.shape["pipe"], 16, 2, mesh.shape["dp"]),
        ("pipe", "sp_0", "sp_1", "dp"),
    )
    in_specs = (
        P("pipe", "dp", SP, None, None),
        P("pipe", "dp", SP, None, None),
        P("pipe", "dp", SP, None, None),
        P("pipe", None, None),
        P("pipe", None, None),
        P("pipe", None, None, None),
        P(),
    )
    out_specs = (
        P("pipe", "dp", SP, None, None),
        P("pipe", "dp", SP, None, None),
        P("pipe", None, "dp"),
        P("pipe", "dp", None),
        P("pipe", None, None, None),
    )
    forward, inverse = fourier_constants()
    program = functools.partial(on_device, forward, inverse, order_constants())
    return jax.shard_map(
        program, mesh=finer, in_specs=in_specs, out_specs=out_specs, check_vma=False
    )
```

```python
import functools
import math

import jax
import jax.numpy as jnp
import numpy as np
from jax import lax
from jax.experimental import pallas as pl
from jax.experimental.pallas import tpu as pltpu
from jax.sharding import Mesh
from jax.sharding import PartitionSpec as P

NLAT = 120
NLON = 240
CH = 128
HID = 768
ROWS = 4
PEERS = 32
VMEM_LIMIT = 16 * 1024 * 1024
LANES = 128
SP = ("sp_0", "sp_1")

ROOT_HALF = 0.7071067811865476
INV_ROOT_TAU = 0.3989422804014327
F32 = jnp.float32
BF16 = jnp.bfloat16


def fourier_constants():
    order = np.arange(128)
    live = (order < NLAT).astype(np.float64)
    value = np.minimum(order, NLAT - 1)
    phase = 2.0 * math.pi / NLON * ((np.arange(NLON)[:, None] * value[None, :]) % NLON)
    scaled = live * (2.0 * math.pi / NLON)
    forward = np.stack([np.cos(phase) * scaled, -np.sin(phase) * scaled], axis=1)
    factor = np.where(value == 0, 1.0, 2.0) * live / (2.0 * math.pi)
    inverse = np.stack([np.cos(phase) * factor, -np.sin(phase) * factor], axis=1)

    def arranged(table):
        table = table.reshape(NLON, 2, PEERS, ROWS).transpose(0, 2, 1, 3)
        return table.reshape(NLON, 256).astype(np.float32).astype(jnp.bfloat16)

    return arranged(forward), arranged(inverse)


def order_constants():
    table = np.zeros((PEERS, 3, 8, LANES), np.float32)
    for position in range(PEERS):
        for row in range(8):
            slot = position * ROWS + row % ROWS
            m = min(slot, NLAT - 1)
            log_start = 0.5 * (
                math.log((2.0 * m + 1.0) / (4.0 * math.pi))
                + math.lgamma(2.0 * m + 1.0)
                - 2.0 * math.lgamma(m + 1.0)
                - m * math.log(4.0)
            )
            table[position, 0, row] = m
            table[position, 1, row] = log_start
            table[position, 2, row] = float(slot < NLAT)
    return table


def tables_kernel(geo_ref, order_ref, ana_ref, syn_ref, work_ref):
    shape = (8, LANES)
    cosine = jnp.broadcast_to(geo_ref[0:1, :], shape)
    log_sine = jnp.broadcast_to(geo_ref[1:2, :], shape)
    weight = geo_ref[2:3, :]
    m = order_ref[0]
    keep = order_ref[2] * jnp.broadcast_to(geo_ref[3:4, :], shape)
    starting = jnp.exp(order_ref[1] + m * log_sine)
    squares = m * m
    previous = jnp.zeros(shape, F32)
    earlier = previous
    for degree in range(NLAT):
        upper = max(4.0 * degree * degree - 1.0, 0.0)
        lower = max(4.0 * (degree - 1.0) ** 2 - 1.0, 1.0)
        ratio_main = jnp.sqrt(upper / jnp.maximum(float(degree * degree) - squares, 1.0))
        ratio_back = jnp.sqrt(jnp.maximum((degree - 1.0) ** 2 - squares, 0.0) / lower)
        rising = ratio_main * (cosine * previous - ratio_back * earlier)
        current = jnp.where(m == float(degree), starting, jnp.where(m < float(degree), rising, 0.0))
        work_ref[degree * 8 : degree * 8 + 8, :] = current * keep
        previous, earlier = current, previous
    work_ref[NLAT * 8 :, :] = jnp.zeros((LANES * 8 - NLAT * 8, LANES), F32)
    for t in range(ROWS):
        table = work_ref[pl.ds(t, LANES, stride=8), :]
        syn_ref[t] = table.astype(BF16)
        ana_ref[t] = (table * weight).astype(BF16)


def to_blocks(out_ref, half, pair):
    blocks = [part.reshape(PEERS, 8, CH) for part in pair]
    out_ref[:, 16 * half : 16 * half + 16, :] = jnp.concatenate(blocks, axis=1).astype(BF16)


def from_blocks(block_ref, half):
    pair = block_ref[:, 16 * half : 16 * half + 16, :].astype(F32)
    return [pair[:, 8 * h : 8 * h + 8].reshape(256, CH).astype(BF16) for h in range(2)]


def matmul(left, right, dims=((1,), (0,))):
    return lax.dot_general(left, right, (dims, ((), ())), preferred_element_type=F32)


def fetch(source, target, sem):
    copy = pltpu.make_async_copy(source, target, sem)
    copy.start()
    return copy


def saved_coeffs_kernel(x_hbm, forward_hbm, out_ref, x_ref, forward_ref, sems):
    table = fetch(forward_hbm, forward_ref, sems.at[ROWS])
    cycles = [fetch(x_hbm.at[j], x_ref.at[j], sems.at[j]) for j in range(ROWS)]
    table.wait()
    for half in range(2):
        cycles[2 * half].wait()
        cycles[2 * half + 1].wait()
        to_blocks(out_ref, half, [matmul(forward_ref[...], x_ref[2 * half + h]) for h in range(2)])


def fresh_coeffs_kernel(x_ref, forward_ref, *rest):
    count = len(rest) // 2
    out_ref = rest[count]
    for source, target in zip(rest[:count], rest[count + 1 :]):
        target[...] = source[...]
    for half in range(2):
        to_blocks(out_ref, half, [matmul(forward_ref[...], x_ref[2 * half + h]) for h in range(2)])


def padded_filter(filt_ref):
    rest = jnp.zeros((LANES - NLAT, CH), F32)
    return [jnp.concatenate([filt_ref[part], rest], axis=0) for part in range(2)]


def spectral(came_ref, goes_ref, ana_ref, syn_ref, filt_ref, spectra_ref=None):
    real, imag = padded_filter(filt_ref)
    for t in range(ROWS):
        parts = [came_ref[pl.ds(r * ROWS + t, LANES, stride=8), :] for r in range(2)]
        spectra = matmul(ana_ref[t], jnp.concatenate(parts, axis=1).astype(BF16))
        if spectra_ref is not None:
            spectra_ref[t] = spectra
        first, second = spectra[:, :CH], spectra[:, CH:]
        filtered = jnp.concatenate(
            [real * first - imag * second, real * second + imag * first], axis=1
        ).astype(BF16)
        values = matmul(syn_ref[t], filtered, ((0,), (0,)))
        for r in range(2):
            goes_ref[pl.ds(r * ROWS + t, LANES, stride=8), :] = values[:, r * CH : (r + 1) * CH]


def saved_spectral_kernel(
    arrived_ref, ana_ref, syn_ref, filt_ref, beside_ref, out_ref, spectra_ref, came_ref, goes_ref
):
    out_ref[:, 32:, :] = beside_ref[...]
    came_ref[...] = arrived_ref[...].reshape(LANES * 8, CH).astype(F32)
    spectral(came_ref, goes_ref, ana_ref, syn_ref, filt_ref, spectra_ref)
    out_ref[:, :32, :] = goes_ref[...].reshape(PEERS, 32, CH).astype(BF16)


def fresh_spectral_kernel(
    arrived_ref, ana_ref, syn_ref, filt_ref, beside_ref, out_ref, came_ref, goes_ref
):
    out_ref[:, :32, :] = beside_ref[...]
    came_ref[...] = arrived_ref[:, 32:, :].reshape(LANES * 8, CH).astype(F32)
    spectral(came_ref, goes_ref, ana_ref, syn_ref, filt_ref)
    out_ref[:, 32:, :] = goes_ref[...].reshape(PEERS, 32, CH).astype(BF16)


def spectral_back_kernel(
    arrived_ref,
    spectra_ref,
    ana_ref,
    syn_ref,
    filt_ref,
    shares_ref,
    out_ref,
    came_ref,
    goes_ref,
):
    came_ref[...] = arrived_ref[:, :32, :].reshape(LANES * 8, CH).astype(F32)
    real, imag = padded_filter(filt_ref)
    total_real = jnp.zeros((LANES, CH), F32)
    total_imag = jnp.zeros((LANES, CH), F32)
    for t in range(ROWS):
        parts = [came_ref[pl.ds(r * ROWS + t, LANES, stride=8), :] for r in range(2)]
        grads = matmul(syn_ref[t], jnp.concatenate(parts, axis=1).astype(BF16))
        first, second = grads[:, :CH], grads[:, CH:]
        spectra = spectra_ref[t]
        s_first, s_second = spectra[:, :CH], spectra[:, CH:]
        total_real = total_real + (first * s_first + second * s_second)
        total_imag = total_imag + (second * s_first - first * s_second)
        grad_spectra = jnp.concatenate(
            [real * first + imag * second, real * second - imag * first], axis=1
        ).astype(BF16)
        coeffs = matmul(ana_ref[t], grad_spectra, ((0,), (0,)))
        for r in range(2):
            goes_ref[pl.ds(r * ROWS + t, LANES, stride=8), :] = coeffs[:, r * CH : (r + 1) * CH]
    out_ref[:, :32, :] = goes_ref[...].reshape(PEERS, 32, CH).astype(BF16)
    filter_part = jnp.concatenate([total_real, total_imag], axis=0).reshape(PEERS, 8, CH)
    sums = jnp.concatenate([shares_ref[...].astype(F32), filter_part], axis=1)
    out_ref[:, 32:, :] = sums.astype(BF16)


def live(cycle_ref, j):
    return jnp.where(cycle_ref[j] < NLAT, 1.0, 0.0).astype(F32)


def mlp_kernel(x_ref, values_ref, inverse_ref, expand_ref, reduce_ref, cycle_ref, out_ref):
    for half in range(2):
        values = from_blocks(values_ref, 2 + half)
        for h in range(2):
            j = 2 * half + h
            mixed = x_ref[j].astype(F32) + matmul(inverse_ref[...], values[h])
            pre = matmul(mixed.astype(BF16), expand_ref[...])
            hidden = (0.5 * pre * (1.0 + lax.erf(pre * ROOT_HALF))).astype(BF16)
            result = mixed + matmul(hidden, reduce_ref[...])
            out_ref[j] = (result * live(cycle_ref, j)).astype(BF16)


def mlp_back_kernel(
    x_ref,
    values_ref,
    cotangent_ref,
    inverse_ref,
    inverse_t_ref,
    expand_ref,
    reduce_ref,
    cycle_ref,
    out_ref,
    grad_mixed_ref,
    shares_ref,
    mixed_ref,
    masked_ref,
    hidden_ref,
    grad_pre_ref,
):
    for half in range(2):
        values = from_blocks(values_ref, half)
        grad_values = []
        for h in range(2):
            j = 2 * half + h
            rows = slice(j * NLON, (j + 1) * NLON)
            mixed = x_ref[j].astype(F32) + matmul(inverse_ref[...], values[h])
            mixed_b = mixed.astype(BF16)
            masked_f = cotangent_ref[j].astype(F32) * live(cycle_ref, j)
            masked = masked_f.astype(BF16)
            mixed_ref[rows, :] = mixed_b
            masked_ref[rows, :] = masked
            pre = matmul(mixed_b, expand_ref[...])
            normal = 0.5 * (1.0 + lax.erf(pre * ROOT_HALF))
            hidden_ref[rows, :] = (pre * normal).astype(BF16)
            slope = normal + pre * jnp.exp(-0.5 * pre * pre) * INV_ROOT_TAU
            grad_hidden = matmul(masked, reduce_ref[...], ((1,), (1,)))
            grad_pre = (grad_hidden * slope).astype(BF16)
            grad_pre_ref[rows, :] = grad_pre
            grad_mixed = masked_f + matmul(grad_pre, expand_ref[...], ((1,), (1,)))
            grad_mixed_ref[j] = grad_mixed
            grad_values.append(matmul(inverse_t_ref[...], grad_mixed.astype(BF16)))
        to_blocks(out_ref, half, grad_values)
    quarter = HID // 4
    pairs = ((grad_pre_ref, mixed_ref), (hidden_ref, masked_ref))
    for side, (wide_ref, narrow_ref) in enumerate(pairs):
        grad = matmul(wide_ref[...], narrow_ref[...], ((0,), (0,))).astype(BF16)
        for d in range(4):
            shares_ref[side, d] = grad[d * quarter : (d + 1) * quarter]


def input_grad_kernel(coeffs_ref, grad_mixed_ref, forward_ref, cycle_ref, out_ref):
    for half in range(2):
        values = from_blocks(coeffs_ref, half)
        for h in range(2):
            j = 2 * half + h
            total = grad_mixed_ref[j] + matmul(forward_ref[...], values[h])
            out_ref[j] = (total * live(cycle_ref, j)).astype(BF16)


def piece_kernel(arrived_ref, share_ref, filter_ref):
    came = arrived_ref[:, 32:, :].astype(F32).reshape(PEERS // 2, 2, 16, CH)
    sums = came.sum(axis=0)
    share_ref[0] = sums[0, :8]
    share_ref[1] = sums[1, :8]
    filter_ref[...] = jnp.broadcast_to((sums[0, 8:] + sums[1, 8:])[None], filter_ref.shape)


def spread_kernel(share_ref, filter_ref, out_ref):
    piece = jnp.concatenate([share_ref[0], share_ref[1], filter_ref[...].sum(axis=0)], axis=0)
    out_ref[...] = jnp.broadcast_to(piece[None], out_ref.shape).astype(BF16)


def result_kernel(
    pieces_ref,
    other_ref,
    core_ref,
    next_ref,
    back_ref,
    expand_ref,
    reduce_ref,
    filter_ref,
    next_out_ref,
    back_out_ref,
):
    next_out_ref[...] = next_ref[...]
    back_out_ref[...] = back_ref[...]
    first = core_ref[0] == 0
    for p in range(PEERS):
        mine, other = pieces_ref[p // 2].astype(F32), other_ref[p // 2].astype(F32)
        piece = jnp.where(first, mine, other) if p % 2 == 0 else jnp.where(first, other, mine)
        expand_ref[p * 6 : p * 6 + 6, :] = piece[:6]
        reduce_ref[p * 6 : p * 6 + 6, :] = piece[8:14]
        side, at = divmod(p, PEERS // 2)
        if at < NLAT // 8:
            filter_ref[side, at * 8 : at * 8 + 8, :] = piece[16:]


def call(
    kernel, outs, args, scratch=(), flops=0, transcendentals=0, smem=(), hbm=(), limit=VMEM_LIMIT
):
    places = {n: pltpu.SMEM for n in smem} | {n: pl.ANY for n in hbm}
    specs = [pl.BlockSpec(memory_space=places.get(n, pltpu.VMEM)) for n in range(len(args))]
    moved = sum(a.size * a.dtype.itemsize for a in (*args, *outs))
    return pl.pallas_call(
        kernel,
        out_shape=outs,
        in_specs=specs,
        out_specs=[pl.BlockSpec(memory_space=pltpu.VMEM)] * len(outs),
        scratch_shapes=list(scratch),
        compiler_params=pltpu.CompilerParams(vmem_limit_bytes=limit),
        cost_estimate=pl.CostEstimate(
            flops=flops, bytes_accessed=moved, transcendentals=transcendentals
        ),
    )(*args)


PAIRED = jax.ShapeDtypeStruct((PEERS, 64, CH), BF16)
SUMMED = jax.ShapeDtypeStruct((PEERS, 48, CH), BF16)
BLOCKS = jax.ShapeDtypeStruct((PEERS, 32, CH), BF16)
TOKENS = jax.ShapeDtypeStruct((ROWS, NLON, CH), BF16)
SPECTRAL_SCRATCH = (pltpu.VMEM((LANES * 8, CH), F32), pltpu.VMEM((LANES * 8, CH), F32))


CORE_SWAP = [(0, 1), (1, 0)]


def exchange(blocks, axes):
    return lax.all_to_all(blocks, axes, split_axis=0, concat_axis=0, tiled=True)


def from_behind(block, axis, distance):
    devices = range(lax.axis_size(axis))
    route = [(i - distance, i) for i in devices if i - distance in devices]
    return lax.ppermute(block, axis, route)


def halved(blocks, axis, route, kept):
    mine = lax.dynamic_index_in_dim(blocks, kept, 0, keepdims=False)
    sent = lax.dynamic_index_in_dim(blocks, 1 - kept, 0, keepdims=False)
    came = lax.ppermute(sent, axis, route)
    return (mine.astype(F32) + came.astype(F32)).astype(BF16)


def around(block, axis, distance):
    count = lax.axis_size(axis)
    return lax.ppermute(block, axis, [(i, (i + distance) % count) for i in range(count)])


def scattered_total(blocks, axis):
    count = lax.axis_size(axis)
    me = lax.axis_index(axis)

    def block_of(distance):
        return lax.dynamic_index_in_dim(blocks, (me + distance) % count, 0, keepdims=False)

    came = [around(block_of(k), axis, k) for k in range(1, count)]
    return sum((block.astype(F32) for block in came), block_of(0).astype(F32))


def share_blocks_of(shares):
    kept = halved(shares, "sp_1", CORE_SWAP, lax.axis_index("sp_1"))
    kept = scattered_total(kept, "dp").astype(BF16)
    return jnp.pad(kept.reshape(PEERS, 6, CH), ((0, 0), (0, 2), (0, 0)))


def on_device(
    forward_np,
    inverse_np,
    orders_np,
    fresh_input,
    saved_input,
    output_grad,
    expand_weight,
    reduce_weight,
    filter_weight,
    cycle_table,
):
    position = lax.axis_index(SP)
    fresh, saved, cotangent = fresh_input[0, 0], saved_input[0, 0], output_grad[0, 0]
    expand, contract, filt = expand_weight[0], reduce_weight[0], filter_weight[0]
    forward = jnp.asarray(forward_np)
    forward_t = jnp.asarray(np.ascontiguousarray(forward_np.T))
    inverse = jnp.asarray(inverse_np)
    inverse_t = jnp.asarray(np.ascontiguousarray(inverse_np.T))
    own_cycles = lax.dynamic_slice_in_dim(cycle_table, position * ROWS, ROWS)
    dft = 2 * ROWS * 256 * NLON * CH
    leg = 2 * 16 * 128 * 128 * CH
    mlp = 2 * ROWS * NLON * CH * HID

    saved_blocks = call(
        saved_coeffs_kernel,
        [BLOCKS],
        [saved, forward_t],
        (
            pltpu.VMEM((ROWS, NLON, CH), BF16),
            pltpu.VMEM((256, NLON), BF16),
            pltpu.SemaphoreType.DMA((ROWS + 1,)),
        ),
        flops=dft,
        hbm=(0, 1),
        limit=60 * 1024 * 1024,
    )[0]
    saved_at_orders = exchange(saved_blocks, SP)
    kept = [inverse, inverse_t, expand, contract]
    fresh_blocks, inverse, inverse_t, expand, contract = call(
        fresh_coeffs_kernel,
        [BLOCKS] + [jax.ShapeDtypeStruct(k.shape, BF16) for k in kept],
        [fresh, forward_t, *kept],
        flops=dft,
    )

    lat_live = (cycle_table < NLAT).astype(F32)
    colatitude = math.pi * (jnp.minimum(cycle_table, NLAT - 1).astype(F32) + 0.5) / NLAT
    sine = jnp.sin(colatitude)
    geo = jnp.stack(
        [jnp.cos(colatitude), jnp.log(sine), math.pi / NLAT * sine * lat_live, lat_live]
    )
    order_rows = lax.dynamic_index_in_dim(jnp.asarray(orders_np), position, 0, keepdims=False)
    tables = jax.ShapeDtypeStruct((ROWS, LANES, LANES), BF16)
    ana, syn = call(
        tables_kernel,
        [tables, tables],
        [geo, order_rows],
        [pltpu.VMEM((LANES * 8, LANES), F32)],
        flops=4_000_000,
    )

    spectra_shape = jax.ShapeDtypeStruct((ROWS, LANES, 2 * CH), F32)
    values_fresh, spectra = call(
        saved_spectral_kernel,
        [PAIRED, spectra_shape],
        [saved_at_orders, ana, syn, filt, fresh_blocks],
        SPECTRAL_SCRATCH,
        flops=leg,
    )
    values_fresh = exchange(values_fresh, SP)

    narrow = pltpu.VMEM((ROWS * NLON, CH), BF16)
    wide = pltpu.VMEM((ROWS * NLON, HID), BF16)
    grad_values, grad_mixed, shares = call(
        mlp_back_kernel,
        [
            BLOCKS,
            jax.ShapeDtypeStruct((ROWS, NLON, CH), F32),
            jax.ShapeDtypeStruct((2, 4, HID // 4, CH), BF16),
        ],
        [saved, values_fresh, cotangent, inverse, inverse_t, expand, contract, own_cycles],
        [narrow, narrow, wide, wide],
        flops=5 * mlp + 2 * dft,
        transcendentals=2 * ROWS * NLON * HID,
        smem=(7,),
    )
    grads_fresh = call(
        fresh_spectral_kernel,
        [PAIRED],
        [values_fresh, ana, syn, filt, grad_values],
        SPECTRAL_SCRATCH,
        flops=leg,
    )[0]
    grads_fresh = exchange(grads_fresh, SP)
    share_blocks = share_blocks_of(shares)

    block = call(
        mlp_kernel,
        [TOKENS],
        [fresh, grads_fresh, inverse, expand, contract, own_cycles],
        flops=2 * mlp + dft,
        transcendentals=ROWS * NLON * HID,
        smem=(5,),
    )[0]
    next_input = from_behind(block, "pipe", 1)
    coeffs_summed = call(
        spectral_back_kernel,
        [SUMMED],
        [grads_fresh, spectra, ana, syn, filt, share_blocks],
        SPECTRAL_SCRATCH,
        flops=leg,
    )[0]
    coeffs_summed = exchange(coeffs_summed, SP)
    coeffs_summed, next_input = lax.optimization_barrier((coeffs_summed, next_input))
    share, filter_piece = call(
        piece_kernel,
        [jax.ShapeDtypeStruct((2, 8, CH), F32), jax.ShapeDtypeStruct((4, 8, CH), F32)],
        [coeffs_summed],
    )
    filter_piece = exchange(filter_piece, "dp")
    input_grad = call(
        input_grad_kernel,
        [TOKENS],
        [coeffs_summed, grad_mixed, forward, own_cycles],
        flops=dft,
        smem=(3,),
    )[0]
    filter_piece, _ = lax.optimization_barrier((filter_piece, input_grad))
    pieces = call(
        spread_kernel, [jax.ShapeDtypeStruct((PEERS // 2, 24, CH), BF16)], [share, filter_piece]
    )[0]
    pieces = exchange(pieces, "sp_0")
    other_pieces = lax.ppermute(pieces, "sp_1", CORE_SWAP)
    sent_back = from_behind(input_grad, "pipe", -1)
    part = jax.ShapeDtypeStruct((HID // 4, CH), F32)
    core = lax.axis_index("sp_1").astype(jnp.int32)[None]
    expand_grad, reduce_grad, filter_grad, next_input, sent_back = call(
        result_kernel,
        [part, part, jax.ShapeDtypeStruct((2, NLAT, CH), F32), TOKENS, TOKENS],
        [pieces, other_pieces, core, next_input, sent_back],
        smem=(2,),
    )
    return (
        next_input[None, None],
        sent_back[None, None],
        expand_grad.T[None],
        reduce_grad[None],
        filter_grad[None],
    )


def solution(mesh):
    finer = Mesh(
        mesh.devices.reshape(mesh.shape["pipe"], 16, 2, mesh.shape["dp"]),
        ("pipe", "sp_0", "sp_1", "dp"),
    )
    in_specs = (
        P("pipe", "dp", SP, None, None),
        P("pipe", "dp", SP, None, None),
        P("pipe", "dp", SP, None, None),
        P("pipe", None, None),
        P("pipe", None, None),
        P("pipe", None, None, None),
        P(),
    )
    out_specs = (
        P("pipe", "dp", SP, None, None),
        P("pipe", "dp", SP, None, None),
        P("pipe", None, "dp"),
        P("pipe", "dp", None),
        P("pipe", None, None, None),
    )
    forward, inverse = fourier_constants()
    program = functools.partial(on_device, forward, inverse, order_constants())
    return jax.shard_map(
        program, mesh=finer, in_specs=in_specs, out_specs=out_specs, check_vma=False
    )
```

```python
import functools
import math

import jax
import jax.numpy as jnp
import numpy as np
from jax import lax
from jax.experimental import pallas as pl
from jax.experimental.pallas import tpu as pltpu
from jax.sharding import Mesh
from jax.sharding import PartitionSpec as P

NLAT = 120
NLON = 240
CH = 128
HID = 768
ROWS = 4
PEERS = 32
VMEM_LIMIT = 16 * 1024 * 1024
LANES = 128
SP = ("sp_0", "sp_1")

ROOT_HALF = 0.7071067811865476
INV_ROOT_TAU = 0.3989422804014327
F32 = jnp.float32
BF16 = jnp.bfloat16


def fourier_constants():
    order = np.arange(128)
    live = (order < NLAT).astype(np.float64)
    value = np.minimum(order, NLAT - 1)
    phase = 2.0 * math.pi / NLON * ((np.arange(NLON)[:, None] * value[None, :]) % NLON)
    scaled = live * (2.0 * math.pi / NLON)
    forward = np.stack([np.cos(phase) * scaled, -np.sin(phase) * scaled], axis=1)
    factor = np.where(value == 0, 1.0, 2.0) * live / (2.0 * math.pi)
    inverse = np.stack([np.cos(phase) * factor, -np.sin(phase) * factor], axis=1)

    def arranged(table):
        table = table.reshape(NLON, 2, PEERS, ROWS).transpose(0, 2, 1, 3)
        return table.reshape(NLON, 256).astype(np.float32).astype(jnp.bfloat16)

    return arranged(forward), arranged(inverse)


def order_constants():
    table = np.zeros((PEERS, 3, 8, LANES), np.float32)
    for position in range(PEERS):
        for row in range(8):
            slot = position * ROWS + row % ROWS
            m = min(slot, NLAT - 1)
            log_start = 0.5 * (
                math.log((2.0 * m + 1.0) / (4.0 * math.pi))
                + math.lgamma(2.0 * m + 1.0)
                - 2.0 * math.lgamma(m + 1.0)
                - m * math.log(4.0)
            )
            table[position, 0, row] = m
            table[position, 1, row] = log_start
            table[position, 2, row] = float(slot < NLAT)
    return table


def tables_kernel(geo_ref, order_ref, ana_ref, syn_ref, work_ref):
    shape = (8, LANES)
    cosine = jnp.broadcast_to(geo_ref[0:1, :], shape)
    log_sine = jnp.broadcast_to(geo_ref[1:2, :], shape)
    weight = geo_ref[2:3, :]
    m = order_ref[0]
    keep = order_ref[2] * jnp.broadcast_to(geo_ref[3:4, :], shape)
    starting = jnp.exp(order_ref[1] + m * log_sine)
    squares = m * m
    previous = jnp.zeros(shape, F32)
    earlier = previous
    for degree in range(NLAT):
        upper = max(4.0 * degree * degree - 1.0, 0.0)
        lower = max(4.0 * (degree - 1.0) ** 2 - 1.0, 1.0)
        ratio_main = jnp.sqrt(upper / jnp.maximum(float(degree * degree) - squares, 1.0))
        ratio_back = jnp.sqrt(jnp.maximum((degree - 1.0) ** 2 - squares, 0.0) / lower)
        rising = ratio_main * (cosine * previous - ratio_back * earlier)
        current = jnp.where(m == float(degree), starting, jnp.where(m < float(degree), rising, 0.0))
        work_ref[degree * 8 : degree * 8 + 8, :] = current * keep
        previous, earlier = current, previous
    work_ref[NLAT * 8 :, :] = jnp.zeros((LANES * 8 - NLAT * 8, LANES), F32)
    for t in range(ROWS):
        table = work_ref[pl.ds(t, LANES, stride=8), :]
        syn_ref[t] = table.astype(BF16)
        ana_ref[t] = (table * weight).astype(BF16)


def to_blocks(out_ref, half, pair):
    blocks = [part.reshape(PEERS, 8, CH) for part in pair]
    out_ref[:, 16 * half : 16 * half + 16, :] = jnp.concatenate(blocks, axis=1).astype(BF16)


def from_blocks(block_ref, half):
    pair = block_ref[:, 16 * half : 16 * half + 16, :].astype(F32)
    return [pair[:, 8 * h : 8 * h + 8].reshape(256, CH).astype(BF16) for h in range(2)]


def matmul(left, right, dims=((1,), (0,))):
    return lax.dot_general(left, right, (dims, ((), ())), preferred_element_type=F32)


def fetch(source, target, sem):
    copy = pltpu.make_async_copy(source, target, sem)
    copy.start()
    return copy


def saved_coeffs_kernel(x_hbm, forward_hbm, out_ref, x_ref, forward_ref, sems):
    table = fetch(forward_hbm, forward_ref, sems.at[ROWS])
    cycles = [fetch(x_hbm.at[j], x_ref.at[j], sems.at[j]) for j in range(ROWS)]
    table.wait()
    for half in range(2):
        cycles[2 * half].wait()
        cycles[2 * half + 1].wait()
        to_blocks(out_ref, half, [matmul(forward_ref[...], x_ref[2 * half + h]) for h in range(2)])


def fresh_coeffs_kernel(x_ref, forward_ref, *rest):
    count = len(rest) // 2
    out_ref = rest[count]
    for source, target in zip(rest[:count], rest[count + 1 :]):
        target[...] = source[...]
    for half in range(2):
        to_blocks(out_ref, half, [matmul(forward_ref[...], x_ref[2 * half + h]) for h in range(2)])


def padded_filter(filt_ref):
    rest = jnp.zeros((LANES - NLAT, CH), F32)
    return [jnp.concatenate([filt_ref[part], rest], axis=0) for part in range(2)]


def spectral(came_ref, goes_ref, ana_ref, syn_ref, filt_ref, spectra_ref=None):
    real, imag = padded_filter(filt_ref)
    for t in range(ROWS):
        parts = [came_ref[pl.ds(r * ROWS + t, LANES, stride=8), :] for r in range(2)]
        spectra = matmul(ana_ref[t], jnp.concatenate(parts, axis=1).astype(BF16))
        if spectra_ref is not None:
            spectra_ref[t] = spectra
        first, second = spectra[:, :CH], spectra[:, CH:]
        filtered = jnp.concatenate(
            [real * first - imag * second, real * second + imag * first], axis=1
        ).astype(BF16)
        values = matmul(syn_ref[t], filtered, ((0,), (0,)))
        for r in range(2):
            goes_ref[pl.ds(r * ROWS + t, LANES, stride=8), :] = values[:, r * CH : (r + 1) * CH]


def saved_spectral_kernel(
    arrived_ref, ana_ref, syn_ref, filt_ref, beside_ref, out_ref, spectra_ref, came_ref, goes_ref
):
    out_ref[:, 32:, :] = beside_ref[...]
    came_ref[...] = arrived_ref[...].reshape(LANES * 8, CH).astype(F32)
    spectral(came_ref, goes_ref, ana_ref, syn_ref, filt_ref, spectra_ref)
    out_ref[:, :32, :] = goes_ref[...].reshape(PEERS, 32, CH).astype(BF16)


def fresh_spectral_kernel(
    arrived_ref, ana_ref, syn_ref, filt_ref, beside_ref, out_ref, came_ref, goes_ref
):
    out_ref[:, :32, :] = beside_ref[...]
    came_ref[...] = arrived_ref[:, 32:, :].reshape(LANES * 8, CH).astype(F32)
    spectral(came_ref, goes_ref, ana_ref, syn_ref, filt_ref)
    out_ref[:, 32:, :] = goes_ref[...].reshape(PEERS, 32, CH).astype(BF16)


def spectral_back_kernel(
    arrived_ref,
    spectra_ref,
    ana_ref,
    syn_ref,
    filt_ref,
    shares_ref,
    out_ref,
    came_ref,
    goes_ref,
):
    came_ref[...] = arrived_ref[:, :32, :].reshape(LANES * 8, CH).astype(F32)
    real, imag = padded_filter(filt_ref)
    total_real = jnp.zeros((LANES, CH), F32)
    total_imag = jnp.zeros((LANES, CH), F32)
    for t in range(ROWS):
        parts = [came_ref[pl.ds(r * ROWS + t, LANES, stride=8), :] for r in range(2)]
        grads = matmul(syn_ref[t], jnp.concatenate(parts, axis=1).astype(BF16))
        first, second = grads[:, :CH], grads[:, CH:]
        spectra = spectra_ref[t]
        s_first, s_second = spectra[:, :CH], spectra[:, CH:]
        total_real = total_real + (first * s_first + second * s_second)
        total_imag = total_imag + (second * s_first - first * s_second)
        grad_spectra = jnp.concatenate(
            [real * first + imag * second, real * second - imag * first], axis=1
        ).astype(BF16)
        coeffs = matmul(ana_ref[t], grad_spectra, ((0,), (0,)))
        for r in range(2):
            goes_ref[pl.ds(r * ROWS + t, LANES, stride=8), :] = coeffs[:, r * CH : (r + 1) * CH]
    out_ref[:, :32, :] = goes_ref[...].reshape(PEERS, 32, CH).astype(BF16)
    filter_part = jnp.concatenate([total_real, total_imag], axis=0).reshape(PEERS, 8, CH)
    sums = jnp.concatenate([shares_ref[...].astype(F32), filter_part], axis=1)
    out_ref[:, 32:, :] = sums.astype(BF16)


def live(cycle_ref, j):
    return jnp.where(cycle_ref[j] < NLAT, 1.0, 0.0).astype(F32)


def mlp_kernel(x_ref, values_ref, inverse_ref, expand_ref, reduce_ref, cycle_ref, out_ref):
    for half in range(2):
        values = from_blocks(values_ref, 2 + half)
        for h in range(2):
            j = 2 * half + h
            mixed = x_ref[j].astype(F32) + matmul(inverse_ref[...], values[h])
            pre = matmul(mixed.astype(BF16), expand_ref[...])
            hidden = (0.5 * pre * (1.0 + lax.erf(pre * ROOT_HALF))).astype(BF16)
            result = mixed + matmul(hidden, reduce_ref[...])
            out_ref[j] = (result * live(cycle_ref, j)).astype(BF16)


def mlp_back_kernel(
    x_ref,
    values_ref,
    cotangent_ref,
    inverse_ref,
    inverse_t_ref,
    expand_ref,
    reduce_ref,
    cycle_ref,
    out_ref,
    grad_mixed_ref,
    shares_ref,
    mixed_ref,
    masked_ref,
    hidden_ref,
    grad_pre_ref,
):
    for half in range(2):
        values = from_blocks(values_ref, half)
        grad_values = []
        for h in range(2):
            j = 2 * half + h
            rows = slice(j * NLON, (j + 1) * NLON)
            mixed = x_ref[j].astype(F32) + matmul(inverse_ref[...], values[h])
            mixed_b = mixed.astype(BF16)
            masked_f = cotangent_ref[j].astype(F32) * live(cycle_ref, j)
            masked = masked_f.astype(BF16)
            mixed_ref[rows, :] = mixed_b
            masked_ref[rows, :] = masked
            pre = matmul(mixed_b, expand_ref[...])
            normal = 0.5 * (1.0 + lax.erf(pre * ROOT_HALF))
            hidden_ref[rows, :] = (pre * normal).astype(BF16)
            slope = normal + pre * jnp.exp(-0.5 * pre * pre) * INV_ROOT_TAU
            grad_hidden = matmul(masked, reduce_ref[...], ((1,), (1,)))
            grad_pre = (grad_hidden * slope).astype(BF16)
            grad_pre_ref[rows, :] = grad_pre
            grad_mixed = masked_f + matmul(grad_pre, expand_ref[...], ((1,), (1,)))
            grad_mixed_ref[j] = grad_mixed
            grad_values.append(matmul(inverse_t_ref[...], grad_mixed.astype(BF16)))
        to_blocks(out_ref, half, grad_values)
    quarter = HID // 4
    pairs = ((grad_pre_ref, mixed_ref), (hidden_ref, masked_ref))
    for side, (wide_ref, narrow_ref) in enumerate(pairs):
        grad = matmul(wide_ref[...], narrow_ref[...], ((0,), (0,))).astype(BF16)
        for d in range(4):
            shares_ref[side, d] = grad[d * quarter : (d + 1) * quarter]


def input_grad_kernel(coeffs_ref, grad_mixed_ref, forward_ref, cycle_ref, out_ref):
    for half in range(2):
        values = from_blocks(coeffs_ref, half)
        for h in range(2):
            j = 2 * half + h
            total = grad_mixed_ref[j] + matmul(forward_ref[...], values[h])
            out_ref[j] = (total * live(cycle_ref, j)).astype(BF16)


def piece_kernel(arrived_ref, out_ref):
    came = arrived_ref[:, 32:, :].astype(F32).reshape(PEERS // 2, 2, 16, CH)
    sums = came.sum(axis=0)
    piece = jnp.concatenate([sums[0, :8], sums[1, :8], sums[0, 8:] + sums[1, 8:]], axis=0)
    out_ref[...] = jnp.broadcast_to(piece[None], out_ref.shape).astype(BF16)


def filter_rows_kernel(pieces_ref, out_ref):
    rows = pieces_ref[...].astype(F32)[:, 16:].reshape(128, CH).astype(BF16)
    out_ref[...] = jnp.broadcast_to(rows[None], out_ref.shape)


def result_kernel(
    pieces_ref,
    other_ref,
    filter_rows_ref,
    core_ref,
    next_ref,
    back_ref,
    expand_ref,
    reduce_ref,
    filter_ref,
    next_out_ref,
    back_out_ref,
):
    next_out_ref[...] = next_ref[...]
    back_out_ref[...] = back_ref[...]
    first = core_ref[0] == 0
    filters = [filter_rows_ref[4 * c : 4 * c + 4].astype(F32).sum(axis=0) for c in range(2)]
    for p in range(PEERS):
        mine, other = pieces_ref[p // 2].astype(F32), other_ref[p // 2].astype(F32)
        piece = jnp.where(first, mine, other) if p % 2 == 0 else jnp.where(first, other, mine)
        expand_ref[p * 6 : p * 6 + 6, :] = piece[:6]
        reduce_ref[p * 6 : p * 6 + 6, :] = piece[8:14]
        side, at = divmod(p, PEERS // 2)
        if at < NLAT // 8:
            rows = filters[p % 2][p // 2 * 8 : p // 2 * 8 + 8]
            filter_ref[side, at * 8 : at * 8 + 8, :] = rows


def call(
    kernel, outs, args, scratch=(), flops=0, transcendentals=0, smem=(), hbm=(), limit=VMEM_LIMIT
):
    places = {n: pltpu.SMEM for n in smem} | {n: pl.ANY for n in hbm}
    specs = [pl.BlockSpec(memory_space=places.get(n, pltpu.VMEM)) for n in range(len(args))]
    moved = sum(a.size * a.dtype.itemsize for a in (*args, *outs))
    return pl.pallas_call(
        kernel,
        out_shape=outs,
        in_specs=specs,
        out_specs=[pl.BlockSpec(memory_space=pltpu.VMEM)] * len(outs),
        scratch_shapes=list(scratch),
        compiler_params=pltpu.CompilerParams(vmem_limit_bytes=limit),
        cost_estimate=pl.CostEstimate(
            flops=flops, bytes_accessed=moved, transcendentals=transcendentals
        ),
    )(*args)


PAIRED = jax.ShapeDtypeStruct((PEERS, 64, CH), BF16)
SUMMED = jax.ShapeDtypeStruct((PEERS, 48, CH), BF16)
BLOCKS = jax.ShapeDtypeStruct((PEERS, 32, CH), BF16)
TOKENS = jax.ShapeDtypeStruct((ROWS, NLON, CH), BF16)
SPECTRAL_SCRATCH = (pltpu.VMEM((LANES * 8, CH), F32), pltpu.VMEM((LANES * 8, CH), F32))


CORE_SWAP = [(0, 1), (1, 0)]


def exchange(blocks, axes):
    return lax.all_to_all(blocks, axes, split_axis=0, concat_axis=0, tiled=True)


def from_behind(block, axis, distance):
    devices = range(lax.axis_size(axis))
    route = [(i - distance, i) for i in devices if i - distance in devices]
    return lax.ppermute(block, axis, route)


def halved(blocks, axis, route, kept):
    mine = lax.dynamic_index_in_dim(blocks, kept, 0, keepdims=False)
    sent = lax.dynamic_index_in_dim(blocks, 1 - kept, 0, keepdims=False)
    came = lax.ppermute(sent, axis, route)
    return (mine.astype(F32) + came.astype(F32)).astype(BF16)


def around(block, axis, distance):
    count = lax.axis_size(axis)
    return lax.ppermute(block, axis, [(i, (i + distance) % count) for i in range(count)])


def scattered_total(blocks, axis):
    count = lax.axis_size(axis)
    me = lax.axis_index(axis)

    def block_of(distance):
        return lax.dynamic_index_in_dim(blocks, (me + distance) % count, 0, keepdims=False)

    came = [around(block_of(k), axis, k) for k in range(1, count)]
    return sum((block.astype(F32) for block in came), block_of(0).astype(F32))


def share_blocks_of(shares):
    kept = halved(shares, "sp_1", CORE_SWAP, lax.axis_index("sp_1"))
    kept = scattered_total(kept, "dp").astype(BF16)
    return jnp.pad(kept.reshape(PEERS, 6, CH), ((0, 0), (0, 2), (0, 0)))


def on_device(
    forward_np,
    inverse_np,
    orders_np,
    fresh_input,
    saved_input,
    output_grad,
    expand_weight,
    reduce_weight,
    filter_weight,
    cycle_table,
):
    position = lax.axis_index(SP)
    fresh, saved, cotangent = fresh_input[0, 0], saved_input[0, 0], output_grad[0, 0]
    expand, contract, filt = expand_weight[0], reduce_weight[0], filter_weight[0]
    forward = jnp.asarray(forward_np)
    forward_t = jnp.asarray(np.ascontiguousarray(forward_np.T))
    inverse = jnp.asarray(inverse_np)
    inverse_t = jnp.asarray(np.ascontiguousarray(inverse_np.T))
    own_cycles = lax.dynamic_slice_in_dim(cycle_table, position * ROWS, ROWS)
    dft = 2 * ROWS * 256 * NLON * CH
    leg = 2 * 16 * 128 * 128 * CH
    mlp = 2 * ROWS * NLON * CH * HID

    saved_blocks = call(
        saved_coeffs_kernel,
        [BLOCKS],
        [saved, forward_t],
        (
            pltpu.VMEM((ROWS, NLON, CH), BF16),
            pltpu.VMEM((256, NLON), BF16),
            pltpu.SemaphoreType.DMA((ROWS + 1,)),
        ),
        flops=dft,
        hbm=(0, 1),
        limit=60 * 1024 * 1024,
    )[0]
    saved_at_orders = exchange(saved_blocks, SP)
    kept = [inverse, inverse_t, expand, contract]
    fresh_blocks, inverse, inverse_t, expand, contract = call(
        fresh_coeffs_kernel,
        [BLOCKS] + [jax.ShapeDtypeStruct(k.shape, BF16) for k in kept],
        [fresh, forward_t, *kept],
        flops=dft,
    )

    lat_live = (cycle_table < NLAT).astype(F32)
    colatitude = math.pi * (jnp.minimum(cycle_table, NLAT - 1).astype(F32) + 0.5) / NLAT
    sine = jnp.sin(colatitude)
    geo = jnp.stack(
        [jnp.cos(colatitude), jnp.log(sine), math.pi / NLAT * sine * lat_live, lat_live]
    )
    order_rows = lax.dynamic_index_in_dim(jnp.asarray(orders_np), position, 0, keepdims=False)
    tables = jax.ShapeDtypeStruct((ROWS, LANES, LANES), BF16)
    ana, syn = call(
        tables_kernel,
        [tables, tables],
        [geo, order_rows],
        [pltpu.VMEM((LANES * 8, LANES), F32)],
        flops=4_000_000,
    )

    spectra_shape = jax.ShapeDtypeStruct((ROWS, LANES, 2 * CH), F32)
    values_fresh, spectra = call(
        saved_spectral_kernel,
        [PAIRED, spectra_shape],
        [saved_at_orders, ana, syn, filt, fresh_blocks],
        SPECTRAL_SCRATCH,
        flops=leg,
    )
    values_fresh = exchange(values_fresh, SP)

    narrow = pltpu.VMEM((ROWS * NLON, CH), BF16)
    wide = pltpu.VMEM((ROWS * NLON, HID), BF16)
    grad_values, grad_mixed, shares = call(
        mlp_back_kernel,
        [
            BLOCKS,
            jax.ShapeDtypeStruct((ROWS, NLON, CH), F32),
            jax.ShapeDtypeStruct((2, 4, HID // 4, CH), BF16),
        ],
        [saved, values_fresh, cotangent, inverse, inverse_t, expand, contract, own_cycles],
        [narrow, narrow, wide, wide],
        flops=5 * mlp + 2 * dft,
        transcendentals=2 * ROWS * NLON * HID,
        smem=(7,),
    )
    grads_fresh = call(
        fresh_spectral_kernel,
        [PAIRED],
        [values_fresh, ana, syn, filt, grad_values],
        SPECTRAL_SCRATCH,
        flops=leg,
    )[0]
    grads_fresh = exchange(grads_fresh, SP)
    share_blocks = share_blocks_of(shares)

    block = call(
        mlp_kernel,
        [TOKENS],
        [fresh, grads_fresh, inverse, expand, contract, own_cycles],
        flops=2 * mlp + dft,
        transcendentals=ROWS * NLON * HID,
        smem=(5,),
    )[0]
    next_input = from_behind(block, "pipe", 1)
    coeffs_summed = call(
        spectral_back_kernel,
        [SUMMED],
        [grads_fresh, spectra, ana, syn, filt, share_blocks],
        SPECTRAL_SCRATCH,
        flops=leg,
    )[0]
    coeffs_summed = exchange(coeffs_summed, SP)
    coeffs_summed, next_input = lax.optimization_barrier((coeffs_summed, next_input))
    pieces = call(
        piece_kernel, [jax.ShapeDtypeStruct((PEERS // 2, 24, CH), BF16)], [coeffs_summed]
    )[0]
    pieces = exchange(pieces, "sp_0")
    filter_rows = call(
        filter_rows_kernel, [jax.ShapeDtypeStruct((8, 128, CH), BF16)], [pieces]
    )[0]
    filter_rows = exchange(filter_rows, ("sp_1", "dp"))
    other_pieces = lax.ppermute(pieces, "sp_1", CORE_SWAP)
    input_grad = call(
        input_grad_kernel,
        [TOKENS],
        [coeffs_summed, grad_mixed, forward, own_cycles],
        flops=dft,
        smem=(3,),
    )[0]
    sent_back = from_behind(input_grad, "pipe", -1)
    part = jax.ShapeDtypeStruct((HID // 4, CH), F32)
    core = lax.axis_index("sp_1").astype(jnp.int32)[None]
    expand_grad, reduce_grad, filter_grad, next_input, sent_back = call(
        result_kernel,
        [part, part, jax.ShapeDtypeStruct((2, NLAT, CH), F32), TOKENS, TOKENS],
        [pieces, other_pieces, filter_rows, core, next_input, sent_back],
        smem=(3,),
    )
    return (
        next_input[None, None],
        sent_back[None, None],
        expand_grad.T[None],
        reduce_grad[None],
        filter_grad[None],
    )


def solution(mesh):
    finer = Mesh(
        mesh.devices.reshape(mesh.shape["pipe"], 16, 2, mesh.shape["dp"]),
        ("pipe", "sp_0", "sp_1", "dp"),
    )
    in_specs = (
        P("pipe", "dp", SP, None, None),
        P("pipe", "dp", SP, None, None),
        P("pipe", "dp", SP, None, None),
        P("pipe", None, None),
        P("pipe", None, None),
        P("pipe", None, None, None),
        P(),
    )
    out_specs = (
        P("pipe", "dp", SP, None, None),
        P("pipe", "dp", SP, None, None),
        P("pipe", None, "dp"),
        P("pipe", "dp", None),
        P("pipe", None, None, None),
    )
    forward, inverse = fourier_constants()
    program = functools.partial(on_device, forward, inverse, order_constants())
    return jax.shard_map(
        program, mesh=finer, in_specs=in_specs, out_specs=out_specs, check_vma=False
    )
```

```python
import functools
import math

import jax
import jax.numpy as jnp
import numpy as np
from jax import lax
from jax.experimental import pallas as pl
from jax.experimental.pallas import tpu as pltpu
from jax.sharding import Mesh
from jax.sharding import PartitionSpec as P

NLAT = 120
NLON = 240
CH = 128
HID = 768
ROWS = 4
PEERS = 32
VMEM_LIMIT = 16 * 1024 * 1024
LANES = 128
SP = ("sp_0", "sp_1")

ROOT_HALF = 0.7071067811865476
INV_ROOT_TAU = 0.3989422804014327
F32 = jnp.float32
BF16 = jnp.bfloat16


def fourier_constants():
    order = np.arange(128)
    live = (order < NLAT).astype(np.float64)
    value = np.minimum(order, NLAT - 1)
    phase = 2.0 * math.pi / NLON * ((np.arange(NLON)[:, None] * value[None, :]) % NLON)
    scaled = live * (2.0 * math.pi / NLON)
    forward = np.stack([np.cos(phase) * scaled, -np.sin(phase) * scaled], axis=1)
    factor = np.where(value == 0, 1.0, 2.0) * live / (2.0 * math.pi)
    inverse = np.stack([np.cos(phase) * factor, -np.sin(phase) * factor], axis=1)

    def arranged(table):
        table = table.reshape(NLON, 2, PEERS, ROWS).transpose(0, 2, 1, 3)
        return table.reshape(NLON, 256).astype(np.float32).astype(jnp.bfloat16)

    return arranged(forward), arranged(inverse)


def order_constants():
    table = np.zeros((PEERS, 3, 8, LANES), np.float32)
    for position in range(PEERS):
        for row in range(8):
            slot = position * ROWS + row % ROWS
            m = min(slot, NLAT - 1)
            log_start = 0.5 * (
                math.log((2.0 * m + 1.0) / (4.0 * math.pi))
                + math.lgamma(2.0 * m + 1.0)
                - 2.0 * math.lgamma(m + 1.0)
                - m * math.log(4.0)
            )
            table[position, 0, row] = m
            table[position, 1, row] = log_start
            table[position, 2, row] = float(slot < NLAT)
    return table


def normal_and_density(u):
    bell = jnp.exp(-0.5 * u * u)
    t = 1.0 / (1.0 + (0.3275911 * ROOT_HALF) * jnp.abs(u))
    series = (
        (((0.5 * 1.061405429 * t - 0.5 * 1.453152027) * t + 0.5 * 1.421413741) * t - 0.5 * 0.284496736)
        * t
        + 0.5 * 0.254829592
    )
    below = series * t * bell
    return jnp.where(u < 0.0, below, 1.0 - below), bell


def tables_kernel(geo_ref, order_ref, ana_ref, syn_ref, work_ref):
    shape = (8, LANES)
    cosine = jnp.broadcast_to(geo_ref[0:1, :], shape)
    log_sine = jnp.broadcast_to(geo_ref[1:2, :], shape)
    weight = geo_ref[2:3, :]
    m = order_ref[0]
    keep = order_ref[2] * jnp.broadcast_to(geo_ref[3:4, :], shape)
    starting = jnp.exp(order_ref[1] + m * log_sine)
    squares = m * m
    previous = jnp.zeros(shape, F32)
    earlier = previous
    for degree in range(NLAT):
        upper = max(4.0 * degree * degree - 1.0, 0.0)
        lower = max(4.0 * (degree - 1.0) ** 2 - 1.0, 1.0)
        ratio_main = jnp.sqrt(upper / jnp.maximum(float(degree * degree) - squares, 1.0))
        ratio_back = jnp.sqrt(jnp.maximum((degree - 1.0) ** 2 - squares, 0.0) / lower)
        rising = ratio_main * (cosine * previous - ratio_back * earlier)
        current = jnp.where(m == float(degree), starting, jnp.where(m < float(degree), rising, 0.0))
        work_ref[degree * 8 : degree * 8 + 8, :] = current * keep
        previous, earlier = current, previous
    work_ref[NLAT * 8 :, :] = jnp.zeros((LANES * 8 - NLAT * 8, LANES), F32)
    for t in range(ROWS):
        table = work_ref[pl.ds(t, LANES, stride=8), :]
        syn_ref[t] = table.astype(BF16)
        ana_ref[t] = (table * weight).astype(BF16)


def to_blocks(out_ref, half, pair):
    blocks = [part.reshape(PEERS, 8, CH) for part in pair]
    out_ref[:, 16 * half : 16 * half + 16, :] = jnp.concatenate(blocks, axis=1).astype(BF16)


def from_blocks(block_ref, half):
    pair = block_ref[:, 16 * half : 16 * half + 16, :].astype(F32)
    return [pair[:, 8 * h : 8 * h + 8].reshape(256, CH).astype(BF16) for h in range(2)]


def matmul(left, right, dims=((1,), (0,))):
    return lax.dot_general(left, right, (dims, ((), ())), preferred_element_type=F32)


def fetch(source, target, sem):
    copy = pltpu.make_async_copy(source, target, sem)
    copy.start()
    return copy


def saved_coeffs_kernel(x_hbm, forward_hbm, out_ref, x_ref, forward_ref, sems):
    table = fetch(forward_hbm, forward_ref, sems.at[ROWS])
    cycles = [fetch(x_hbm.at[j], x_ref.at[j], sems.at[j]) for j in range(ROWS)]
    table.wait()
    for half in range(2):
        cycles[2 * half].wait()
        cycles[2 * half + 1].wait()
        to_blocks(out_ref, half, [matmul(forward_ref[...], x_ref[2 * half + h]) for h in range(2)])


def fresh_coeffs_kernel(x_ref, forward_ref, *rest):
    count = len(rest) // 2
    out_ref = rest[count]
    for source, target in zip(rest[:count], rest[count + 1 :]):
        target[...] = source[...]
    for half in range(2):
        to_blocks(out_ref, half, [matmul(forward_ref[...], x_ref[2 * half + h]) for h in range(2)])


def padded_filter(filt_ref):
    rest = jnp.zeros((LANES - NLAT, CH), F32)
    return [jnp.concatenate([filt_ref[part], rest], axis=0) for part in range(2)]


def spectral(came_ref, goes_ref, ana_ref, syn_ref, filt_ref, spectra_ref=None):
    real, imag = padded_filter(filt_ref)
    for t in range(ROWS):
        parts = [came_ref[pl.ds(r * ROWS + t, LANES, stride=8), :] for r in range(2)]
        spectra = matmul(ana_ref[t], jnp.concatenate(parts, axis=1).astype(BF16))
        if spectra_ref is not None:
            spectra_ref[t] = spectra
        first, second = spectra[:, :CH], spectra[:, CH:]
        filtered = jnp.concatenate(
            [real * first - imag * second, real * second + imag * first], axis=1
        ).astype(BF16)
        values = matmul(syn_ref[t], filtered, ((0,), (0,)))
        for r in range(2):
            goes_ref[pl.ds(r * ROWS + t, LANES, stride=8), :] = values[:, r * CH : (r + 1) * CH]


def saved_spectral_kernel(
    arrived_ref, ana_ref, syn_ref, filt_ref, beside_ref, out_ref, spectra_ref, came_ref, goes_ref
):
    out_ref[:, 32:, :] = beside_ref[...]
    came_ref[...] = arrived_ref[...].reshape(LANES * 8, CH).astype(F32)
    spectral(came_ref, goes_ref, ana_ref, syn_ref, filt_ref, spectra_ref)
    out_ref[:, :32, :] = goes_ref[...].reshape(PEERS, 32, CH).astype(BF16)


def fresh_spectral_kernel(
    arrived_ref, ana_ref, syn_ref, filt_ref, beside_ref, out_ref, came_ref, goes_ref
):
    out_ref[:, :32, :] = beside_ref[...]
    came_ref[...] = arrived_ref[:, 32:, :].reshape(LANES * 8, CH).astype(F32)
    spectral(came_ref, goes_ref, ana_ref, syn_ref, filt_ref)
    out_ref[:, 32:, :] = goes_ref[...].reshape(PEERS, 32, CH).astype(BF16)


def spectral_back_kernel(
    arrived_ref,
    spectra_ref,
    ana_ref,
    syn_ref,
    filt_ref,
    shares_ref,
    out_ref,
    came_ref,
    goes_ref,
):
    came_ref[...] = arrived_ref[:, :32, :].reshape(LANES * 8, CH).astype(F32)
    real, imag = padded_filter(filt_ref)
    total_real = jnp.zeros((LANES, CH), F32)
    total_imag = jnp.zeros((LANES, CH), F32)
    for t in range(ROWS):
        parts = [came_ref[pl.ds(r * ROWS + t, LANES, stride=8), :] for r in range(2)]
        grads = matmul(syn_ref[t], jnp.concatenate(parts, axis=1).astype(BF16))
        first, second = grads[:, :CH], grads[:, CH:]
        spectra = spectra_ref[t]
        s_first, s_second = spectra[:, :CH], spectra[:, CH:]
        total_real = total_real + (first * s_first + second * s_second)
        total_imag = total_imag + (second * s_first - first * s_second)
        grad_spectra = jnp.concatenate(
            [real * first + imag * second, real * second - imag * first], axis=1
        ).astype(BF16)
        coeffs = matmul(ana_ref[t], grad_spectra, ((0,), (0,)))
        for r in range(2):
            goes_ref[pl.ds(r * ROWS + t, LANES, stride=8), :] = coeffs[:, r * CH : (r + 1) * CH]
    out_ref[:, :32, :] = goes_ref[...].reshape(PEERS, 32, CH).astype(BF16)
    filter_part = jnp.concatenate([total_real, total_imag], axis=0).reshape(PEERS, 8, CH)
    sums = jnp.concatenate([shares_ref[...].astype(F32), filter_part], axis=1)
    out_ref[:, 32:, :] = sums.astype(BF16)


def live(cycle_ref, j):
    return jnp.where(cycle_ref[j] < NLAT, 1.0, 0.0).astype(F32)


def mlp_kernel(x_ref, values_ref, inverse_ref, expand_ref, reduce_ref, cycle_ref, out_ref):
    for half in range(2):
        values = from_blocks(values_ref, 2 + half)
        for h in range(2):
            j = 2 * half + h
            mixed = x_ref[j].astype(F32) + matmul(inverse_ref[...], values[h])
            pre = matmul(mixed.astype(BF16), expand_ref[...])
            hidden = (pre * normal_and_density(pre)[0]).astype(BF16)
            result = mixed + matmul(hidden, reduce_ref[...])
            out_ref[j] = (result * live(cycle_ref, j)).astype(BF16)


def mlp_back_kernel(
    x_ref,
    values_ref,
    cotangent_ref,
    inverse_ref,
    inverse_t_ref,
    expand_ref,
    reduce_ref,
    cycle_ref,
    out_ref,
    grad_mixed_ref,
    shares_ref,
    mixed_ref,
    masked_ref,
    hidden_ref,
    grad_pre_ref,
):
    for half in range(2):
        values = from_blocks(values_ref, half)
        grad_values = []
        for h in range(2):
            j = 2 * half + h
            rows = slice(j * NLON, (j + 1) * NLON)
            mixed = x_ref[j].astype(F32) + matmul(inverse_ref[...], values[h])
            mixed_b = mixed.astype(BF16)
            masked_f = cotangent_ref[j].astype(F32) * live(cycle_ref, j)
            masked = masked_f.astype(BF16)
            mixed_ref[rows, :] = mixed_b
            masked_ref[rows, :] = masked
            pre = matmul(mixed_b, expand_ref[...])
            normal, bell = normal_and_density(pre)
            hidden_ref[rows, :] = (pre * normal).astype(BF16)
            slope = normal + pre * bell * INV_ROOT_TAU
            grad_hidden = matmul(masked, reduce_ref[...], ((1,), (1,)))
            grad_pre = (grad_hidden * slope).astype(BF16)
            grad_pre_ref[rows, :] = grad_pre
            grad_mixed = masked_f + matmul(grad_pre, expand_ref[...], ((1,), (1,)))
            grad_mixed_ref[j] = grad_mixed
            grad_values.append(matmul(inverse_t_ref[...], grad_mixed.astype(BF16)))
        to_blocks(out_ref, half, grad_values)
    quarter = HID // 4
    pairs = ((grad_pre_ref, mixed_ref), (hidden_ref, masked_ref))
    for side, (wide_ref, narrow_ref) in enumerate(pairs):
        grad = matmul(wide_ref[...], narrow_ref[...], ((0,), (0,))).astype(BF16)
        for d in range(4):
            shares_ref[side, d] = grad[d * quarter : (d + 1) * quarter]


def input_grad_kernel(coeffs_ref, grad_mixed_ref, forward_ref, cycle_ref, out_ref):
    for half in range(2):
        values = from_blocks(coeffs_ref, half)
        for h in range(2):
            j = 2 * half + h
            total = grad_mixed_ref[j] + matmul(forward_ref[...], values[h])
            out_ref[j] = (total * live(cycle_ref, j)).astype(BF16)


def piece_kernel(arrived_ref, out_ref):
    came = arrived_ref[:, 32:, :].astype(F32).reshape(PEERS // 2, 2, 16, CH)
    sums = came.sum(axis=0)
    piece = jnp.concatenate([sums[0, :8], sums[1, :8], sums[0, 8:] + sums[1, 8:]], axis=0)
    out_ref[...] = jnp.broadcast_to(piece[None], out_ref.shape).astype(BF16)


def filter_rows_kernel(pieces_ref, out_ref):
    rows = pieces_ref[...].astype(F32)[:, 16:].reshape(128, CH).astype(BF16)
    out_ref[...] = jnp.broadcast_to(rows[None], out_ref.shape)


def result_kernel(
    pieces_ref,
    other_ref,
    filter_rows_ref,
    core_ref,
    next_ref,
    back_ref,
    expand_ref,
    reduce_ref,
    filter_ref,
    next_out_ref,
    back_out_ref,
):
    next_out_ref[...] = next_ref[...]
    back_out_ref[...] = back_ref[...]
    first = core_ref[0] == 0
    filters = [filter_rows_ref[4 * c : 4 * c + 4].astype(F32).sum(axis=0) for c in range(2)]
    for p in range(PEERS):
        mine, other = pieces_ref[p // 2].astype(F32), other_ref[p // 2].astype(F32)
        piece = jnp.where(first, mine, other) if p % 2 == 0 else jnp.where(first, other, mine)
        expand_ref[p * 6 : p * 6 + 6, :] = piece[:6]
        reduce_ref[p * 6 : p * 6 + 6, :] = piece[8:14]
        side, at = divmod(p, PEERS // 2)
        if at < NLAT // 8:
            rows = filters[p % 2][p // 2 * 8 : p // 2 * 8 + 8]
            filter_ref[side, at * 8 : at * 8 + 8, :] = rows


def call(
    kernel, outs, args, scratch=(), flops=0, transcendentals=0, smem=(), hbm=(), limit=VMEM_LIMIT
):
    places = {n: pltpu.SMEM for n in smem} | {n: pl.ANY for n in hbm}
    specs = [pl.BlockSpec(memory_space=places.get(n, pltpu.VMEM)) for n in range(len(args))]
    moved = sum(a.size * a.dtype.itemsize for a in (*args, *outs))
    return pl.pallas_call(
        kernel,
        out_shape=outs,
        in_specs=specs,
        out_specs=[pl.BlockSpec(memory_space=pltpu.VMEM)] * len(outs),
        scratch_shapes=list(scratch),
        compiler_params=pltpu.CompilerParams(vmem_limit_bytes=limit),
        cost_estimate=pl.CostEstimate(
            flops=flops, bytes_accessed=moved, transcendentals=transcendentals
        ),
    )(*args)


PAIRED = jax.ShapeDtypeStruct((PEERS, 64, CH), BF16)
SUMMED = jax.ShapeDtypeStruct((PEERS, 48, CH), BF16)
BLOCKS = jax.ShapeDtypeStruct((PEERS, 32, CH), BF16)
TOKENS = jax.ShapeDtypeStruct((ROWS, NLON, CH), BF16)
SPECTRAL_SCRATCH = (pltpu.VMEM((LANES * 8, CH), F32), pltpu.VMEM((LANES * 8, CH), F32))


CORE_SWAP = [(0, 1), (1, 0)]


def exchange(blocks, axes):
    return lax.all_to_all(blocks, axes, split_axis=0, concat_axis=0, tiled=True)


def from_behind(block, axis, distance):
    devices = range(lax.axis_size(axis))
    route = [(i - distance, i) for i in devices if i - distance in devices]
    return lax.ppermute(block, axis, route)


def halved(blocks, axis, route, kept):
    mine = lax.dynamic_index_in_dim(blocks, kept, 0, keepdims=False)
    sent = lax.dynamic_index_in_dim(blocks, 1 - kept, 0, keepdims=False)
    came = lax.ppermute(sent, axis, route)
    return (mine.astype(F32) + came.astype(F32)).astype(BF16)


def around(block, axis, distance):
    count = lax.axis_size(axis)
    return lax.ppermute(block, axis, [(i, (i + distance) % count) for i in range(count)])


def scattered_total(blocks, axis):
    count = lax.axis_size(axis)
    me = lax.axis_index(axis)

    def block_of(distance):
        return lax.dynamic_index_in_dim(blocks, (me + distance) % count, 0, keepdims=False)

    came = [around(block_of(k), axis, k) for k in range(1, count)]
    return sum((block.astype(F32) for block in came), block_of(0).astype(F32))


def share_blocks_of(shares):
    kept = halved(shares, "sp_1", CORE_SWAP, lax.axis_index("sp_1"))
    kept = scattered_total(kept, "dp").astype(BF16)
    return jnp.pad(kept.reshape(PEERS, 6, CH), ((0, 0), (0, 2), (0, 0)))


def on_device(
    forward_np,
    inverse_np,
    orders_np,
    fresh_input,
    saved_input,
    output_grad,
    expand_weight,
    reduce_weight,
    filter_weight,
    cycle_table,
):
    position = lax.axis_index(SP)
    fresh, saved, cotangent = fresh_input[0, 0], saved_input[0, 0], output_grad[0, 0]
    expand, contract, filt = expand_weight[0], reduce_weight[0], filter_weight[0]
    forward = jnp.asarray(forward_np)
    forward_t = jnp.asarray(np.ascontiguousarray(forward_np.T))
    inverse = jnp.asarray(inverse_np)
    inverse_t = jnp.asarray(np.ascontiguousarray(inverse_np.T))
    own_cycles = lax.dynamic_slice_in_dim(cycle_table, position * ROWS, ROWS)
    dft = 2 * ROWS * 256 * NLON * CH
    leg = 2 * 16 * 128 * 128 * CH
    mlp = 2 * ROWS * NLON * CH * HID

    saved_blocks = call(
        saved_coeffs_kernel,
        [BLOCKS],
        [saved, forward_t],
        (
            pltpu.VMEM((ROWS, NLON, CH), BF16),
            pltpu.VMEM((256, NLON), BF16),
            pltpu.SemaphoreType.DMA((ROWS + 1,)),
        ),
        flops=dft,
        hbm=(0, 1),
        limit=60 * 1024 * 1024,
    )[0]
    saved_at_orders = exchange(saved_blocks, SP)
    kept = [inverse, inverse_t, expand, contract]
    fresh_blocks, inverse, inverse_t, expand, contract = call(
        fresh_coeffs_kernel,
        [BLOCKS] + [jax.ShapeDtypeStruct(k.shape, BF16) for k in kept],
        [fresh, forward_t, *kept],
        flops=dft,
    )

    lat_live = (cycle_table < NLAT).astype(F32)
    colatitude = math.pi * (jnp.minimum(cycle_table, NLAT - 1).astype(F32) + 0.5) / NLAT
    sine = jnp.sin(colatitude)
    geo = jnp.stack(
        [jnp.cos(colatitude), jnp.log(sine), math.pi / NLAT * sine * lat_live, lat_live]
    )
    order_rows = lax.dynamic_index_in_dim(jnp.asarray(orders_np), position, 0, keepdims=False)
    tables = jax.ShapeDtypeStruct((ROWS, LANES, LANES), BF16)
    ana, syn = call(
        tables_kernel,
        [tables, tables],
        [geo, order_rows],
        [pltpu.VMEM((LANES * 8, LANES), F32)],
        flops=4_000_000,
    )

    spectra_shape = jax.ShapeDtypeStruct((ROWS, LANES, 2 * CH), F32)
    values_fresh, spectra = call(
        saved_spectral_kernel,
        [PAIRED, spectra_shape],
        [saved_at_orders, ana, syn, filt, fresh_blocks],
        SPECTRAL_SCRATCH,
        flops=leg,
    )
    values_fresh = exchange(values_fresh, SP)

    narrow = pltpu.VMEM((ROWS * NLON, CH), BF16)
    wide = pltpu.VMEM((ROWS * NLON, HID), BF16)
    grad_values, grad_mixed, shares = call(
        mlp_back_kernel,
        [
            BLOCKS,
            jax.ShapeDtypeStruct((ROWS, NLON, CH), F32),
            jax.ShapeDtypeStruct((2, 4, HID // 4, CH), BF16),
        ],
        [saved, values_fresh, cotangent, inverse, inverse_t, expand, contract, own_cycles],
        [narrow, narrow, wide, wide],
        flops=5 * mlp + 2 * dft,
        transcendentals=2 * ROWS * NLON * HID,
        smem=(7,),
    )
    grads_fresh = call(
        fresh_spectral_kernel,
        [PAIRED],
        [values_fresh, ana, syn, filt, grad_values],
        SPECTRAL_SCRATCH,
        flops=leg,
    )[0]
    grads_fresh = exchange(grads_fresh, SP)
    share_blocks = share_blocks_of(shares)

    block = call(
        mlp_kernel,
        [TOKENS],
        [fresh, grads_fresh, inverse, expand, contract, own_cycles],
        flops=2 * mlp + dft,
        transcendentals=ROWS * NLON * HID,
        smem=(5,),
    )[0]
    next_input = from_behind(block, "pipe", 1)
    coeffs_summed = call(
        spectral_back_kernel,
        [SUMMED],
        [grads_fresh, spectra, ana, syn, filt, share_blocks],
        SPECTRAL_SCRATCH,
        flops=leg,
    )[0]
    coeffs_summed = exchange(coeffs_summed, SP)
    coeffs_summed, next_input = lax.optimization_barrier((coeffs_summed, next_input))
    pieces = call(
        piece_kernel, [jax.ShapeDtypeStruct((PEERS // 2, 24, CH), BF16)], [coeffs_summed]
    )[0]
    pieces = exchange(pieces, "sp_0")
    filter_rows = call(
        filter_rows_kernel, [jax.ShapeDtypeStruct((8, 128, CH), BF16)], [pieces]
    )[0]
    filter_rows = exchange(filter_rows, ("sp_1", "dp"))
    other_pieces = lax.ppermute(pieces, "sp_1", CORE_SWAP)
    input_grad = call(
        input_grad_kernel,
        [TOKENS],
        [coeffs_summed, grad_mixed, forward, own_cycles],
        flops=dft,
        smem=(3,),
    )[0]
    sent_back = from_behind(input_grad, "pipe", -1)
    part = jax.ShapeDtypeStruct((HID // 4, CH), F32)
    core = lax.axis_index("sp_1").astype(jnp.int32)[None]
    expand_grad, reduce_grad, filter_grad, next_input, sent_back = call(
        result_kernel,
        [part, part, jax.ShapeDtypeStruct((2, NLAT, CH), F32), TOKENS, TOKENS],
        [pieces, other_pieces, filter_rows, core, next_input, sent_back],
        smem=(3,),
    )
    return (
        next_input[None, None],
        sent_back[None, None],
        expand_grad.T[None],
        reduce_grad[None],
        filter_grad[None],
    )


def solution(mesh):
    finer = Mesh(
        mesh.devices.reshape(mesh.shape["pipe"], 16, 2, mesh.shape["dp"]),
        ("pipe", "sp_0", "sp_1", "dp"),
    )
    in_specs = (
        P("pipe", "dp", SP, None, None),
        P("pipe", "dp", SP, None, None),
        P("pipe", "dp", SP, None, None),
        P("pipe", None, None),
        P("pipe", None, None),
        P("pipe", None, None, None),
        P(),
    )
    out_specs = (
        P("pipe", "dp", SP, None, None),
        P("pipe", "dp", SP, None, None),
        P("pipe", None, "dp"),
        P("pipe", "dp", None),
        P("pipe", None, None, None),
    )
    forward, inverse = fourier_constants()
    program = functools.partial(on_device, forward, inverse, order_constants())
    return jax.shard_map(
        program, mesh=finer, in_specs=in_specs, out_specs=out_specs, check_vma=False
    )
```

```python
import functools
import math

import jax
import jax.numpy as jnp
import numpy as np
from jax import lax
from jax.experimental import pallas as pl
from jax.experimental.pallas import tpu as pltpu
from jax.sharding import Mesh
from jax.sharding import PartitionSpec as P

NLAT = 120
NLON = 240
CH = 128
HID = 768
ROWS = 4
PEERS = 32
VMEM_LIMIT = 16 * 1024 * 1024
LANES = 128
SP = ("sp_0", "sp_1")

ROOT_HALF = 0.7071067811865476
INV_ROOT_TAU = 0.3989422804014327
F32 = jnp.float32
BF16 = jnp.bfloat16


def fourier_constants():
    order = np.arange(128)
    live = (order < NLAT).astype(np.float64)
    value = np.minimum(order, NLAT - 1)
    phase = 2.0 * math.pi / NLON * ((np.arange(NLON)[:, None] * value[None, :]) % NLON)
    scaled = live * (2.0 * math.pi / NLON)
    forward = np.stack([np.cos(phase) * scaled, -np.sin(phase) * scaled], axis=1)
    factor = np.where(value == 0, 1.0, 2.0) * live / (2.0 * math.pi)
    inverse = np.stack([np.cos(phase) * factor, -np.sin(phase) * factor], axis=1)

    def arranged(table, places):
        table = table.reshape(NLON, 2, PEERS, ROWS).transpose(0, *places)
        return table.reshape(NLON, 256).astype(np.float32).astype(jnp.bfloat16)

    saved, fresh = (2, 1, 3), (3, 1, 2)
    return [arranged(table, places) for places in (saved, fresh) for table in (forward, inverse)]


def order_constants():
    table = np.zeros((PEERS, 3, 8, LANES), np.float32)
    for position in range(PEERS):
        for row in range(8):
            slot = position * ROWS + row % ROWS
            m = min(slot, NLAT - 1)
            log_start = 0.5 * (
                math.log((2.0 * m + 1.0) / (4.0 * math.pi))
                + math.lgamma(2.0 * m + 1.0)
                - 2.0 * math.lgamma(m + 1.0)
                - m * math.log(4.0)
            )
            table[position, 0, row] = m
            table[position, 1, row] = log_start
            table[position, 2, row] = float(slot < NLAT)
    return table


def tables_kernel(geo_ref, order_ref, ana_ref, syn_ref, work_ref):
    shape = (8, LANES)
    cosine = jnp.broadcast_to(geo_ref[0:1, :], shape)
    log_sine = jnp.broadcast_to(geo_ref[1:2, :], shape)
    weight = geo_ref[2:3, :]
    m = order_ref[0]
    keep = order_ref[2] * jnp.broadcast_to(geo_ref[3:4, :], shape)
    starting = jnp.exp(order_ref[1] + m * log_sine)
    squares = m * m
    previous = jnp.zeros(shape, F32)
    earlier = previous
    for degree in range(NLAT):
        upper = max(4.0 * degree * degree - 1.0, 0.0)
        lower = max(4.0 * (degree - 1.0) ** 2 - 1.0, 1.0)
        ratio_main = jnp.sqrt(upper / jnp.maximum(float(degree * degree) - squares, 1.0))
        ratio_back = jnp.sqrt(jnp.maximum((degree - 1.0) ** 2 - squares, 0.0) / lower)
        rising = ratio_main * (cosine * previous - ratio_back * earlier)
        current = jnp.where(m == float(degree), starting, jnp.where(m < float(degree), rising, 0.0))
        work_ref[degree * 8 : degree * 8 + 8, :] = current * keep
        previous, earlier = current, previous
    work_ref[NLAT * 8 :, :] = jnp.zeros((LANES * 8 - NLAT * 8, LANES), F32)
    for t in range(ROWS):
        table = work_ref[pl.ds(t, LANES, stride=8), :]
        syn_ref[t] = table.astype(BF16)
        ana_ref[t] = (table * weight).astype(BF16)


def to_blocks(out_ref, half, pair):
    blocks = [part.reshape(PEERS, 8, CH) for part in pair]
    out_ref[:, 16 * half : 16 * half + 16, :] = jnp.concatenate(blocks, axis=1).astype(BF16)


def from_blocks(block_ref, half):
    pair = block_ref[:, 16 * half : 16 * half + 16, :].astype(F32)
    return [pair[:, 8 * h : 8 * h + 8].reshape(256, CH).astype(BF16) for h in range(2)]


def matmul(left, right, dims=((1,), (0,))):
    return lax.dot_general(left, right, (dims, ((), ())), preferred_element_type=F32)


def fetch(source, target, sem):
    copy = pltpu.make_async_copy(source, target, sem)
    copy.start()
    return copy


def saved_coeffs_kernel(x_hbm, forward_hbm, out_ref, x_ref, forward_ref, sems):
    table = fetch(forward_hbm, forward_ref, sems.at[ROWS])
    cycles = [fetch(x_hbm.at[j], x_ref.at[j], sems.at[j]) for j in range(ROWS)]
    table.wait()
    for half in range(2):
        cycles[2 * half].wait()
        cycles[2 * half + 1].wait()
        to_blocks(out_ref, half, [matmul(forward_ref[...], x_ref[2 * half + h]) for h in range(2)])


def fresh_coeffs_kernel(x_ref, forward_ref, *rest):
    *rest, work_ref = rest
    count = len(rest) // 2 - 1
    own_ref, lent_ref = rest[count : count + 2]
    for source, target in zip(rest[:count], rest[count + 2 :]):
        target[...] = source[...]
    for j in range(ROWS):
        coeffs = matmul(forward_ref[...], x_ref[j])
        for place in range(8):
            target = pl.ds(place // 2 * 256 + j * 2 + place % 2, PEERS, stride=8)
            work_ref[target, :] = coeffs[place * PEERS : (place + 1) * PEERS]
    groups = [work_ref[256 * u : 256 * u + 256, :].reshape(PEERS, 8, CH) for u in range(ROWS)]
    own_ref[...] = jnp.concatenate(groups[:3], axis=1).astype(BF16)
    lent_ref[...] = groups[3].astype(BF16)


def padded_filter(filt_ref):
    rest = jnp.zeros((LANES - NLAT, CH), F32)
    return [jnp.concatenate([filt_ref[part], rest], axis=0) for part in range(2)]


def filter_step(spectra, real, imag):
    first, second = spectra[:, :CH], spectra[:, CH:]
    return jnp.concatenate(
        [real * first - imag * second, real * second + imag * first], axis=1
    ).astype(BF16)


def spectral(came_ref, goes_ref, ana_ref, syn_ref, filt_ref, spectra_ref):
    real, imag = padded_filter(filt_ref)
    for t in range(ROWS):
        parts = [came_ref[pl.ds(r * ROWS + t, LANES, stride=8), :] for r in range(2)]
        spectra = matmul(ana_ref[t], jnp.concatenate(parts, axis=1).astype(BF16))
        spectra_ref[t] = spectra
        values = matmul(syn_ref[t], filter_step(spectra, real, imag), ((0,), (0,)))
        for r in range(2):
            goes_ref[pl.ds(r * ROWS + t, LANES, stride=8), :] = values[:, r * CH : (r + 1) * CH]


def saved_spectral_kernel(
    arrived_ref, ana_ref, syn_ref, filt_ref, beside_ref, out_ref, spectra_ref, came_ref, goes_ref
):
    out_ref[:, 32:, :] = beside_ref[...]
    came_ref[...] = arrived_ref[...].reshape(LANES * 8, CH).astype(F32)
    spectral(came_ref, goes_ref, ana_ref, syn_ref, filt_ref, spectra_ref)
    out_ref[:, :32, :] = goes_ref[...].reshape(PEERS, 32, CH).astype(BF16)


def fresh_spectral_kernel(
    arrived_ref,
    ana_ref,
    syn_ref,
    filt_ref,
    lent_a_ref,
    lent_b_ref,
    lent_c_ref,
    last_ref,
    beside_ref,
    out_ref,
    came_ref,
    goes_ref,
):
    out_ref[:, :32, :] = beside_ref[...]
    came = arrived_ref[:, 32:, :].astype(F32)
    last = last_ref[0]
    own = padded_filter(filt_ref)
    for u, lent_ref in enumerate((lent_a_ref, lent_b_ref, lent_c_ref)):
        came_ref[256 * u : 256 * u + 256, :] = came[:, 8 * u : 8 * u + 8].reshape(256, CH)
        lent = padded_filter(lent_ref)
        real, imag = [jnp.where(last == 1, lent[part], own[part]) for part in range(2)]
        t = jnp.where(last == 1, 3, u)
        parts = [came_ref[pl.ds(256 * u + r, LANES, stride=2), :] for r in range(2)]
        spectra = matmul(ana_ref[t], jnp.concatenate(parts, axis=1).astype(BF16))
        values = matmul(syn_ref[t], filter_step(spectra, real, imag), ((0,), (0,)))
        for r in range(2):
            goes_ref[pl.ds(256 * u + r, LANES, stride=2), :] = values[:, r * CH : (r + 1) * CH]
    groups = [goes_ref[256 * u : 256 * u + 256, :].reshape(PEERS, 8, CH) for u in range(3)]
    out_ref[:, 32:, :] = jnp.concatenate(groups, axis=1).astype(BF16)


def spectral_back_kernel(
    arrived_ref,
    spectra_ref,
    ana_ref,
    syn_ref,
    filt_ref,
    shares_ref,
    out_ref,
    came_ref,
    goes_ref,
):
    came_ref[...] = arrived_ref[:, :32, :].reshape(LANES * 8, CH).astype(F32)
    real, imag = padded_filter(filt_ref)
    total_real = jnp.zeros((LANES, CH), F32)
    total_imag = jnp.zeros((LANES, CH), F32)
    for t in range(ROWS):
        parts = [came_ref[pl.ds(r * ROWS + t, LANES, stride=8), :] for r in range(2)]
        grads = matmul(syn_ref[t], jnp.concatenate(parts, axis=1).astype(BF16))
        first, second = grads[:, :CH], grads[:, CH:]
        spectra = spectra_ref[t]
        s_first, s_second = spectra[:, :CH], spectra[:, CH:]
        total_real = total_real + (first * s_first + second * s_second)
        total_imag = total_imag + (second * s_first - first * s_second)
        grad_spectra = jnp.concatenate(
            [real * first + imag * second, real * second - imag * first], axis=1
        ).astype(BF16)
        coeffs = matmul(ana_ref[t], grad_spectra, ((0,), (0,)))
        for r in range(2):
            goes_ref[pl.ds(r * ROWS + t, LANES, stride=8), :] = coeffs[:, r * CH : (r + 1) * CH]
    out_ref[:, :32, :] = goes_ref[...].reshape(PEERS, 32, CH).astype(BF16)
    filter_part = jnp.concatenate([total_real, total_imag], axis=0).reshape(PEERS, 8, CH)
    sums = jnp.concatenate([shares_ref[...].astype(F32), filter_part], axis=1)
    out_ref[:, 32:, :] = sums.astype(BF16)


def live(cycle_ref, j):
    return jnp.where(cycle_ref[j] < NLAT, 1.0, 0.0).astype(F32)


def mlp_kernel(
    x_ref,
    values_ref,
    lent_a_ref,
    lent_b_ref,
    lent_c_ref,
    inverse_ref,
    expand_ref,
    reduce_ref,
    cycle_ref,
    out_ref,
    work_ref,
):
    own = values_ref[:, 32:, :].astype(F32)
    lent = [ref[...].astype(F32) for ref in (lent_a_ref, lent_b_ref, lent_c_ref)]
    for u in range(3):
        work_ref[256 * u : 256 * u + 256, :] = own[:, 8 * u : 8 * u + 8].reshape(256, CH)
    work_ref[768:, :] = (lent[0] + lent[1] + lent[2]).reshape(256, CH)
    for j in range(ROWS):
        parts = [
            work_ref[pl.ds(place // 2 * 256 + j * 2 + place % 2, PEERS, stride=8), :]
            for place in range(8)
        ]
        values = jnp.concatenate(parts, axis=0).astype(BF16)
        mixed = x_ref[j].astype(F32) + matmul(inverse_ref[...], values)
        pre = matmul(mixed.astype(BF16), expand_ref[...])
        hidden = (0.5 * pre * (1.0 + lax.erf(pre * ROOT_HALF))).astype(BF16)
        result = mixed + matmul(hidden, reduce_ref[...])
        out_ref[j] = (result * live(cycle_ref, j)).astype(BF16)


def mlp_back_kernel(
    x_ref,
    values_ref,
    cotangent_ref,
    inverse_ref,
    inverse_t_ref,
    expand_ref,
    reduce_ref,
    cycle_ref,
    out_ref,
    grad_mixed_ref,
    shares_ref,
    mixed_ref,
    masked_ref,
    hidden_ref,
    grad_pre_ref,
):
    for half in range(2):
        values = from_blocks(values_ref, half)
        grad_values = []
        for h in range(2):
            j = 2 * half + h
            rows = slice(j * NLON, (j + 1) * NLON)
            mixed = x_ref[j].astype(F32) + matmul(inverse_ref[...], values[h])
            mixed_b = mixed.astype(BF16)
            masked_f = cotangent_ref[j].astype(F32) * live(cycle_ref, j)
            masked = masked_f.astype(BF16)
            mixed_ref[rows, :] = mixed_b
            masked_ref[rows, :] = masked
            pre = matmul(mixed_b, expand_ref[...])
            normal = 0.5 * (1.0 + lax.erf(pre * ROOT_HALF))
            hidden_ref[rows, :] = (pre * normal).astype(BF16)
            slope = normal + pre * jnp.exp(-0.5 * pre * pre) * INV_ROOT_TAU
            grad_hidden = matmul(masked, reduce_ref[...], ((1,), (1,)))
            grad_pre = (grad_hidden * slope).astype(BF16)
            grad_pre_ref[rows, :] = grad_pre
            grad_mixed = masked_f + matmul(grad_pre, expand_ref[...], ((1,), (1,)))
            grad_mixed_ref[j] = grad_mixed
            grad_values.append(matmul(inverse_t_ref[...], grad_mixed.astype(BF16)))
        to_blocks(out_ref, half, grad_values)
    quarter = HID // 4
    pairs = ((grad_pre_ref, mixed_ref), (hidden_ref, masked_ref))
    for side, (wide_ref, narrow_ref) in enumerate(pairs):
        grad = matmul(wide_ref[...], narrow_ref[...], ((0,), (0,))).astype(BF16)
        for d in range(4):
            shares_ref[side, d] = grad[d * quarter : (d + 1) * quarter]


def input_grad_kernel(coeffs_ref, grad_mixed_ref, forward_ref, cycle_ref, out_ref):
    for half in range(2):
        values = from_blocks(coeffs_ref, half)
        for h in range(2):
            j = 2 * half + h
            total = grad_mixed_ref[j] + matmul(forward_ref[...], values[h])
            out_ref[j] = (total * live(cycle_ref, j)).astype(BF16)


def piece_kernel(arrived_ref, out_ref):
    came = arrived_ref[:, 32:, :].astype(F32).reshape(PEERS // 2, 2, 16, CH)
    sums = came.sum(axis=0)
    piece = jnp.concatenate([sums[0, :8], sums[1, :8], sums[0, 8:] + sums[1, 8:]], axis=0)
    out_ref[...] = jnp.broadcast_to(piece[None], out_ref.shape).astype(BF16)


def filter_rows_kernel(pieces_ref, out_ref):
    rows = pieces_ref[...].astype(F32)[:, 16:].reshape(128, CH).astype(BF16)
    out_ref[...] = jnp.broadcast_to(rows[None], out_ref.shape)


def result_kernel(
    pieces_ref,
    other_ref,
    filter_rows_ref,
    core_ref,
    next_ref,
    back_ref,
    expand_ref,
    reduce_ref,
    filter_ref,
    next_out_ref,
    back_out_ref,
):
    next_out_ref[...] = next_ref[...]
    back_out_ref[...] = back_ref[...]
    first = core_ref[0] == 0
    filters = [filter_rows_ref[4 * c : 4 * c + 4].astype(F32).sum(axis=0) for c in range(2)]
    for p in range(PEERS):
        mine, other = pieces_ref[p // 2].astype(F32), other_ref[p // 2].astype(F32)
        piece = jnp.where(first, mine, other) if p % 2 == 0 else jnp.where(first, other, mine)
        expand_ref[p * 6 : p * 6 + 6, :] = piece[:6]
        reduce_ref[p * 6 : p * 6 + 6, :] = piece[8:14]
        side, at = divmod(p, PEERS // 2)
        if at < NLAT // 8:
            rows = filters[p % 2][p // 2 * 8 : p // 2 * 8 + 8]
            filter_ref[side, at * 8 : at * 8 + 8, :] = rows


def call(
    kernel, outs, args, scratch=(), flops=0, transcendentals=0, smem=(), hbm=(), limit=VMEM_LIMIT
):
    places = {n: pltpu.SMEM for n in smem} | {n: pl.ANY for n in hbm}
    specs = [pl.BlockSpec(memory_space=places.get(n, pltpu.VMEM)) for n in range(len(args))]
    moved = sum(a.size * a.dtype.itemsize for a in (*args, *outs))
    return pl.pallas_call(
        kernel,
        out_shape=outs,
        in_specs=specs,
        out_specs=[pl.BlockSpec(memory_space=pltpu.VMEM)] * len(outs),
        scratch_shapes=list(scratch),
        compiler_params=pltpu.CompilerParams(vmem_limit_bytes=limit),
        cost_estimate=pl.CostEstimate(
            flops=flops, bytes_accessed=moved, transcendentals=transcendentals
        ),
    )(*args)


PAIRED = jax.ShapeDtypeStruct((PEERS, 56, CH), BF16)
OWN = jax.ShapeDtypeStruct((PEERS, 24, CH), BF16)
LENT = jax.ShapeDtypeStruct((PEERS, 8, CH), BF16)
SUMMED = jax.ShapeDtypeStruct((PEERS, 48, CH), BF16)
BLOCKS = jax.ShapeDtypeStruct((PEERS, 32, CH), BF16)
TOKENS = jax.ShapeDtypeStruct((ROWS, NLON, CH), BF16)
SPECTRAL_SCRATCH = (pltpu.VMEM((LANES * 8, CH), F32), pltpu.VMEM((LANES * 8, CH), F32))


CORE_SWAP = [(0, 1), (1, 0)]


def exchange(blocks, axes):
    return lax.all_to_all(blocks, axes, split_axis=0, concat_axis=0, tiled=True)


def from_behind(block, axis, distance):
    devices = range(lax.axis_size(axis))
    route = [(i - distance, i) for i in devices if i - distance in devices]
    return lax.ppermute(block, axis, route)


def to_last(block):
    return [lax.ppermute(block, "pipe", [(p, 3)]) for p in range(3)]


def halved(blocks, axis, route, kept):
    mine = lax.dynamic_index_in_dim(blocks, kept, 0, keepdims=False)
    sent = lax.dynamic_index_in_dim(blocks, 1 - kept, 0, keepdims=False)
    came = lax.ppermute(sent, axis, route)
    return (mine.astype(F32) + came.astype(F32)).astype(BF16)


def around(block, axis, distance):
    count = lax.axis_size(axis)
    return lax.ppermute(block, axis, [(i, (i + distance) % count) for i in range(count)])


def scattered_total(blocks, axis):
    count = lax.axis_size(axis)
    me = lax.axis_index(axis)

    def block_of(distance):
        return lax.dynamic_index_in_dim(blocks, (me + distance) % count, 0, keepdims=False)

    came = [around(block_of(k), axis, k) for k in range(1, count)]
    return sum((block.astype(F32) for block in came), block_of(0).astype(F32))


def share_blocks_of(shares):
    kept = halved(shares, "sp_1", CORE_SWAP, lax.axis_index("sp_1"))
    kept = scattered_total(kept, "dp").astype(BF16)
    return jnp.pad(kept.reshape(PEERS, 6, CH), ((0, 0), (0, 2), (0, 0)))


def on_device(
    tables_np,
    orders_np,
    fresh_input,
    saved_input,
    output_grad,
    expand_weight,
    reduce_weight,
    filter_weight,
    cycle_table,
):
    position = lax.axis_index(SP)
    fresh, saved, cotangent = fresh_input[0, 0], saved_input[0, 0], output_grad[0, 0]
    expand, contract, filt = expand_weight[0], reduce_weight[0], filter_weight[0]
    forward_np, inverse_np, fresh_forward_np, fresh_inverse_np = tables_np
    forward = jnp.asarray(forward_np)
    fresh_forward_t = jnp.asarray(np.ascontiguousarray(fresh_forward_np.T))
    fresh_inverse = jnp.asarray(fresh_inverse_np)
    last = lax.axis_index("pipe") == 3
    forward_t = jnp.asarray(np.ascontiguousarray(forward_np.T))
    inverse = jnp.asarray(inverse_np)
    inverse_t = jnp.asarray(np.ascontiguousarray(inverse_np.T))
    own_cycles = lax.dynamic_slice_in_dim(cycle_table, position * ROWS, ROWS)
    dft = 2 * ROWS * 256 * NLON * CH
    leg = 2 * 16 * 128 * 128 * CH
    mlp = 2 * ROWS * NLON * CH * HID

    saved_blocks = call(
        saved_coeffs_kernel,
        [BLOCKS],
        [saved, forward_t],
        (
            pltpu.VMEM((ROWS, NLON, CH), BF16),
            pltpu.VMEM((256, NLON), BF16),
            pltpu.SemaphoreType.DMA((ROWS + 1,)),
        ),
        flops=dft,
        hbm=(0, 1),
        limit=60 * 1024 * 1024,
    )[0]
    saved_at_orders = exchange(saved_blocks, SP)
    kept = [inverse, inverse_t, expand, contract]
    fresh_own, fresh_lent, inverse, inverse_t, expand, contract = call(
        fresh_coeffs_kernel,
        [OWN, LENT] + [jax.ShapeDtypeStruct(k.shape, BF16) for k in kept],
        [fresh, fresh_forward_t, *kept],
        [pltpu.VMEM((LANES * 8, CH), F32)],
        flops=dft,
    )
    fresh_blocks = jnp.where(last, jnp.concatenate(to_last(fresh_lent), axis=1), fresh_own)

    lat_live = (cycle_table < NLAT).astype(F32)
    colatitude = math.pi * (jnp.minimum(cycle_table, NLAT - 1).astype(F32) + 0.5) / NLAT
    sine = jnp.sin(colatitude)
    geo = jnp.stack(
        [jnp.cos(colatitude), jnp.log(sine), math.pi / NLAT * sine * lat_live, lat_live]
    )
    order_rows = lax.dynamic_index_in_dim(jnp.asarray(orders_np), position, 0, keepdims=False)
    tables = jax.ShapeDtypeStruct((ROWS, LANES, LANES), BF16)
    ana, syn = call(
        tables_kernel,
        [tables, tables],
        [geo, order_rows],
        [pltpu.VMEM((LANES * 8, LANES), F32)],
        flops=4_000_000,
    )

    spectra_shape = jax.ShapeDtypeStruct((ROWS, LANES, 2 * CH), F32)
    values_fresh, spectra = call(
        saved_spectral_kernel,
        [PAIRED, spectra_shape],
        [saved_at_orders, ana, syn, filt, fresh_blocks],
        SPECTRAL_SCRATCH,
        flops=leg,
    )
    lent_filt, values_fresh = lax.optimization_barrier((filt, values_fresh))
    lent_filters = to_last(lent_filt)
    values_fresh = exchange(values_fresh, SP)

    narrow = pltpu.VMEM((ROWS * NLON, CH), BF16)
    wide = pltpu.VMEM((ROWS * NLON, HID), BF16)
    grad_values, grad_mixed, shares = call(
        mlp_back_kernel,
        [
            BLOCKS,
            jax.ShapeDtypeStruct((ROWS, NLON, CH), F32),
            jax.ShapeDtypeStruct((2, 4, HID // 4, CH), BF16),
        ],
        [saved, values_fresh, cotangent, inverse, inverse_t, expand, contract, own_cycles],
        [narrow, narrow, wide, wide],
        flops=5 * mlp + 2 * dft,
        transcendentals=2 * ROWS * NLON * HID,
        smem=(7,),
    )
    grads_fresh = call(
        fresh_spectral_kernel,
        [PAIRED],
        [
            values_fresh,
            ana,
            syn,
            filt,
            *lent_filters,
            last.astype(jnp.int32)[None],
            grad_values,
        ],
        SPECTRAL_SCRATCH,
        flops=leg,
        smem=(7,),
    )[0]
    grads_fresh = exchange(grads_fresh, SP)
    share_blocks = share_blocks_of(shares)

    lent_values = [
        lax.ppermute(grads_fresh[:, 32 + 8 * p : 40 + 8 * p], "pipe", [(3, p)]) for p in range(3)
    ]
    block = call(
        mlp_kernel,
        [TOKENS],
        [fresh, grads_fresh, *lent_values, fresh_inverse, expand, contract, own_cycles],
        [pltpu.VMEM((LANES * 8, CH), F32)],
        flops=2 * mlp + dft,
        transcendentals=ROWS * NLON * HID,
        smem=(8,),
    )[0]
    next_input = from_behind(block, "pipe", 1)
    coeffs_summed = call(
        spectral_back_kernel,
        [SUMMED],
        [grads_fresh, spectra, ana, syn, filt, share_blocks],
        SPECTRAL_SCRATCH,
        flops=leg,
    )[0]
    coeffs_summed = exchange(coeffs_summed, SP)
    coeffs_summed, next_input = lax.optimization_barrier((coeffs_summed, next_input))
    pieces = call(
        piece_kernel, [jax.ShapeDtypeStruct((PEERS // 2, 24, CH), BF16)], [coeffs_summed]
    )[0]
    pieces = exchange(pieces, "sp_0")
    filter_rows = call(
        filter_rows_kernel, [jax.ShapeDtypeStruct((8, 128, CH), BF16)], [pieces]
    )[0]
    filter_rows = exchange(filter_rows, ("sp_1", "dp"))
    other_pieces = lax.ppermute(pieces, "sp_1", CORE_SWAP)
    input_grad = call(
        input_grad_kernel,
        [TOKENS],
        [coeffs_summed, grad_mixed, forward, own_cycles],
        flops=dft,
        smem=(3,),
    )[0]
    sent_back = from_behind(input_grad, "pipe", -1)
    part = jax.ShapeDtypeStruct((HID // 4, CH), F32)
    core = lax.axis_index("sp_1").astype(jnp.int32)[None]
    expand_grad, reduce_grad, filter_grad, next_input, sent_back = call(
        result_kernel,
        [part, part, jax.ShapeDtypeStruct((2, NLAT, CH), F32), TOKENS, TOKENS],
        [pieces, other_pieces, filter_rows, core, next_input, sent_back],
        smem=(3,),
    )
    return (
        next_input[None, None],
        sent_back[None, None],
        expand_grad.T[None],
        reduce_grad[None],
        filter_grad[None],
    )


def solution(mesh):
    finer = Mesh(
        mesh.devices.reshape(mesh.shape["pipe"], 16, 2, mesh.shape["dp"]),
        ("pipe", "sp_0", "sp_1", "dp"),
    )
    in_specs = (
        P("pipe", "dp", SP, None, None),
        P("pipe", "dp", SP, None, None),
        P("pipe", "dp", SP, None, None),
        P("pipe", None, None),
        P("pipe", None, None),
        P("pipe", None, None, None),
        P(),
    )
    out_specs = (
        P("pipe", "dp", SP, None, None),
        P("pipe", "dp", SP, None, None),
        P("pipe", None, "dp"),
        P("pipe", "dp", None),
        P("pipe", None, None, None),
    )
    program = functools.partial(on_device, fourier_constants(), order_constants())
    return jax.shard_map(
        program, mesh=finer, in_specs=in_specs, out_specs=out_specs, check_vma=False
    )
```

```python
import functools
import math

import jax
import jax.numpy as jnp
import numpy as np
from jax import lax
from jax.experimental import pallas as pl
from jax.experimental.pallas import tpu as pltpu
from jax.sharding import Mesh
from jax.sharding import PartitionSpec as P

NLAT = 120
NLON = 240
CH = 128
HID = 768
ROWS = 4
PEERS = 32
VMEM_LIMIT = 16 * 1024 * 1024
LANES = 128
SP = ("sp_0", "sp_1")

ROOT_HALF = 0.7071067811865476
INV_ROOT_TAU = 0.3989422804014327
F32 = jnp.float32
BF16 = jnp.bfloat16


def fourier_constants():
    order = np.arange(128)
    live = (order < NLAT).astype(np.float64)
    value = np.minimum(order, NLAT - 1)
    phase = 2.0 * math.pi / NLON * ((np.arange(NLON)[:, None] * value[None, :]) % NLON)
    scaled = live * (2.0 * math.pi / NLON)
    forward = np.stack([np.cos(phase) * scaled, -np.sin(phase) * scaled], axis=1)
    factor = np.where(value == 0, 1.0, 2.0) * live / (2.0 * math.pi)
    inverse = np.stack([np.cos(phase) * factor, -np.sin(phase) * factor], axis=1)

    def arranged(table, places):
        table = table.reshape(NLON, 2, PEERS, ROWS).transpose(0, *places)
        return table.reshape(NLON, 256).astype(np.float32).astype(jnp.bfloat16)

    saved, fresh = (2, 1, 3), (3, 1, 2)
    return [arranged(table, places) for places in (saved, fresh) for table in (forward, inverse)]


def order_constants():
    table = np.zeros((PEERS, 3, 8, LANES), np.float32)
    for position in range(PEERS):
        for row in range(8):
            slot = position * ROWS + row % ROWS
            m = min(slot, NLAT - 1)
            log_start = 0.5 * (
                math.log((2.0 * m + 1.0) / (4.0 * math.pi))
                + math.lgamma(2.0 * m + 1.0)
                - 2.0 * math.lgamma(m + 1.0)
                - m * math.log(4.0)
            )
            table[position, 0, row] = m
            table[position, 1, row] = log_start
            table[position, 2, row] = float(slot < NLAT)
    return table


def tables_kernel(geo_ref, order_ref, ana_ref, syn_ref, work_ref):
    shape = (8, LANES)
    cosine = jnp.broadcast_to(geo_ref[0:1, :], shape)
    log_sine = jnp.broadcast_to(geo_ref[1:2, :], shape)
    weight = geo_ref[2:3, :]
    m = order_ref[0]
    keep = order_ref[2] * jnp.broadcast_to(geo_ref[3:4, :], shape)
    starting = jnp.exp(order_ref[1] + m * log_sine)
    squares = m * m
    previous = jnp.zeros(shape, F32)
    earlier = previous
    for degree in range(NLAT):
        upper = max(4.0 * degree * degree - 1.0, 0.0)
        lower = max(4.0 * (degree - 1.0) ** 2 - 1.0, 1.0)
        ratio_main = jnp.sqrt(upper / jnp.maximum(float(degree * degree) - squares, 1.0))
        ratio_back = jnp.sqrt(jnp.maximum((degree - 1.0) ** 2 - squares, 0.0) / lower)
        rising = ratio_main * (cosine * previous - ratio_back * earlier)
        current = jnp.where(m == float(degree), starting, jnp.where(m < float(degree), rising, 0.0))
        work_ref[degree * 8 : degree * 8 + 8, :] = current * keep
        previous, earlier = current, previous
    work_ref[NLAT * 8 :, :] = jnp.zeros((LANES * 8 - NLAT * 8, LANES), F32)
    for t in range(ROWS):
        table = work_ref[pl.ds(t, LANES, stride=8), :]
        syn_ref[t] = table.astype(BF16)
        ana_ref[t] = (table * weight).astype(BF16)


def to_blocks(out_ref, half, pair):
    blocks = [part.reshape(PEERS, 8, CH) for part in pair]
    out_ref[:, 16 * half : 16 * half + 16, :] = jnp.concatenate(blocks, axis=1).astype(BF16)


def from_blocks(block_ref, half):
    pair = block_ref[:, 16 * half : 16 * half + 16, :].astype(F32)
    return [pair[:, 8 * h : 8 * h + 8].reshape(256, CH).astype(BF16) for h in range(2)]


def matmul(left, right, dims=((1,), (0,))):
    return lax.dot_general(left, right, (dims, ((), ())), preferred_element_type=F32)


def fetch(source, target, sem):
    copy = pltpu.make_async_copy(source, target, sem)
    copy.start()
    return copy


def saved_coeffs_kernel(x_hbm, forward_hbm, out_ref, x_ref, forward_ref, sems):
    table = fetch(forward_hbm, forward_ref, sems.at[ROWS])
    cycles = [fetch(x_hbm.at[j], x_ref.at[j], sems.at[j]) for j in range(ROWS)]
    table.wait()
    for half in range(2):
        cycles[2 * half].wait()
        cycles[2 * half + 1].wait()
        to_blocks(out_ref, half, [matmul(forward_ref[...], x_ref[2 * half + h]) for h in range(2)])


def fresh_coeffs_kernel(x_ref, forward_ref, *rest):
    *sources, own_ref, lent_ref, packed_ref, work_ref = rest
    row = 0
    for source in sources:
        rows, columns = source.shape
        for start in range(0, columns, CH):
            width = min(CH, columns - start)
            packed_ref[row : row + rows, :width] = source[:, start : start + width]
            row += rows
    for j in range(ROWS):
        coeffs = matmul(forward_ref[...], x_ref[j])
        for place in range(8):
            target = pl.ds(place // 2 * 256 + j * 2 + place % 2, PEERS, stride=8)
            work_ref[target, :] = coeffs[place * PEERS : (place + 1) * PEERS]
    groups = [work_ref[256 * u : 256 * u + 256, :].reshape(PEERS, 8, CH) for u in range(ROWS)]
    own_ref[...] = jnp.concatenate(groups[:3], axis=1).astype(BF16)
    lent_ref[...] = groups[3].astype(BF16)


def padded_filter(filt_ref):
    rest = jnp.zeros((LANES - NLAT, CH), F32)
    return [jnp.concatenate([filt_ref[part], rest], axis=0) for part in range(2)]


def filter_step(spectra, real, imag):
    first, second = spectra[:, :CH], spectra[:, CH:]
    return jnp.concatenate(
        [real * first - imag * second, real * second + imag * first], axis=1
    ).astype(BF16)


def spectral(came_ref, goes_ref, ana_ref, syn_ref, filt_ref, spectra_ref):
    real, imag = padded_filter(filt_ref)
    for t in range(ROWS):
        parts = [came_ref[pl.ds(r * ROWS + t, LANES, stride=8), :] for r in range(2)]
        spectra = matmul(ana_ref[t], jnp.concatenate(parts, axis=1).astype(BF16))
        spectra_ref[t] = spectra
        values = matmul(syn_ref[t], filter_step(spectra, real, imag), ((0,), (0,)))
        for r in range(2):
            goes_ref[pl.ds(r * ROWS + t, LANES, stride=8), :] = values[:, r * CH : (r + 1) * CH]


def saved_spectral_kernel(
    arrived_ref, ana_ref, syn_ref, filt_ref, beside_ref, out_ref, spectra_ref, came_ref, goes_ref
):
    out_ref[:, 32:, :] = beside_ref[...]
    came_ref[...] = arrived_ref[...].reshape(LANES * 8, CH).astype(F32)
    spectral(came_ref, goes_ref, ana_ref, syn_ref, filt_ref, spectra_ref)
    out_ref[:, :32, :] = goes_ref[...].reshape(PEERS, 32, CH).astype(BF16)


def fresh_spectral_kernel(
    arrived_ref,
    ana_ref,
    syn_ref,
    filt_ref,
    lent_a_ref,
    lent_b_ref,
    lent_c_ref,
    last_ref,
    beside_ref,
    out_ref,
    came_ref,
    goes_ref,
):
    out_ref[:, :32, :] = beside_ref[...]
    came = arrived_ref[:, 32:, :].astype(F32)
    last = last_ref[0]
    own = padded_filter(filt_ref)
    for u, lent_ref in enumerate((lent_a_ref, lent_b_ref, lent_c_ref)):
        came_ref[256 * u : 256 * u + 256, :] = came[:, 8 * u : 8 * u + 8].reshape(256, CH)
        lent = padded_filter(lent_ref)
        real, imag = [jnp.where(last == 1, lent[part], own[part]) for part in range(2)]
        t = jnp.where(last == 1, 3, u)
        parts = [came_ref[pl.ds(256 * u + r, LANES, stride=2), :] for r in range(2)]
        spectra = matmul(ana_ref[t], jnp.concatenate(parts, axis=1).astype(BF16))
        values = matmul(syn_ref[t], filter_step(spectra, real, imag), ((0,), (0,)))
        for r in range(2):
            goes_ref[pl.ds(256 * u + r, LANES, stride=2), :] = values[:, r * CH : (r + 1) * CH]
    groups = [goes_ref[256 * u : 256 * u + 256, :].reshape(PEERS, 8, CH) for u in range(3)]
    out_ref[:, 32:, :] = jnp.concatenate(groups, axis=1).astype(BF16)


def spectral_back_kernel(
    arrived_ref,
    spectra_ref,
    ana_ref,
    syn_ref,
    filt_ref,
    shares_ref,
    out_ref,
    came_ref,
    goes_ref,
):
    came_ref[...] = arrived_ref[:, :32, :].reshape(LANES * 8, CH).astype(F32)
    real, imag = padded_filter(filt_ref)
    total_real = jnp.zeros((LANES, CH), F32)
    total_imag = jnp.zeros((LANES, CH), F32)
    for t in range(ROWS):
        parts = [came_ref[pl.ds(r * ROWS + t, LANES, stride=8), :] for r in range(2)]
        grads = matmul(syn_ref[t], jnp.concatenate(parts, axis=1).astype(BF16))
        first, second = grads[:, :CH], grads[:, CH:]
        spectra = spectra_ref[t]
        s_first, s_second = spectra[:, :CH], spectra[:, CH:]
        total_real = total_real + (first * s_first + second * s_second)
        total_imag = total_imag + (second * s_first - first * s_second)
        grad_spectra = jnp.concatenate(
            [real * first + imag * second, real * second - imag * first], axis=1
        ).astype(BF16)
        coeffs = matmul(ana_ref[t], grad_spectra, ((0,), (0,)))
        for r in range(2):
            goes_ref[pl.ds(r * ROWS + t, LANES, stride=8), :] = coeffs[:, r * CH : (r + 1) * CH]
    out_ref[:, :32, :] = goes_ref[...].reshape(PEERS, 32, CH).astype(BF16)
    filter_part = jnp.concatenate([total_real, total_imag], axis=0).reshape(PEERS, 8, CH)
    sums = jnp.concatenate([shares_ref[...].astype(F32), filter_part], axis=1)
    out_ref[:, 32:, :] = sums.astype(BF16)


PLACES = {}
for _name, _rows, _columns in (
    ("contract", HID, CH),
    ("expand", CH, HID),
    ("inverse", NLON, 256),
    ("fresh_inverse", NLON, 256),
    ("inverse_t", 256, NLON),
):
    PLACES[_name] = (sum(r * -(-c // CH) for _, r, c in PLACES.values()), _rows, _columns)
PACKED_ROWS = sum(r * -(-c // CH) for _, r, c in PLACES.values())


def unpacked(packed_ref, name):
    row, rows, columns = PLACES[name]
    blocks = [
        packed_ref[row + n * rows : row + (n + 1) * rows, :] for n in range(-(-columns // CH))
    ]
    return jnp.concatenate(blocks, axis=1)[:, :columns] if len(blocks) > 1 else blocks[0]


def live(cycle_ref, j):
    return jnp.where(cycle_ref[j] < NLAT, 1.0, 0.0).astype(F32)


def mlp_kernel(
    x_ref,
    values_ref,
    lent_a_ref,
    lent_b_ref,
    lent_c_ref,
    packed_ref,
    cycle_ref,
    out_ref,
    work_ref,
):
    names = ("fresh_inverse", "expand", "contract")
    inverse, expand, contract = [unpacked(packed_ref, name) for name in names]
    own = values_ref[:, 32:, :].astype(F32)
    lent = [ref[...].astype(F32) for ref in (lent_a_ref, lent_b_ref, lent_c_ref)]
    for u in range(3):
        work_ref[256 * u : 256 * u + 256, :] = own[:, 8 * u : 8 * u + 8].reshape(256, CH)
    work_ref[768:, :] = (lent[0] + lent[1] + lent[2]).reshape(256, CH)
    for j in range(ROWS):
        parts = [
            work_ref[pl.ds(place // 2 * 256 + j * 2 + place % 2, PEERS, stride=8), :]
            for place in range(8)
        ]
        values = jnp.concatenate(parts, axis=0).astype(BF16)
        mixed = x_ref[j].astype(F32) + matmul(inverse, values)
        pre = matmul(mixed.astype(BF16), expand)
        hidden = (0.5 * pre * (1.0 + lax.erf(pre * ROOT_HALF))).astype(BF16)
        result = mixed + matmul(hidden, contract)
        out_ref[j] = (result * live(cycle_ref, j)).astype(BF16)


def mlp_back_kernel(
    x_ref,
    values_ref,
    cotangent_ref,
    packed_ref,
    cycle_ref,
    out_ref,
    grad_mixed_ref,
    shares_ref,
    mixed_ref,
    masked_ref,
    hidden_ref,
    grad_pre_ref,
):
    names = ("inverse", "inverse_t", "expand", "contract")
    inverse, inverse_t, expand, contract = [unpacked(packed_ref, name) for name in names]
    for half in range(2):
        values = from_blocks(values_ref, half)
        grad_values = []
        for h in range(2):
            j = 2 * half + h
            rows = slice(j * NLON, (j + 1) * NLON)
            mixed = x_ref[j].astype(F32) + matmul(inverse, values[h])
            mixed_b = mixed.astype(BF16)
            masked_f = cotangent_ref[j].astype(F32) * live(cycle_ref, j)
            masked = masked_f.astype(BF16)
            mixed_ref[rows, :] = mixed_b
            masked_ref[rows, :] = masked
            pre = matmul(mixed_b, expand)
            normal = 0.5 * (1.0 + lax.erf(pre * ROOT_HALF))
            hidden_ref[rows, :] = (pre * normal).astype(BF16)
            slope = normal + pre * jnp.exp(-0.5 * pre * pre) * INV_ROOT_TAU
            grad_hidden = matmul(masked, contract, ((1,), (1,)))
            grad_pre = (grad_hidden * slope).astype(BF16)
            grad_pre_ref[rows, :] = grad_pre
            grad_mixed = masked_f + matmul(grad_pre, expand, ((1,), (1,)))
            grad_mixed_ref[j] = grad_mixed
            grad_values.append(matmul(inverse_t, grad_mixed.astype(BF16)))
        to_blocks(out_ref, half, grad_values)
    quarter = HID // 4
    pairs = ((grad_pre_ref, mixed_ref), (hidden_ref, masked_ref))
    for side, (wide_ref, narrow_ref) in enumerate(pairs):
        grad = matmul(wide_ref[...], narrow_ref[...], ((0,), (0,))).astype(BF16)
        for d in range(4):
            shares_ref[side, d] = grad[d * quarter : (d + 1) * quarter]


def input_grad_kernel(coeffs_ref, grad_mixed_ref, forward_ref, cycle_ref, out_ref):
    for half in range(2):
        values = from_blocks(coeffs_ref, half)
        for h in range(2):
            j = 2 * half + h
            total = grad_mixed_ref[j] + matmul(forward_ref[...], values[h])
            out_ref[j] = (total * live(cycle_ref, j)).astype(BF16)


def piece_kernel(arrived_ref, out_ref):
    came = arrived_ref[:, 32:, :].astype(F32).reshape(PEERS // 2, 2, 16, CH)
    sums = came.sum(axis=0)
    piece = jnp.concatenate([sums[0, :8], sums[1, :8], sums[0, 8:] + sums[1, 8:]], axis=0)
    out_ref[...] = jnp.broadcast_to(piece[None], out_ref.shape).astype(BF16)


def filter_rows_kernel(pieces_ref, out_ref):
    rows = pieces_ref[...].astype(F32)[:, 16:].reshape(128, CH).astype(BF16)
    out_ref[...] = jnp.broadcast_to(rows[None], out_ref.shape)


def result_kernel(
    pieces_ref,
    other_ref,
    filter_rows_ref,
    core_ref,
    next_ref,
    back_ref,
    expand_ref,
    reduce_ref,
    filter_ref,
    next_out_ref,
    back_out_ref,
):
    next_out_ref[...] = next_ref[...]
    back_out_ref[...] = back_ref[...]
    first = core_ref[0] == 0
    filters = [filter_rows_ref[4 * c : 4 * c + 4].astype(F32).sum(axis=0) for c in range(2)]
    for p in range(PEERS):
        mine, other = pieces_ref[p // 2].astype(F32), other_ref[p // 2].astype(F32)
        piece = jnp.where(first, mine, other) if p % 2 == 0 else jnp.where(first, other, mine)
        expand_ref[p * 6 : p * 6 + 6, :] = piece[:6]
        reduce_ref[p * 6 : p * 6 + 6, :] = piece[8:14]
        side, at = divmod(p, PEERS // 2)
        if at < NLAT // 8:
            rows = filters[p % 2][p // 2 * 8 : p // 2 * 8 + 8]
            filter_ref[side, at * 8 : at * 8 + 8, :] = rows


def call(
    kernel, outs, args, scratch=(), flops=0, transcendentals=0, smem=(), hbm=(), limit=VMEM_LIMIT
):
    places = {n: pltpu.SMEM for n in smem} | {n: pl.ANY for n in hbm}
    specs = [pl.BlockSpec(memory_space=places.get(n, pltpu.VMEM)) for n in range(len(args))]
    moved = sum(a.size * a.dtype.itemsize for a in (*args, *outs))
    return pl.pallas_call(
        kernel,
        out_shape=outs,
        in_specs=specs,
        out_specs=[pl.BlockSpec(memory_space=pltpu.VMEM)] * len(outs),
        scratch_shapes=list(scratch),
        compiler_params=pltpu.CompilerParams(vmem_limit_bytes=limit),
        cost_estimate=pl.CostEstimate(
            flops=flops, bytes_accessed=moved, transcendentals=transcendentals
        ),
    )(*args)


PAIRED = jax.ShapeDtypeStruct((PEERS, 56, CH), BF16)
OWN = jax.ShapeDtypeStruct((PEERS, 24, CH), BF16)
LENT = jax.ShapeDtypeStruct((PEERS, 8, CH), BF16)
SUMMED = jax.ShapeDtypeStruct((PEERS, 48, CH), BF16)
BLOCKS = jax.ShapeDtypeStruct((PEERS, 32, CH), BF16)
TOKENS = jax.ShapeDtypeStruct((ROWS, NLON, CH), BF16)
SPECTRAL_SCRATCH = (pltpu.VMEM((LANES * 8, CH), F32), pltpu.VMEM((LANES * 8, CH), F32))


CORE_SWAP = [(0, 1), (1, 0)]


def exchange(blocks, axes):
    return lax.all_to_all(blocks, axes, split_axis=0, concat_axis=0, tiled=True)


def from_behind(block, axis, distance):
    devices = range(lax.axis_size(axis))
    route = [(i - distance, i) for i in devices if i - distance in devices]
    return lax.ppermute(block, axis, route)


def to_last(block):
    return [lax.ppermute(block, "pipe", [(p, 3)]) for p in range(3)]


def halved(blocks, axis, route, kept):
    mine = lax.dynamic_index_in_dim(blocks, kept, 0, keepdims=False)
    sent = lax.dynamic_index_in_dim(blocks, 1 - kept, 0, keepdims=False)
    came = lax.ppermute(sent, axis, route)
    return (mine.astype(F32) + came.astype(F32)).astype(BF16)


def around(block, axis, distance):
    count = lax.axis_size(axis)
    return lax.ppermute(block, axis, [(i, (i + distance) % count) for i in range(count)])


def scattered_total(blocks, axis):
    count = lax.axis_size(axis)
    me = lax.axis_index(axis)

    def block_of(distance):
        return lax.dynamic_index_in_dim(blocks, (me + distance) % count, 0, keepdims=False)

    came = [around(block_of(k), axis, k) for k in range(1, count)]
    return sum((block.astype(F32) for block in came), block_of(0).astype(F32))


def share_blocks_of(shares):
    kept = halved(shares, "sp_1", CORE_SWAP, lax.axis_index("sp_1"))
    kept = scattered_total(kept, "dp").astype(BF16)
    return jnp.pad(kept.reshape(PEERS, 6, CH), ((0, 0), (0, 2), (0, 0)))


def on_device(
    tables_np,
    orders_np,
    fresh_input,
    saved_input,
    output_grad,
    expand_weight,
    reduce_weight,
    filter_weight,
    cycle_table,
):
    position = lax.axis_index(SP)
    fresh, saved, cotangent = fresh_input[0, 0], saved_input[0, 0], output_grad[0, 0]
    expand, contract, filt = expand_weight[0], reduce_weight[0], filter_weight[0]
    forward_np, inverse_np, fresh_forward_np, fresh_inverse_np = tables_np
    forward = jnp.asarray(forward_np)
    fresh_forward_t = jnp.asarray(np.ascontiguousarray(fresh_forward_np.T))
    fresh_inverse = jnp.asarray(fresh_inverse_np)
    last = lax.axis_index("pipe") == 3
    forward_t = jnp.asarray(np.ascontiguousarray(forward_np.T))
    inverse = jnp.asarray(inverse_np)
    inverse_t = jnp.asarray(np.ascontiguousarray(inverse_np.T))
    own_cycles = lax.dynamic_slice_in_dim(cycle_table, position * ROWS, ROWS)
    dft = 2 * ROWS * 256 * NLON * CH
    leg = 2 * 16 * 128 * 128 * CH
    mlp = 2 * ROWS * NLON * CH * HID

    saved_blocks = call(
        saved_coeffs_kernel,
        [BLOCKS],
        [saved, forward_t],
        (
            pltpu.VMEM((ROWS, NLON, CH), BF16),
            pltpu.VMEM((256, NLON), BF16),
            pltpu.SemaphoreType.DMA((ROWS + 1,)),
        ),
        flops=dft,
        hbm=(0, 1),
        limit=60 * 1024 * 1024,
    )[0]
    saved_at_orders = exchange(saved_blocks, SP)
    kept = [contract, expand, inverse, fresh_inverse, inverse_t]
    fresh_own, fresh_lent, packed = call(
        fresh_coeffs_kernel,
        [OWN, LENT, jax.ShapeDtypeStruct((PACKED_ROWS, CH), BF16)],
        [fresh, fresh_forward_t, *kept],
        [pltpu.VMEM((LANES * 8, CH), F32)],
        flops=dft,
    )
    fresh_blocks = jnp.where(last, jnp.concatenate(to_last(fresh_lent), axis=1), fresh_own)

    lat_live = (cycle_table < NLAT).astype(F32)
    colatitude = math.pi * (jnp.minimum(cycle_table, NLAT - 1).astype(F32) + 0.5) / NLAT
    sine = jnp.sin(colatitude)
    geo = jnp.stack(
        [jnp.cos(colatitude), jnp.log(sine), math.pi / NLAT * sine * lat_live, lat_live]
    )
    order_rows = lax.dynamic_index_in_dim(jnp.asarray(orders_np), position, 0, keepdims=False)
    tables = jax.ShapeDtypeStruct((ROWS, LANES, LANES), BF16)
    ana, syn = call(
        tables_kernel,
        [tables, tables],
        [geo, order_rows],
        [pltpu.VMEM((LANES * 8, LANES), F32)],
        flops=4_000_000,
    )

    spectra_shape = jax.ShapeDtypeStruct((ROWS, LANES, 2 * CH), F32)
    values_fresh, spectra = call(
        saved_spectral_kernel,
        [PAIRED, spectra_shape],
        [saved_at_orders, ana, syn, filt, fresh_blocks],
        SPECTRAL_SCRATCH,
        flops=leg,
    )
    lent_filt, values_fresh = lax.optimization_barrier((filt, values_fresh))
    lent_filters = to_last(lent_filt)
    values_fresh = exchange(values_fresh, SP)

    narrow = pltpu.VMEM((ROWS * NLON, CH), BF16)
    wide = pltpu.VMEM((ROWS * NLON, HID), BF16)
    grad_values, grad_mixed, shares = call(
        mlp_back_kernel,
        [
            BLOCKS,
            jax.ShapeDtypeStruct((ROWS, NLON, CH), F32),
            jax.ShapeDtypeStruct((2, 4, HID // 4, CH), BF16),
        ],
        [saved, values_fresh, cotangent, packed, own_cycles],
        [narrow, narrow, wide, wide],
        flops=5 * mlp + 2 * dft,
        transcendentals=2 * ROWS * NLON * HID,
        smem=(4,),
    )
    grads_fresh = call(
        fresh_spectral_kernel,
        [PAIRED],
        [
            values_fresh,
            ana,
            syn,
            filt,
            *lent_filters,
            last.astype(jnp.int32)[None],
            grad_values,
        ],
        SPECTRAL_SCRATCH,
        flops=leg,
        smem=(7,),
    )[0]
    grads_fresh = exchange(grads_fresh, SP)
    share_blocks = share_blocks_of(shares)

    lent_values = [
        lax.ppermute(grads_fresh[:, 32 + 8 * p : 40 + 8 * p], "pipe", [(3, p)]) for p in range(3)
    ]
    block = call(
        mlp_kernel,
        [TOKENS],
        [fresh, grads_fresh, *lent_values, packed, own_cycles],
        [pltpu.VMEM((LANES * 8, CH), F32)],
        flops=2 * mlp + dft,
        transcendentals=ROWS * NLON * HID,
        smem=(6,),
    )[0]
    next_input = from_behind(block, "pipe", 1)
    coeffs_summed = call(
        spectral_back_kernel,
        [SUMMED],
        [grads_fresh, spectra, ana, syn, filt, share_blocks],
        SPECTRAL_SCRATCH,
        flops=leg,
    )[0]
    coeffs_summed = exchange(coeffs_summed, SP)
    coeffs_summed, _ = lax.optimization_barrier((coeffs_summed, block))
    pieces = call(
        piece_kernel, [jax.ShapeDtypeStruct((PEERS // 2, 24, CH), BF16)], [coeffs_summed]
    )[0]
    pieces = exchange(pieces, "sp_0")
    filter_rows = call(
        filter_rows_kernel, [jax.ShapeDtypeStruct((8, 128, CH), BF16)], [pieces]
    )[0]
    filter_rows = exchange(filter_rows, ("sp_1", "dp"))
    other_pieces = lax.ppermute(pieces, "sp_1", CORE_SWAP)
    input_grad = call(
        input_grad_kernel,
        [TOKENS],
        [coeffs_summed, grad_mixed, forward, own_cycles],
        flops=dft,
        smem=(3,),
    )[0]
    sent_back = from_behind(input_grad, "pipe", -1)
    part = jax.ShapeDtypeStruct((HID // 4, CH), F32)
    core = lax.axis_index("sp_1").astype(jnp.int32)[None]
    expand_grad, reduce_grad, filter_grad, next_input, sent_back = call(
        result_kernel,
        [part, part, jax.ShapeDtypeStruct((2, NLAT, CH), F32), TOKENS, TOKENS],
        [pieces, other_pieces, filter_rows, core, next_input, sent_back],
        smem=(3,),
    )
    return (
        next_input[None, None],
        sent_back[None, None],
        expand_grad.T[None],
        reduce_grad[None],
        filter_grad[None],
    )


def solution(mesh):
    finer = Mesh(
        mesh.devices.reshape(mesh.shape["pipe"], 16, 2, mesh.shape["dp"]),
        ("pipe", "sp_0", "sp_1", "dp"),
    )
    in_specs = (
        P("pipe", "dp", SP, None, None),
        P("pipe", "dp", SP, None, None),
        P("pipe", "dp", SP, None, None),
        P("pipe", None, None),
        P("pipe", None, None),
        P("pipe", None, None, None),
        P(),
    )
    out_specs = (
        P("pipe", "dp", SP, None, None),
        P("pipe", "dp", SP, None, None),
        P("pipe", None, "dp"),
        P("pipe", "dp", None),
        P("pipe", None, None, None),
    )
    program = functools.partial(on_device, fourier_constants(), order_constants())
    return jax.shard_map(
        program, mesh=finer, in_specs=in_specs, out_specs=out_specs, check_vma=False
    )
```

```python
import functools
import math

import jax
import jax.numpy as jnp
import numpy as np
from jax import lax
from jax.experimental import pallas as pl
from jax.experimental.pallas import tpu as pltpu
from jax.sharding import Mesh
from jax.sharding import PartitionSpec as P

NLAT = 120
NLON = 240
CH = 128
HID = 768
ROWS = 4
PEERS = 32
VMEM_LIMIT = 16 * 1024 * 1024
LANES = 128
SP = ("sp_0", "sp_1")

ROOT_HALF = 0.7071067811865476
INV_ROOT_TAU = 0.3989422804014327
F32 = jnp.float32
BF16 = jnp.bfloat16


def fourier_constants():
    order = np.arange(128)
    live = (order < NLAT).astype(np.float64)
    value = np.minimum(order, NLAT - 1)
    phase = 2.0 * math.pi / NLON * ((np.arange(NLON)[:, None] * value[None, :]) % NLON)
    scaled = live * (2.0 * math.pi / NLON)
    forward = np.stack([np.cos(phase) * scaled, -np.sin(phase) * scaled], axis=1)
    factor = np.where(value == 0, 1.0, 2.0) * live / (2.0 * math.pi)
    inverse = np.stack([np.cos(phase) * factor, -np.sin(phase) * factor], axis=1)

    def arranged(table, places):
        table = table.reshape(NLON, 2, PEERS, ROWS).transpose(0, *places)
        return table.reshape(NLON, 256).astype(np.float32).astype(jnp.bfloat16)

    saved, fresh = (2, 1, 3), (3, 1, 2)
    return [arranged(table, places) for places in (saved, fresh) for table in (forward, inverse)]


def order_constants():
    table = np.zeros((PEERS, 3, 8, LANES), np.float32)
    for position in range(PEERS):
        for row in range(8):
            slot = position * ROWS + row % ROWS
            m = min(slot, NLAT - 1)
            log_start = 0.5 * (
                math.log((2.0 * m + 1.0) / (4.0 * math.pi))
                + math.lgamma(2.0 * m + 1.0)
                - 2.0 * math.lgamma(m + 1.0)
                - m * math.log(4.0)
            )
            table[position, 0, row] = m
            table[position, 1, row] = log_start
            table[position, 2, row] = float(slot < NLAT)
    return table


def tables_kernel(geo_ref, order_ref, ana_ref, syn_ref, work_ref):
    shape = (8, LANES)
    cosine = jnp.broadcast_to(geo_ref[0:1, :], shape)
    log_sine = jnp.broadcast_to(geo_ref[1:2, :], shape)
    weight = geo_ref[2:3, :]
    m = order_ref[0]
    keep = order_ref[2] * jnp.broadcast_to(geo_ref[3:4, :], shape)
    starting = jnp.exp(order_ref[1] + m * log_sine)
    squares = m * m
    previous = jnp.zeros(shape, F32)
    earlier = previous
    for degree in range(NLAT):
        upper = max(4.0 * degree * degree - 1.0, 0.0)
        lower = max(4.0 * (degree - 1.0) ** 2 - 1.0, 1.0)
        ratio_main = jnp.sqrt(upper / jnp.maximum(float(degree * degree) - squares, 1.0))
        ratio_back = jnp.sqrt(jnp.maximum((degree - 1.0) ** 2 - squares, 0.0) / lower)
        rising = ratio_main * (cosine * previous - ratio_back * earlier)
        current = jnp.where(m == float(degree), starting, jnp.where(m < float(degree), rising, 0.0))
        work_ref[degree * 8 : degree * 8 + 8, :] = current * keep
        previous, earlier = current, previous
    work_ref[NLAT * 8 :, :] = jnp.zeros((LANES * 8 - NLAT * 8, LANES), F32)
    for t in range(ROWS):
        table = work_ref[pl.ds(t, LANES, stride=8), :]
        syn_ref[t] = table.astype(BF16)
        ana_ref[t] = (table * weight).astype(BF16)


def to_blocks(out_ref, half, pair):
    blocks = [part.reshape(PEERS, 8, CH) for part in pair]
    out_ref[:, 16 * half : 16 * half + 16, :] = jnp.concatenate(blocks, axis=1).astype(BF16)


def from_blocks(block_ref, half):
    pair = block_ref[:, 16 * half : 16 * half + 16, :].astype(F32)
    return [pair[:, 8 * h : 8 * h + 8].reshape(256, CH).astype(BF16) for h in range(2)]


def matmul(left, right, dims=((1,), (0,))):
    return lax.dot_general(left, right, (dims, ((), ())), preferred_element_type=F32)


def fetch(source, target, sem):
    copy = pltpu.make_async_copy(source, target, sem)
    copy.start()
    return copy


def saved_coeffs_kernel(x_hbm, forward_hbm, out_ref, x_ref, forward_ref, sems):
    table = fetch(forward_hbm, forward_ref, sems.at[ROWS])
    cycles = [fetch(x_hbm.at[j], x_ref.at[j], sems.at[j]) for j in range(ROWS)]
    table.wait()
    for half in range(2):
        cycles[2 * half].wait()
        cycles[2 * half + 1].wait()
        to_blocks(out_ref, half, [matmul(forward_ref[...], x_ref[2 * half + h]) for h in range(2)])


def fresh_coeffs_kernel(x_ref, forward_ref, *rest):
    *sources, own_ref, lent_ref, packed_ref, work_ref = rest
    row = 0
    for source in sources:
        rows, columns = source.shape
        for start in range(0, columns, CH):
            width = min(CH, columns - start)
            packed_ref[row : row + rows, :width] = source[:, start : start + width]
            row += rows
    for j in range(ROWS):
        coeffs = matmul(forward_ref[...], x_ref[j])
        for place in range(8):
            target = pl.ds(place // 2 * 256 + j * 2 + place % 2, PEERS, stride=8)
            work_ref[target, :] = coeffs[place * PEERS : (place + 1) * PEERS]
    groups = [work_ref[256 * u : 256 * u + 256, :].reshape(PEERS, 8, CH) for u in range(ROWS)]
    own_ref[...] = jnp.concatenate(groups[:3], axis=1).astype(BF16)
    lent_ref[...] = groups[3].astype(BF16)


def padded_filter(filt_ref):
    rest = jnp.zeros((LANES - NLAT, CH), F32)
    return [jnp.concatenate([filt_ref[part], rest], axis=0) for part in range(2)]


def filter_step(spectra, real, imag):
    first, second = spectra[:, :CH], spectra[:, CH:]
    return jnp.concatenate(
        [real * first - imag * second, real * second + imag * first], axis=1
    ).astype(BF16)


def spectral(came_ref, goes_ref, ana_ref, syn_ref, filt_ref, spectra_ref):
    real, imag = padded_filter(filt_ref)
    for t in range(ROWS):
        parts = [came_ref[pl.ds(r * ROWS + t, LANES, stride=8), :] for r in range(2)]
        spectra = matmul(ana_ref[t], jnp.concatenate(parts, axis=1).astype(BF16))
        spectra_ref[t] = spectra
        values = matmul(syn_ref[t], filter_step(spectra, real, imag), ((0,), (0,)))
        for r in range(2):
            goes_ref[pl.ds(r * ROWS + t, LANES, stride=8), :] = values[:, r * CH : (r + 1) * CH]


def saved_spectral_kernel(
    arrived_ref, ana_ref, syn_ref, filt_ref, beside_ref, out_ref, spectra_ref, came_ref, goes_ref
):
    out_ref[:, 32:, :] = beside_ref[...]
    came_ref[...] = arrived_ref[...].reshape(LANES * 8, CH).astype(F32)
    spectral(came_ref, goes_ref, ana_ref, syn_ref, filt_ref, spectra_ref)
    out_ref[:, :32, :] = goes_ref[...].reshape(PEERS, 32, CH).astype(BF16)


def fresh_spectral(arrived_ref, ana_ref, syn_ref, filters_ref, last_ref, came_ref, goes_ref):
    came = arrived_ref[:, 32:, :].astype(F32)
    last = last_ref[0]
    for u in range(3):
        came_ref[256 * u : 256 * u + 256, :] = came[:, 8 * u : 8 * u + 8].reshape(256, CH)
        real, imag = padded_filter(filters_ref.at[u])
        t = jnp.where(last == 1, 3, u)
        parts = [came_ref[pl.ds(256 * u + r, LANES, stride=2), :] for r in range(2)]
        spectra = matmul(ana_ref[t], jnp.concatenate(parts, axis=1).astype(BF16))
        values = matmul(syn_ref[t], filter_step(spectra, real, imag), ((0,), (0,)))
        for r in range(2):
            goes_ref[pl.ds(256 * u + r, LANES, stride=2), :] = values[:, r * CH : (r + 1) * CH]
    groups = [goes_ref[256 * u : 256 * u + 256, :].reshape(PEERS, 8, CH) for u in range(3)]
    return jnp.concatenate(groups, axis=1).astype(BF16)


def spectral_back_kernel(
    arrived_ref,
    spectra_ref,
    ana_ref,
    syn_ref,
    filt_ref,
    shares_ref,
    out_ref,
    came_ref,
    goes_ref,
):
    came_ref[...] = arrived_ref[:, :32, :].reshape(LANES * 8, CH).astype(F32)
    real, imag = padded_filter(filt_ref)
    total_real = jnp.zeros((LANES, CH), F32)
    total_imag = jnp.zeros((LANES, CH), F32)
    for t in range(ROWS):
        parts = [came_ref[pl.ds(r * ROWS + t, LANES, stride=8), :] for r in range(2)]
        grads = matmul(syn_ref[t], jnp.concatenate(parts, axis=1).astype(BF16))
        first, second = grads[:, :CH], grads[:, CH:]
        spectra = spectra_ref[t]
        s_first, s_second = spectra[:, :CH], spectra[:, CH:]
        total_real = total_real + (first * s_first + second * s_second)
        total_imag = total_imag + (second * s_first - first * s_second)
        grad_spectra = jnp.concatenate(
            [real * first + imag * second, real * second - imag * first], axis=1
        ).astype(BF16)
        coeffs = matmul(ana_ref[t], grad_spectra, ((0,), (0,)))
        for r in range(2):
            goes_ref[pl.ds(r * ROWS + t, LANES, stride=8), :] = coeffs[:, r * CH : (r + 1) * CH]
    out_ref[:, :32, :] = goes_ref[...].reshape(PEERS, 32, CH).astype(BF16)
    filter_part = jnp.concatenate([total_real, total_imag], axis=0).reshape(PEERS, 8, CH)
    sums = jnp.concatenate([shares_ref[...].astype(F32), filter_part], axis=1)
    out_ref[:, 32:, :] = sums.astype(BF16)


PLACES = {}
for _name, _rows, _columns in (
    ("contract", HID, CH),
    ("expand", CH, HID),
    ("inverse", NLON, 256),
    ("fresh_inverse", NLON, 256),
    ("inverse_t", 256, NLON),
):
    PLACES[_name] = (sum(r * -(-c // CH) for _, r, c in PLACES.values()), _rows, _columns)
PACKED_ROWS = sum(r * -(-c // CH) for _, r, c in PLACES.values())


def unpacked(packed_ref, name):
    row, rows, columns = PLACES[name]
    blocks = [
        packed_ref[row + n * rows : row + (n + 1) * rows, :] for n in range(-(-columns // CH))
    ]
    return jnp.concatenate(blocks, axis=1)[:, :columns] if len(blocks) > 1 else blocks[0]


def live(cycle_ref, j):
    return jnp.where(cycle_ref[j] < NLAT, 1.0, 0.0).astype(F32)


def mlp_kernel(
    x_ref,
    values_ref,
    lent_a_ref,
    lent_b_ref,
    lent_c_ref,
    packed_ref,
    cycle_ref,
    out_ref,
    work_ref,
):
    names = ("fresh_inverse", "expand", "contract")
    inverse, expand, contract = [unpacked(packed_ref, name) for name in names]
    own = values_ref[:, 32:, :].astype(F32)
    lent = [ref[...].astype(F32) for ref in (lent_a_ref, lent_b_ref, lent_c_ref)]
    for u in range(3):
        work_ref[256 * u : 256 * u + 256, :] = own[:, 8 * u : 8 * u + 8].reshape(256, CH)
    work_ref[768:, :] = (lent[0] + lent[1] + lent[2]).reshape(256, CH)
    for j in range(ROWS):
        parts = [
            work_ref[pl.ds(place // 2 * 256 + j * 2 + place % 2, PEERS, stride=8), :]
            for place in range(8)
        ]
        values = jnp.concatenate(parts, axis=0).astype(BF16)
        mixed = x_ref[j].astype(F32) + matmul(inverse, values)
        pre = matmul(mixed.astype(BF16), expand)
        hidden = (0.5 * pre * (1.0 + lax.erf(pre * ROOT_HALF))).astype(BF16)
        result = mixed + matmul(hidden, contract)
        out_ref[j] = (result * live(cycle_ref, j)).astype(BF16)


def mlp_back_kernel(
    x_ref,
    values_ref,
    cotangent_ref,
    packed_ref,
    cycle_ref,
    ana_ref,
    syn_ref,
    filters_ref,
    last_ref,
    out_ref,
    grad_mixed_ref,
    shares_ref,
    mixed_ref,
    masked_ref,
    hidden_ref,
    grad_pre_ref,
    came_ref,
    goes_ref,
):
    names = ("inverse", "inverse_t", "expand", "contract")
    inverse, inverse_t, expand, contract = [unpacked(packed_ref, name) for name in names]
    for half in range(2):
        values = from_blocks(values_ref, half)
        grad_values = []
        for h in range(2):
            j = 2 * half + h
            rows = slice(j * NLON, (j + 1) * NLON)
            mixed = x_ref[j].astype(F32) + matmul(inverse, values[h])
            mixed_b = mixed.astype(BF16)
            masked_f = cotangent_ref[j].astype(F32) * live(cycle_ref, j)
            masked = masked_f.astype(BF16)
            mixed_ref[rows, :] = mixed_b
            masked_ref[rows, :] = masked
            pre = matmul(mixed_b, expand)
            normal = 0.5 * (1.0 + lax.erf(pre * ROOT_HALF))
            hidden_ref[rows, :] = (pre * normal).astype(BF16)
            slope = normal + pre * jnp.exp(-0.5 * pre * pre) * INV_ROOT_TAU
            grad_hidden = matmul(masked, contract, ((1,), (1,)))
            grad_pre = (grad_hidden * slope).astype(BF16)
            grad_pre_ref[rows, :] = grad_pre
            grad_mixed = masked_f + matmul(grad_pre, expand, ((1,), (1,)))
            grad_mixed_ref[j] = grad_mixed
            grad_values.append(matmul(inverse_t, grad_mixed.astype(BF16)))
        to_blocks(out_ref, half, grad_values)
    out_ref[:, 32:, :] = fresh_spectral(
        values_ref,
        ana_ref,
        syn_ref,
        filters_ref,
        last_ref,
        came_ref,
        goes_ref,
    )
    quarter = HID // 4
    pairs = ((grad_pre_ref, mixed_ref), (hidden_ref, masked_ref))
    for side, (wide_ref, narrow_ref) in enumerate(pairs):
        grad = matmul(wide_ref[...], narrow_ref[...], ((0,), (0,))).astype(BF16)
        for d in range(4):
            shares_ref[side, d] = grad[d * quarter : (d + 1) * quarter]


def input_grad_kernel(coeffs_ref, grad_mixed_ref, forward_ref, cycle_ref, out_ref):
    for half in range(2):
        values = from_blocks(coeffs_ref, half)
        for h in range(2):
            j = 2 * half + h
            total = grad_mixed_ref[j] + matmul(forward_ref[...], values[h])
            out_ref[j] = (total * live(cycle_ref, j)).astype(BF16)


def piece_kernel(arrived_ref, out_ref):
    came = arrived_ref[:, 32:, :].astype(F32).reshape(PEERS // 2, 2, 16, CH)
    sums = came.sum(axis=0)
    piece = jnp.concatenate([sums[0, :8], sums[1, :8], sums[0, 8:] + sums[1, 8:]], axis=0)
    out_ref[...] = jnp.broadcast_to(piece[None], out_ref.shape).astype(BF16)


def filter_rows_kernel(pieces_ref, out_ref):
    rows = pieces_ref[...].astype(F32)[:, 16:].reshape(128, CH).astype(BF16)
    out_ref[...] = jnp.broadcast_to(rows[None], out_ref.shape)


def result_kernel(
    pieces_ref,
    other_ref,
    filter_rows_ref,
    core_ref,
    next_ref,
    back_ref,
    expand_ref,
    reduce_ref,
    filter_ref,
    next_out_ref,
    back_out_ref,
):
    next_out_ref[...] = next_ref[...]
    back_out_ref[...] = back_ref[...]
    first = core_ref[0] == 0
    filters = [filter_rows_ref[4 * c : 4 * c + 4].astype(F32).sum(axis=0) for c in range(2)]
    for p in range(PEERS):
        mine, other = pieces_ref[p // 2].astype(F32), other_ref[p // 2].astype(F32)
        piece = jnp.where(first, mine, other) if p % 2 == 0 else jnp.where(first, other, mine)
        expand_ref[p * 6 : p * 6 + 6, :] = piece[:6]
        reduce_ref[p * 6 : p * 6 + 6, :] = piece[8:14]
        side, at = divmod(p, PEERS // 2)
        if at < NLAT // 8:
            rows = filters[p % 2][p // 2 * 8 : p // 2 * 8 + 8]
            filter_ref[side, at * 8 : at * 8 + 8, :] = rows


def call(
    kernel, outs, args, scratch=(), flops=0, transcendentals=0, smem=(), hbm=(), limit=VMEM_LIMIT
):
    places = {n: pltpu.SMEM for n in smem} | {n: pl.ANY for n in hbm}
    specs = [pl.BlockSpec(memory_space=places.get(n, pltpu.VMEM)) for n in range(len(args))]
    moved = sum(a.size * a.dtype.itemsize for a in (*args, *outs))
    return pl.pallas_call(
        kernel,
        out_shape=outs,
        in_specs=specs,
        out_specs=[pl.BlockSpec(memory_space=pltpu.VMEM)] * len(outs),
        scratch_shapes=list(scratch),
        compiler_params=pltpu.CompilerParams(vmem_limit_bytes=limit),
        cost_estimate=pl.CostEstimate(
            flops=flops, bytes_accessed=moved, transcendentals=transcendentals
        ),
    )(*args)


PAIRED = jax.ShapeDtypeStruct((PEERS, 56, CH), BF16)
OWN = jax.ShapeDtypeStruct((PEERS, 24, CH), BF16)
LENT = jax.ShapeDtypeStruct((PEERS, 8, CH), BF16)
SUMMED = jax.ShapeDtypeStruct((PEERS, 48, CH), BF16)
BLOCKS = jax.ShapeDtypeStruct((PEERS, 32, CH), BF16)
TOKENS = jax.ShapeDtypeStruct((ROWS, NLON, CH), BF16)
SPECTRAL_SCRATCH = (pltpu.VMEM((LANES * 8, CH), F32), pltpu.VMEM((LANES * 8, CH), F32))


CORE_SWAP = [(0, 1), (1, 0)]


def exchange(blocks, axes):
    return lax.all_to_all(blocks, axes, split_axis=0, concat_axis=0, tiled=True)


def from_behind(block, axis, distance):
    devices = range(lax.axis_size(axis))
    route = [(i - distance, i) for i in devices if i - distance in devices]
    return lax.ppermute(block, axis, route)


def to_last(block):
    return [lax.ppermute(block, "pipe", [(p, 3)]) for p in range(3)]


def halved(blocks, axis, route, kept):
    mine = lax.dynamic_index_in_dim(blocks, kept, 0, keepdims=False)
    sent = lax.dynamic_index_in_dim(blocks, 1 - kept, 0, keepdims=False)
    came = lax.ppermute(sent, axis, route)
    return (mine.astype(F32) + came.astype(F32)).astype(BF16)


def around(block, axis, distance):
    count = lax.axis_size(axis)
    return lax.ppermute(block, axis, [(i, (i + distance) % count) for i in range(count)])


def scattered_total(blocks, axis):
    count = lax.axis_size(axis)
    me = lax.axis_index(axis)

    def block_of(distance):
        return lax.dynamic_index_in_dim(blocks, (me + distance) % count, 0, keepdims=False)

    came = [around(block_of(k), axis, k) for k in range(1, count)]
    return sum((block.astype(F32) for block in came), block_of(0).astype(F32))


def share_blocks_of(shares):
    kept = halved(shares, "sp_1", CORE_SWAP, lax.axis_index("sp_1"))
    kept = scattered_total(kept, "dp").astype(BF16)
    return jnp.pad(kept.reshape(PEERS, 6, CH), ((0, 0), (0, 2), (0, 0)))


def on_device(
    tables_np,
    orders_np,
    fresh_input,
    saved_input,
    output_grad,
    expand_weight,
    reduce_weight,
    filter_weight,
    cycle_table,
):
    position = lax.axis_index(SP)
    fresh, saved, cotangent = fresh_input[0, 0], saved_input[0, 0], output_grad[0, 0]
    expand, contract, filt = expand_weight[0], reduce_weight[0], filter_weight[0]
    forward_np, inverse_np, fresh_forward_np, fresh_inverse_np = tables_np
    forward = jnp.asarray(forward_np)
    fresh_forward_t = jnp.asarray(np.ascontiguousarray(fresh_forward_np.T))
    fresh_inverse = jnp.asarray(fresh_inverse_np)
    last = lax.axis_index("pipe") == 3
    forward_t = jnp.asarray(np.ascontiguousarray(forward_np.T))
    inverse = jnp.asarray(inverse_np)
    inverse_t = jnp.asarray(np.ascontiguousarray(inverse_np.T))
    own_cycles = lax.dynamic_slice_in_dim(cycle_table, position * ROWS, ROWS)
    dft = 2 * ROWS * 256 * NLON * CH
    leg = 2 * 16 * 128 * 128 * CH
    mlp = 2 * ROWS * NLON * CH * HID

    saved_blocks = call(
        saved_coeffs_kernel,
        [BLOCKS],
        [saved, forward_t],
        (
            pltpu.VMEM((ROWS, NLON, CH), BF16),
            pltpu.VMEM((256, NLON), BF16),
            pltpu.SemaphoreType.DMA((ROWS + 1,)),
        ),
        flops=dft,
        hbm=(0, 1),
        limit=60 * 1024 * 1024,
    )[0]
    saved_at_orders = exchange(saved_blocks, SP)
    kept = [contract, expand, inverse, fresh_inverse, inverse_t]
    fresh_own, fresh_lent, packed = call(
        fresh_coeffs_kernel,
        [OWN, LENT, jax.ShapeDtypeStruct((PACKED_ROWS, CH), BF16)],
        [fresh, fresh_forward_t, *kept],
        [pltpu.VMEM((LANES * 8, CH), F32)],
        flops=dft,
    )
    fresh_blocks = jnp.where(last, jnp.concatenate(to_last(fresh_lent), axis=1), fresh_own)

    lat_live = (cycle_table < NLAT).astype(F32)
    colatitude = math.pi * (jnp.minimum(cycle_table, NLAT - 1).astype(F32) + 0.5) / NLAT
    sine = jnp.sin(colatitude)
    geo = jnp.stack(
        [jnp.cos(colatitude), jnp.log(sine), math.pi / NLAT * sine * lat_live, lat_live]
    )
    order_rows = lax.dynamic_index_in_dim(jnp.asarray(orders_np), position, 0, keepdims=False)
    tables = jax.ShapeDtypeStruct((ROWS, LANES, LANES), BF16)
    ana, syn = call(
        tables_kernel,
        [tables, tables],
        [geo, order_rows],
        [pltpu.VMEM((LANES * 8, LANES), F32)],
        flops=4_000_000,
    )

    spectra_shape = jax.ShapeDtypeStruct((ROWS, LANES, 2 * CH), F32)
    values_fresh, spectra = call(
        saved_spectral_kernel,
        [PAIRED, spectra_shape],
        [saved_at_orders, ana, syn, filt, fresh_blocks],
        SPECTRAL_SCRATCH,
        flops=leg,
    )
    lent_filt, values_fresh = lax.optimization_barrier((filt, values_fresh))
    fresh_filters = jnp.where(last, jnp.stack(to_last(lent_filt)), filt[None])
    values_fresh = exchange(values_fresh, SP)

    narrow = pltpu.VMEM((ROWS * NLON, CH), BF16)
    wide = pltpu.VMEM((ROWS * NLON, HID), BF16)
    grads_fresh, grad_mixed, shares = call(
        mlp_back_kernel,
        [
            PAIRED,
            jax.ShapeDtypeStruct((ROWS, NLON, CH), F32),
            jax.ShapeDtypeStruct((2, 4, HID // 4, CH), BF16),
        ],
        [
            saved,
            values_fresh,
            cotangent,
            packed,
            own_cycles,
            ana,
            syn,
            fresh_filters,
            last.astype(jnp.int32)[None],
        ],
        [narrow, narrow, wide, wide, *SPECTRAL_SCRATCH],
        flops=5 * mlp + 2 * dft + leg,
        transcendentals=2 * ROWS * NLON * HID,
        smem=(4, 8),
    )
    grads_fresh = exchange(grads_fresh, SP)
    share_blocks = share_blocks_of(shares)

    lent_values = [
        lax.ppermute(grads_fresh[:, 32 + 8 * p : 40 + 8 * p], "pipe", [(3, p)]) for p in range(3)
    ]
    block = call(
        mlp_kernel,
        [TOKENS],
        [fresh, grads_fresh, *lent_values, packed, own_cycles],
        [pltpu.VMEM((LANES * 8, CH), F32)],
        flops=2 * mlp + dft,
        transcendentals=ROWS * NLON * HID,
        smem=(6,),
    )[0]
    next_input = from_behind(block, "pipe", 1)
    coeffs_summed = call(
        spectral_back_kernel,
        [SUMMED],
        [grads_fresh, spectra, ana, syn, filt, share_blocks],
        SPECTRAL_SCRATCH,
        flops=leg,
    )[0]
    coeffs_summed = exchange(coeffs_summed, SP)
    coeffs_summed, _ = lax.optimization_barrier((coeffs_summed, block))
    pieces = call(
        piece_kernel, [jax.ShapeDtypeStruct((PEERS // 2, 24, CH), BF16)], [coeffs_summed]
    )[0]
    pieces = exchange(pieces, "sp_0")
    filter_rows = call(
        filter_rows_kernel, [jax.ShapeDtypeStruct((8, 128, CH), BF16)], [pieces]
    )[0]
    filter_rows = exchange(filter_rows, ("sp_1", "dp"))
    other_pieces = lax.ppermute(pieces, "sp_1", CORE_SWAP)
    input_grad = call(
        input_grad_kernel,
        [TOKENS],
        [coeffs_summed, grad_mixed, forward, own_cycles],
        flops=dft,
        smem=(3,),
    )[0]
    sent_back = from_behind(input_grad, "pipe", -1)
    part = jax.ShapeDtypeStruct((HID // 4, CH), F32)
    core = lax.axis_index("sp_1").astype(jnp.int32)[None]
    expand_grad, reduce_grad, filter_grad, next_input, sent_back = call(
        result_kernel,
        [part, part, jax.ShapeDtypeStruct((2, NLAT, CH), F32), TOKENS, TOKENS],
        [pieces, other_pieces, filter_rows, core, next_input, sent_back],
        smem=(3,),
    )
    return (
        next_input[None, None],
        sent_back[None, None],
        expand_grad.T[None],
        reduce_grad[None],
        filter_grad[None],
    )


def solution(mesh):
    finer = Mesh(
        mesh.devices.reshape(mesh.shape["pipe"], 16, 2, mesh.shape["dp"]),
        ("pipe", "sp_0", "sp_1", "dp"),
    )
    in_specs = (
        P("pipe", "dp", SP, None, None),
        P("pipe", "dp", SP, None, None),
        P("pipe", "dp", SP, None, None),
        P("pipe", None, None),
        P("pipe", None, None),
        P("pipe", None, None, None),
        P(),
    )
    out_specs = (
        P("pipe", "dp", SP, None, None),
        P("pipe", "dp", SP, None, None),
        P("pipe", None, "dp"),
        P("pipe", "dp", None),
        P("pipe", None, None, None),
    )
    program = functools.partial(on_device, fourier_constants(), order_constants())
    return jax.shard_map(
        program, mesh=finer, in_specs=in_specs, out_specs=out_specs, check_vma=False
    )
```

```python
import functools
import math

import jax
import jax.numpy as jnp
import numpy as np
from jax import lax
from jax.experimental import pallas as pl
from jax.experimental.pallas import tpu as pltpu
from jax.sharding import Mesh
from jax.sharding import PartitionSpec as P

NLAT = 120
NLON = 240
CH = 128
HID = 768
ROWS = 4
PEERS = 32
VMEM_LIMIT = 16 * 1024 * 1024
LANES = 128
SP = ("sp_0", "sp_1")

ROOT_HALF = 0.7071067811865476
INV_ROOT_TAU = 0.3989422804014327
F32 = jnp.float32
BF16 = jnp.bfloat16


def fourier_constants():
    order = np.arange(128)
    live = (order < NLAT).astype(np.float64)
    value = np.minimum(order, NLAT - 1)
    phase = 2.0 * math.pi / NLON * ((np.arange(NLON)[:, None] * value[None, :]) % NLON)
    scaled = live * (2.0 * math.pi / NLON)
    forward = np.stack([np.cos(phase) * scaled, -np.sin(phase) * scaled], axis=1)
    factor = np.where(value == 0, 1.0, 2.0) * live / (2.0 * math.pi)
    inverse = np.stack([np.cos(phase) * factor, -np.sin(phase) * factor], axis=1)

    def arranged(table, places):
        table = table.reshape(NLON, 2, PEERS, ROWS).transpose(0, *places)
        return table.reshape(NLON, 256).astype(np.float32).astype(jnp.bfloat16)

    saved, fresh = (2, 1, 3), (3, 1, 2)
    return [arranged(table, places) for places in (saved, fresh) for table in (forward, inverse)]


def order_constants():
    table = np.zeros((PEERS, 3, 8, LANES), np.float32)
    for position in range(PEERS):
        for row in range(8):
            slot = position * ROWS + row % ROWS
            m = min(slot, NLAT - 1)
            log_start = 0.5 * (
                math.log((2.0 * m + 1.0) / (4.0 * math.pi))
                + math.lgamma(2.0 * m + 1.0)
                - 2.0 * math.lgamma(m + 1.0)
                - m * math.log(4.0)
            )
            table[position, 0, row] = m
            table[position, 1, row] = log_start
            table[position, 2, row] = float(slot < NLAT)
    return table


def tables_kernel(geo_ref, order_ref, ana_ref, syn_ref, work_ref):
    shape = (8, LANES)
    cosine = jnp.broadcast_to(geo_ref[0:1, :], shape)
    log_sine = jnp.broadcast_to(geo_ref[1:2, :], shape)
    weight = geo_ref[2:3, :]
    m = order_ref[0]
    keep = order_ref[2] * jnp.broadcast_to(geo_ref[3:4, :], shape)
    starting = jnp.exp(order_ref[1] + m * log_sine)
    squares = m * m
    previous = jnp.zeros(shape, F32)
    earlier = previous
    for degree in range(NLAT):
        upper = max(4.0 * degree * degree - 1.0, 0.0)
        lower = max(4.0 * (degree - 1.0) ** 2 - 1.0, 1.0)
        ratio_main = jnp.sqrt(upper / jnp.maximum(float(degree * degree) - squares, 1.0))
        ratio_back = jnp.sqrt(jnp.maximum((degree - 1.0) ** 2 - squares, 0.0) / lower)
        rising = ratio_main * (cosine * previous - ratio_back * earlier)
        current = jnp.where(m == float(degree), starting, jnp.where(m < float(degree), rising, 0.0))
        work_ref[degree * 8 : degree * 8 + 8, :] = current * keep
        previous, earlier = current, previous
    work_ref[NLAT * 8 :, :] = jnp.zeros((LANES * 8 - NLAT * 8, LANES), F32)
    for t in range(ROWS):
        table = work_ref[pl.ds(t, LANES, stride=8), :]
        syn_ref[t] = table.astype(BF16)
        ana_ref[t] = (table * weight).astype(BF16)


def to_blocks(out_ref, half, pair):
    blocks = [part.reshape(PEERS, 8, CH) for part in pair]
    out_ref[:, 16 * half : 16 * half + 16, :] = jnp.concatenate(blocks, axis=1).astype(BF16)


def from_blocks(block_ref, half):
    pair = block_ref[:, 16 * half : 16 * half + 16, :].astype(F32)
    return [pair[:, 8 * h : 8 * h + 8].reshape(256, CH).astype(BF16) for h in range(2)]


def matmul(left, right, dims=((1,), (0,))):
    return lax.dot_general(left, right, (dims, ((), ())), preferred_element_type=F32)


def fetch(source, target, sem):
    copy = pltpu.make_async_copy(source, target, sem)
    copy.start()
    return copy


def saved_coeffs_kernel(x_hbm, forward_hbm, out_ref, x_ref, forward_ref, sems):
    table = fetch(forward_hbm, forward_ref, sems.at[ROWS])
    cycles = [fetch(x_hbm.at[j], x_ref.at[j], sems.at[j]) for j in range(ROWS)]
    table.wait()
    for half in range(2):
        cycles[2 * half].wait()
        cycles[2 * half + 1].wait()
        to_blocks(out_ref, half, [matmul(forward_ref[...], x_ref[2 * half + h]) for h in range(2)])


def fresh_coeffs_kernel(x_ref, forward_ref, *rest):
    *sources, own_ref, lent_ref, packed_ref, work_ref = rest
    row = 0
    for source in sources:
        rows, columns = source.shape
        for start in range(0, columns, CH):
            width = min(CH, columns - start)
            packed_ref[row : row + rows, :width] = source[:, start : start + width]
            row += rows
    for j in range(ROWS):
        coeffs = matmul(forward_ref[...], x_ref[j])
        for place in range(8):
            target = pl.ds(place // 2 * 256 + j * 2 + place % 2, PEERS, stride=8)
            work_ref[target, :] = coeffs[place * PEERS : (place + 1) * PEERS]
    groups = [work_ref[256 * u : 256 * u + 256, :].reshape(PEERS, 8, CH) for u in range(ROWS)]
    own_ref[...] = jnp.concatenate(groups[:3], axis=1).astype(BF16)
    lent_ref[...] = groups[3].astype(BF16)


def padded_filter(filt_ref):
    rest = jnp.zeros((LANES - NLAT, CH), F32)
    return [jnp.concatenate([filt_ref[part], rest], axis=0) for part in range(2)]


def filter_step(spectra, real, imag):
    first, second = spectra[:, :CH], spectra[:, CH:]
    return jnp.concatenate(
        [real * first - imag * second, real * second + imag * first], axis=1
    ).astype(BF16)


def spectral(came_ref, goes_ref, ana_ref, syn_ref, filt_ref, spectra_ref):
    real, imag = padded_filter(filt_ref)
    for t in range(ROWS):
        parts = [came_ref[pl.ds(r * ROWS + t, LANES, stride=8), :] for r in range(2)]
        spectra = matmul(ana_ref[t], jnp.concatenate(parts, axis=1).astype(BF16))
        spectra_ref[t] = spectra.astype(BF16)
        values = matmul(syn_ref[t], filter_step(spectra, real, imag), ((0,), (0,)))
        for r in range(2):
            goes_ref[pl.ds(r * ROWS + t, LANES, stride=8), :] = values[:, r * CH : (r + 1) * CH]


def saved_spectral_kernel(
    arrived_ref, ana_ref, syn_ref, filt_ref, beside_ref, out_ref, spectra_ref, came_ref, goes_ref
):
    out_ref[:, 32:, :] = beside_ref[...]
    came_ref[...] = arrived_ref[...].reshape(LANES * 8, CH).astype(F32)
    spectral(came_ref, goes_ref, ana_ref, syn_ref, filt_ref, spectra_ref)
    out_ref[:, :32, :] = goes_ref[...].reshape(PEERS, 32, CH).astype(BF16)


def fresh_spectral(arrived_ref, ana_ref, syn_ref, filters_ref, last_ref, came_ref, goes_ref):
    came = arrived_ref[:, 32:, :].astype(F32)
    last = last_ref[0]
    for u in range(3):
        came_ref[256 * u : 256 * u + 256, :] = came[:, 8 * u : 8 * u + 8].reshape(256, CH)
        real, imag = padded_filter(filters_ref.at[u])
        t = jnp.where(last == 1, 3, u)
        parts = [came_ref[pl.ds(256 * u + r, LANES, stride=2), :] for r in range(2)]
        spectra = matmul(ana_ref[t], jnp.concatenate(parts, axis=1).astype(BF16))
        values = matmul(syn_ref[t], filter_step(spectra, real, imag), ((0,), (0,)))
        for r in range(2):
            goes_ref[pl.ds(256 * u + r, LANES, stride=2), :] = values[:, r * CH : (r + 1) * CH]
    groups = [goes_ref[256 * u : 256 * u + 256, :].reshape(PEERS, 8, CH) for u in range(3)]
    return jnp.concatenate(groups, axis=1).astype(BF16)


def spectral_back_kernel(
    arrived_ref,
    spectra_ref,
    ana_ref,
    syn_ref,
    filt_ref,
    shares_ref,
    out_ref,
    came_ref,
    goes_ref,
):
    came_ref[...] = arrived_ref[:, :32, :].reshape(LANES * 8, CH).astype(F32)
    real, imag = padded_filter(filt_ref)
    total_real = jnp.zeros((LANES, CH), F32)
    total_imag = jnp.zeros((LANES, CH), F32)
    for t in range(ROWS):
        parts = [came_ref[pl.ds(r * ROWS + t, LANES, stride=8), :] for r in range(2)]
        grads = matmul(syn_ref[t], jnp.concatenate(parts, axis=1).astype(BF16))
        first, second = grads[:, :CH], grads[:, CH:]
        spectra = spectra_ref[t].astype(F32)
        s_first, s_second = spectra[:, :CH], spectra[:, CH:]
        total_real = total_real + (first * s_first + second * s_second)
        total_imag = total_imag + (second * s_first - first * s_second)
        grad_spectra = jnp.concatenate(
            [real * first + imag * second, real * second - imag * first], axis=1
        ).astype(BF16)
        coeffs = matmul(ana_ref[t], grad_spectra, ((0,), (0,)))
        for r in range(2):
            goes_ref[pl.ds(r * ROWS + t, LANES, stride=8), :] = coeffs[:, r * CH : (r + 1) * CH]
    out_ref[:, :32, :] = goes_ref[...].reshape(PEERS, 32, CH).astype(BF16)
    filter_part = jnp.concatenate([total_real, total_imag], axis=0).reshape(PEERS, 8, CH)
    sums = jnp.concatenate([shares_ref[...].astype(F32), filter_part], axis=1)
    out_ref[:, 32:, :] = sums.astype(BF16)


PLACES = {}
for _name, _rows, _columns in (
    ("contract", HID, CH),
    ("expand", CH, HID),
    ("inverse", NLON, 256),
    ("fresh_inverse", NLON, 256),
    ("inverse_t", 256, NLON),
    ("cotangent", ROWS * NLON, CH),
):
    PLACES[_name] = (sum(r * -(-c // CH) for _, r, c in PLACES.values()), _rows, _columns)
PACKED_ROWS = sum(r * -(-c // CH) for _, r, c in PLACES.values())


def unpacked(packed_ref, name):
    row, rows, columns = PLACES[name]
    blocks = [
        packed_ref[row + n * rows : row + (n + 1) * rows, :] for n in range(-(-columns // CH))
    ]
    return jnp.concatenate(blocks, axis=1)[:, :columns] if len(blocks) > 1 else blocks[0]


def live(cycle_ref, j):
    return jnp.where(cycle_ref[j] < NLAT, 1.0, 0.0).astype(F32)


def mlp_kernel(
    x_ref,
    values_ref,
    lent_a_ref,
    lent_b_ref,
    lent_c_ref,
    packed_ref,
    cycle_ref,
    out_ref,
    work_ref,
):
    names = ("fresh_inverse", "expand", "contract")
    inverse, expand, contract = [unpacked(packed_ref, name) for name in names]
    own = values_ref[:, 32:, :].astype(F32)
    lent = [ref[...].astype(F32) for ref in (lent_a_ref, lent_b_ref, lent_c_ref)]
    for u in range(3):
        work_ref[256 * u : 256 * u + 256, :] = own[:, 8 * u : 8 * u + 8].reshape(256, CH)
    work_ref[768:, :] = (lent[0] + lent[1] + lent[2]).reshape(256, CH)
    for j in range(ROWS):
        parts = [
            work_ref[pl.ds(place // 2 * 256 + j * 2 + place % 2, PEERS, stride=8), :]
            for place in range(8)
        ]
        values = jnp.concatenate(parts, axis=0).astype(BF16)
        mixed = x_ref[j].astype(F32) + matmul(inverse, values)
        pre = matmul(mixed.astype(BF16), expand)
        hidden = (0.5 * pre * (1.0 + lax.erf(pre * ROOT_HALF))).astype(BF16)
        result = mixed + matmul(hidden, contract)
        out_ref[j] = (result * live(cycle_ref, j)).astype(BF16)


def mlp_back_kernel(
    x_ref,
    values_ref,
    packed_ref,
    cycle_ref,
    ana_ref,
    syn_ref,
    filters_ref,
    last_ref,
    out_ref,
    grad_mixed_ref,
    shares_ref,
    mixed_ref,
    masked_ref,
    hidden_ref,
    grad_pre_ref,
    came_ref,
    goes_ref,
):
    names = ("inverse", "inverse_t", "expand", "contract")
    inverse, inverse_t, expand, contract = [unpacked(packed_ref, name) for name in names]
    cotangent = unpacked(packed_ref, "cotangent")
    for half in range(2):
        values = from_blocks(values_ref, half)
        grad_values = []
        for h in range(2):
            j = 2 * half + h
            rows = slice(j * NLON, (j + 1) * NLON)
            mixed = x_ref[j].astype(F32) + matmul(inverse, values[h])
            mixed_b = mixed.astype(BF16)
            masked_f = cotangent[rows].astype(F32) * live(cycle_ref, j)
            masked = masked_f.astype(BF16)
            mixed_ref[rows, :] = mixed_b
            masked_ref[rows, :] = masked
            pre = matmul(mixed_b, expand)
            normal = 0.5 * (1.0 + lax.erf(pre * ROOT_HALF))
            hidden_ref[rows, :] = (pre * normal).astype(BF16)
            slope = normal + pre * jnp.exp(-0.5 * pre * pre) * INV_ROOT_TAU
            grad_hidden = matmul(masked, contract, ((1,), (1,)))
            grad_pre = (grad_hidden * slope).astype(BF16)
            grad_pre_ref[rows, :] = grad_pre
            grad_mixed = masked_f + matmul(grad_pre, expand, ((1,), (1,)))
            grad_mixed_ref[j] = grad_mixed.astype(BF16)
            grad_values.append(matmul(inverse_t, grad_mixed.astype(BF16)))
        to_blocks(out_ref, half, grad_values)
    out_ref[:, 32:, :] = fresh_spectral(
        values_ref,
        ana_ref,
        syn_ref,
        filters_ref,
        last_ref,
        came_ref,
        goes_ref,
    )
    quarter = HID // 4
    pairs = ((grad_pre_ref, mixed_ref), (hidden_ref, masked_ref))
    for side, (wide_ref, narrow_ref) in enumerate(pairs):
        grad = matmul(wide_ref[...], narrow_ref[...], ((0,), (0,))).astype(BF16)
        for d in range(4):
            shares_ref[side, d] = grad[d * quarter : (d + 1) * quarter]


def input_grad_kernel(coeffs_ref, grad_mixed_ref, forward_ref, cycle_ref, out_ref):
    for half in range(2):
        values = from_blocks(coeffs_ref, half)
        for h in range(2):
            j = 2 * half + h
            total = grad_mixed_ref[j].astype(F32) + matmul(forward_ref[...], values[h])
            out_ref[j] = (total * live(cycle_ref, j)).astype(BF16)


def piece_kernel(arrived_ref, out_ref):
    came = arrived_ref[:, 32:, :].astype(F32).reshape(PEERS // 2, 2, 16, CH)
    sums = came.sum(axis=0)
    piece = jnp.concatenate([sums[0, :8], sums[1, :8], sums[0, 8:] + sums[1, 8:]], axis=0)
    out_ref[...] = jnp.broadcast_to(piece[None], out_ref.shape).astype(BF16)


def filter_rows_kernel(pieces_ref, out_ref):
    rows = pieces_ref[...].astype(F32)[:, 16:].reshape(128, CH).astype(BF16)
    out_ref[...] = jnp.broadcast_to(rows[None], out_ref.shape)


def result_kernel(
    pieces_ref,
    other_ref,
    filter_rows_ref,
    core_ref,
    next_ref,
    back_ref,
    expand_ref,
    reduce_ref,
    filter_ref,
    next_out_ref,
    back_out_ref,
):
    next_out_ref[...] = next_ref[...]
    back_out_ref[...] = back_ref[...]
    first = core_ref[0] == 0
    filters = [filter_rows_ref[4 * c : 4 * c + 4].astype(F32).sum(axis=0) for c in range(2)]
    for p in range(PEERS):
        mine, other = pieces_ref[p // 2].astype(F32), other_ref[p // 2].astype(F32)
        piece = jnp.where(first, mine, other) if p % 2 == 0 else jnp.where(first, other, mine)
        expand_ref[p * 6 : p * 6 + 6, :] = piece[:6]
        reduce_ref[p * 6 : p * 6 + 6, :] = piece[8:14]
        side, at = divmod(p, PEERS // 2)
        if at < NLAT // 8:
            rows = filters[p % 2][p // 2 * 8 : p // 2 * 8 + 8]
            filter_ref[side, at * 8 : at * 8 + 8, :] = rows


def call(
    kernel, outs, args, scratch=(), flops=0, transcendentals=0, smem=(), hbm=(), limit=VMEM_LIMIT
):
    places = {n: pltpu.SMEM for n in smem} | {n: pl.ANY for n in hbm}
    specs = [pl.BlockSpec(memory_space=places.get(n, pltpu.VMEM)) for n in range(len(args))]
    moved = sum(a.size * a.dtype.itemsize for a in (*args, *outs))
    return pl.pallas_call(
        kernel,
        out_shape=outs,
        in_specs=specs,
        out_specs=[pl.BlockSpec(memory_space=pltpu.VMEM)] * len(outs),
        scratch_shapes=list(scratch),
        compiler_params=pltpu.CompilerParams(vmem_limit_bytes=limit),
        cost_estimate=pl.CostEstimate(
            flops=flops, bytes_accessed=moved, transcendentals=transcendentals
        ),
    )(*args)


PAIRED = jax.ShapeDtypeStruct((PEERS, 56, CH), BF16)
OWN = jax.ShapeDtypeStruct((PEERS, 24, CH), BF16)
LENT = jax.ShapeDtypeStruct((PEERS, 8, CH), BF16)
SUMMED = jax.ShapeDtypeStruct((PEERS, 48, CH), BF16)
BLOCKS = jax.ShapeDtypeStruct((PEERS, 32, CH), BF16)
TOKENS = jax.ShapeDtypeStruct((ROWS, NLON, CH), BF16)
SPECTRAL_SCRATCH = (pltpu.VMEM((LANES * 8, CH), F32), pltpu.VMEM((LANES * 8, CH), F32))


CORE_SWAP = [(0, 1), (1, 0)]


def exchange(blocks, axes):
    return lax.all_to_all(blocks, axes, split_axis=0, concat_axis=0, tiled=True)


def from_behind(block, axis, distance):
    devices = range(lax.axis_size(axis))
    route = [(i - distance, i) for i in devices if i - distance in devices]
    return lax.ppermute(block, axis, route)


def to_last(block):
    return [lax.ppermute(block, "pipe", [(p, 3)]) for p in range(3)]


def halved(blocks, axis, route, kept):
    mine = lax.dynamic_index_in_dim(blocks, kept, 0, keepdims=False)
    sent = lax.dynamic_index_in_dim(blocks, 1 - kept, 0, keepdims=False)
    came = lax.ppermute(sent, axis, route)
    return (mine.astype(F32) + came.astype(F32)).astype(BF16)


def around(block, axis, distance):
    count = lax.axis_size(axis)
    return lax.ppermute(block, axis, [(i, (i + distance) % count) for i in range(count)])


def scattered_total(blocks, axis):
    count = lax.axis_size(axis)
    me = lax.axis_index(axis)

    def block_of(distance):
        return lax.dynamic_index_in_dim(blocks, (me + distance) % count, 0, keepdims=False)

    came = [around(block_of(k), axis, k) for k in range(1, count)]
    return sum((block.astype(F32) for block in came), block_of(0).astype(F32))


def share_blocks_of(shares):
    kept = halved(shares, "sp_1", CORE_SWAP, lax.axis_index("sp_1"))
    kept = scattered_total(kept, "dp").astype(BF16)
    return jnp.pad(kept.reshape(PEERS, 6, CH), ((0, 0), (0, 2), (0, 0)))


def on_device(
    tables_np,
    orders_np,
    fresh_input,
    saved_input,
    output_grad,
    expand_weight,
    reduce_weight,
    filter_weight,
    cycle_table,
):
    position = lax.axis_index(SP)
    fresh, saved, cotangent = fresh_input[0, 0], saved_input[0, 0], output_grad[0, 0]
    expand, contract, filt = expand_weight[0], reduce_weight[0], filter_weight[0]
    forward_np, inverse_np, fresh_forward_np, fresh_inverse_np = tables_np
    forward = jnp.asarray(forward_np)
    fresh_forward_t = jnp.asarray(np.ascontiguousarray(fresh_forward_np.T))
    fresh_inverse = jnp.asarray(fresh_inverse_np)
    last = lax.axis_index("pipe") == 3
    forward_t = jnp.asarray(np.ascontiguousarray(forward_np.T))
    inverse = jnp.asarray(inverse_np)
    inverse_t = jnp.asarray(np.ascontiguousarray(inverse_np.T))
    own_cycles = lax.dynamic_slice_in_dim(cycle_table, position * ROWS, ROWS)
    dft = 2 * ROWS * 256 * NLON * CH
    leg = 2 * 16 * 128 * 128 * CH
    mlp = 2 * ROWS * NLON * CH * HID

    saved_blocks = call(
        saved_coeffs_kernel,
        [BLOCKS],
        [saved, forward_t],
        (
            pltpu.VMEM((ROWS, NLON, CH), BF16),
            pltpu.VMEM((256, NLON), BF16),
            pltpu.SemaphoreType.DMA((ROWS + 1,)),
        ),
        flops=dft,
        hbm=(0, 1),
        limit=60 * 1024 * 1024,
    )[0]
    saved_at_orders = exchange(saved_blocks, SP)
    kept = [contract, expand, inverse, fresh_inverse, inverse_t]
    kept += [tokens.reshape(ROWS * NLON, CH) for tokens in (cotangent,)]
    fresh_own, fresh_lent, packed = call(
        fresh_coeffs_kernel,
        [OWN, LENT, jax.ShapeDtypeStruct((PACKED_ROWS, CH), BF16)],
        [fresh, fresh_forward_t, *kept],
        [pltpu.VMEM((LANES * 8, CH), F32)],
        flops=dft,
    )
    fresh_blocks = jnp.where(last, jnp.concatenate(to_last(fresh_lent), axis=1), fresh_own)

    lat_live = (cycle_table < NLAT).astype(F32)
    colatitude = math.pi * (jnp.minimum(cycle_table, NLAT - 1).astype(F32) + 0.5) / NLAT
    sine = jnp.sin(colatitude)
    geo = jnp.stack(
        [jnp.cos(colatitude), jnp.log(sine), math.pi / NLAT * sine * lat_live, lat_live]
    )
    order_rows = lax.dynamic_index_in_dim(jnp.asarray(orders_np), position, 0, keepdims=False)
    tables = jax.ShapeDtypeStruct((ROWS, LANES, LANES), BF16)
    ana, syn = call(
        tables_kernel,
        [tables, tables],
        [geo, order_rows],
        [pltpu.VMEM((LANES * 8, LANES), F32)],
        flops=4_000_000,
    )

    spectra_shape = jax.ShapeDtypeStruct((ROWS, LANES, 2 * CH), BF16)
    values_fresh, spectra = call(
        saved_spectral_kernel,
        [PAIRED, spectra_shape],
        [saved_at_orders, ana, syn, filt, fresh_blocks],
        SPECTRAL_SCRATCH,
        flops=leg,
    )
    lent_filt, values_fresh = lax.optimization_barrier((filt, values_fresh))
    fresh_filters = jnp.where(last, jnp.stack(to_last(lent_filt)), filt[None])
    values_fresh = exchange(values_fresh, SP)

    narrow = pltpu.VMEM((ROWS * NLON, CH), BF16)
    wide = pltpu.VMEM((ROWS * NLON, HID), BF16)
    grads_fresh, grad_mixed, shares = call(
        mlp_back_kernel,
        [
            PAIRED,
            TOKENS,
            jax.ShapeDtypeStruct((2, 4, HID // 4, CH), BF16),
        ],
        [
            saved,
            values_fresh,
            packed,
            own_cycles,
            ana,
            syn,
            fresh_filters,
            last.astype(jnp.int32)[None],
        ],
        [narrow, narrow, wide, wide, *SPECTRAL_SCRATCH],
        flops=5 * mlp + 2 * dft + leg,
        transcendentals=2 * ROWS * NLON * HID,
        smem=(3, 7),
    )
    grads_fresh = exchange(grads_fresh, SP)
    share_blocks = share_blocks_of(shares)

    lent_values = [
        lax.ppermute(grads_fresh[:, 32 + 8 * p : 40 + 8 * p], "pipe", [(3, p)]) for p in range(3)
    ]
    block = call(
        mlp_kernel,
        [TOKENS],
        [fresh, grads_fresh, *lent_values, packed, own_cycles],
        [pltpu.VMEM((LANES * 8, CH), F32)],
        flops=2 * mlp + dft,
        transcendentals=ROWS * NLON * HID,
        smem=(6,),
    )[0]
    next_input = from_behind(block, "pipe", 1)
    coeffs_summed = call(
        spectral_back_kernel,
        [SUMMED],
        [grads_fresh, spectra, ana, syn, filt, share_blocks],
        SPECTRAL_SCRATCH,
        flops=leg,
    )[0]
    coeffs_summed = exchange(coeffs_summed, SP)
    coeffs_summed, _ = lax.optimization_barrier((coeffs_summed, block))
    pieces = call(
        piece_kernel, [jax.ShapeDtypeStruct((PEERS // 2, 24, CH), BF16)], [coeffs_summed]
    )[0]
    pieces = exchange(pieces, "sp_0")
    filter_rows = call(
        filter_rows_kernel, [jax.ShapeDtypeStruct((8, 128, CH), BF16)], [pieces]
    )[0]
    filter_rows = exchange(filter_rows, ("sp_1", "dp"))
    other_pieces = lax.ppermute(pieces, "sp_1", CORE_SWAP)
    input_grad = call(
        input_grad_kernel,
        [TOKENS],
        [coeffs_summed, grad_mixed, forward, own_cycles],
        flops=dft,
        smem=(3,),
    )[0]
    sent_back = from_behind(input_grad, "pipe", -1)
    part = jax.ShapeDtypeStruct((HID // 4, CH), F32)
    core = lax.axis_index("sp_1").astype(jnp.int32)[None]
    expand_grad, reduce_grad, filter_grad, next_input, sent_back = call(
        result_kernel,
        [part, part, jax.ShapeDtypeStruct((2, NLAT, CH), F32), TOKENS, TOKENS],
        [pieces, other_pieces, filter_rows, core, next_input, sent_back],
        smem=(3,),
    )
    return (
        next_input[None, None],
        sent_back[None, None],
        expand_grad.T[None],
        reduce_grad[None],
        filter_grad[None],
    )


def solution(mesh):
    finer = Mesh(
        mesh.devices.reshape(mesh.shape["pipe"], 16, 2, mesh.shape["dp"]),
        ("pipe", "sp_0", "sp_1", "dp"),
    )
    in_specs = (
        P("pipe", "dp", SP, None, None),
        P("pipe", "dp", SP, None, None),
        P("pipe", "dp", SP, None, None),
        P("pipe", None, None),
        P("pipe", None, None),
        P("pipe", None, None, None),
        P(),
    )
    out_specs = (
        P("pipe", "dp", SP, None, None),
        P("pipe", "dp", SP, None, None),
        P("pipe", None, "dp"),
        P("pipe", "dp", None),
        P("pipe", None, None, None),
    )
    program = functools.partial(on_device, fourier_constants(), order_constants())
    return jax.shard_map(
        program, mesh=finer, in_specs=in_specs, out_specs=out_specs, check_vma=False
    )
```

```python
import functools
import math

import jax
import jax.numpy as jnp
import numpy as np
from jax import lax
from jax.experimental import pallas as pl
from jax.experimental.pallas import tpu as pltpu
from jax.sharding import Mesh
from jax.sharding import PartitionSpec as P

NLAT = 120
NLON = 240
CH = 128
HID = 768
ROWS = 4
PEERS = 32
VMEM_LIMIT = 16 * 1024 * 1024
LANES = 128
SP = ("sp_0", "sp_1")

ROOT_HALF = 0.7071067811865476
INV_ROOT_TAU = 0.3989422804014327
F32 = jnp.float32
BF16 = jnp.bfloat16


def fourier_constants():
    order = np.arange(128)
    live = (order < NLAT).astype(np.float64)
    value = np.minimum(order, NLAT - 1)
    phase = 2.0 * math.pi / NLON * ((np.arange(NLON)[:, None] * value[None, :]) % NLON)
    scaled = live * (2.0 * math.pi / NLON)
    forward = np.stack([np.cos(phase) * scaled, -np.sin(phase) * scaled], axis=1)
    factor = np.where(value == 0, 1.0, 2.0) * live / (2.0 * math.pi)
    inverse = np.stack([np.cos(phase) * factor, -np.sin(phase) * factor], axis=1)

    def arranged(table, places):
        table = table.reshape(NLON, 2, PEERS, ROWS).transpose(0, *places)
        return table.reshape(NLON, 256).astype(np.float32).astype(jnp.bfloat16)

    saved, fresh = (2, 1, 3), (3, 1, 2)
    return [arranged(table, places) for places in (saved, fresh) for table in (forward, inverse)]


def order_constants():
    table = np.zeros((PEERS, 3, 8, LANES), np.float32)
    for position in range(PEERS):
        for row in range(8):
            slot = position * ROWS + row % ROWS
            m = min(slot, NLAT - 1)
            log_start = 0.5 * (
                math.log((2.0 * m + 1.0) / (4.0 * math.pi))
                + math.lgamma(2.0 * m + 1.0)
                - 2.0 * math.lgamma(m + 1.0)
                - m * math.log(4.0)
            )
            table[position, 0, row] = m
            table[position, 1, row] = log_start
            table[position, 2, row] = float(slot < NLAT)
    return table


def tables_kernel(geo_ref, order_ref, ana_ref, syn_ref, work_ref):
    shape = (8, LANES)
    cosine = jnp.broadcast_to(geo_ref[0:1, :], shape)
    log_sine = jnp.broadcast_to(geo_ref[1:2, :], shape)
    weight = geo_ref[2:3, :]
    m = order_ref[0]
    keep = order_ref[2] * jnp.broadcast_to(geo_ref[3:4, :], shape)
    starting = jnp.exp(order_ref[1] + m * log_sine)
    squares = m * m
    previous = jnp.zeros(shape, F32)
    earlier = previous
    for degree in range(NLAT):
        upper = max(4.0 * degree * degree - 1.0, 0.0)
        lower = max(4.0 * (degree - 1.0) ** 2 - 1.0, 1.0)
        ratio_main = jnp.sqrt(upper / jnp.maximum(float(degree * degree) - squares, 1.0))
        ratio_back = jnp.sqrt(jnp.maximum((degree - 1.0) ** 2 - squares, 0.0) / lower)
        rising = ratio_main * (cosine * previous - ratio_back * earlier)
        current = jnp.where(m == float(degree), starting, jnp.where(m < float(degree), rising, 0.0))
        work_ref[degree * 8 : degree * 8 + 8, :] = current * keep
        previous, earlier = current, previous
    work_ref[NLAT * 8 :, :] = jnp.zeros((LANES * 8 - NLAT * 8, LANES), F32)
    for t in range(ROWS):
        table = work_ref[pl.ds(t, LANES, stride=8), :]
        syn_ref[t] = table.astype(BF16)
        ana_ref[t] = (table * weight).astype(BF16)


def to_blocks(out_ref, half, pair):
    blocks = [part.reshape(PEERS, 8, CH) for part in pair]
    out_ref[:, 16 * half : 16 * half + 16, :] = jnp.concatenate(blocks, axis=1).astype(BF16)


def from_blocks(block_ref, half):
    pair = block_ref[:, 16 * half : 16 * half + 16, :].astype(F32)
    return [pair[:, 8 * h : 8 * h + 8].reshape(256, CH).astype(BF16) for h in range(2)]


def matmul(left, right, dims=((1,), (0,))):
    return lax.dot_general(left, right, (dims, ((), ())), preferred_element_type=F32)


def fetch(source, target, sem):
    copy = pltpu.make_async_copy(source, target, sem)
    copy.start()
    return copy


def saved_coeffs_kernel(x_hbm, forward_hbm, out_ref, x_ref, forward_ref, sems):
    table = fetch(forward_hbm, forward_ref, sems.at[ROWS])
    cycles = [fetch(x_hbm.at[j], x_ref.at[j], sems.at[j]) for j in range(ROWS)]
    table.wait()
    for half in range(2):
        cycles[2 * half].wait()
        cycles[2 * half + 1].wait()
        to_blocks(out_ref, half, [matmul(forward_ref[...], x_ref[2 * half + h]) for h in range(2)])


def fresh_coeffs_kernel(x_ref, forward_ref, *rest):
    *sources, own_ref, lent_ref, packed_ref, work_ref = rest
    row = 0
    for source in sources:
        rows, columns = source.shape
        for start in range(0, columns, CH):
            width = min(CH, columns - start)
            packed_ref[row : row + rows, :width] = source[:, start : start + width]
            row += rows
    contract_ref, expand_ref = sources[:2]
    for n in range(HID // CH):
        columns = slice(n * CH, (n + 1) * CH)
        packed_ref[row + n * CH : row + (n + 1) * CH, :] = contract_ref[columns, :].T
        packed_ref[row + HID + n * CH : row + HID + (n + 1) * CH, :] = expand_ref[:, columns].T
    for j in range(ROWS):
        coeffs = matmul(forward_ref[...], x_ref[j])
        for place in range(8):
            target = pl.ds(place // 2 * 256 + j * 2 + place % 2, PEERS, stride=8)
            work_ref[target, :] = coeffs[place * PEERS : (place + 1) * PEERS]
    groups = [work_ref[256 * u : 256 * u + 256, :].reshape(PEERS, 8, CH) for u in range(ROWS)]
    own_ref[...] = jnp.concatenate(groups[:3], axis=1).astype(BF16)
    lent_ref[...] = groups[3].astype(BF16)


def padded_filter(filt_ref):
    rest = jnp.zeros((LANES - NLAT, CH), F32)
    return [jnp.concatenate([filt_ref[part], rest], axis=0) for part in range(2)]


def filter_step(spectra, real, imag):
    first, second = spectra[:, :CH], spectra[:, CH:]
    return jnp.concatenate(
        [real * first - imag * second, real * second + imag * first], axis=1
    ).astype(BF16)


def spectral(came_ref, goes_ref, ana_ref, syn_ref, filt_ref, spectra_ref):
    real, imag = padded_filter(filt_ref)
    for t in range(ROWS):
        parts = [came_ref[pl.ds(r * ROWS + t, LANES, stride=8), :] for r in range(2)]
        spectra = matmul(ana_ref[t], jnp.concatenate(parts, axis=1).astype(BF16))
        spectra_ref[t] = spectra.astype(BF16)
        values = matmul(syn_ref[t], filter_step(spectra, real, imag), ((0,), (0,)))
        for r in range(2):
            goes_ref[pl.ds(r * ROWS + t, LANES, stride=8), :] = values[:, r * CH : (r + 1) * CH]


def saved_spectral_kernel(
    arrived_ref, ana_ref, syn_ref, filt_ref, beside_ref, out_ref, spectra_ref, came_ref, goes_ref
):
    out_ref[:, 32:, :] = beside_ref[...]
    came_ref[...] = arrived_ref[...].reshape(LANES * 8, CH).astype(F32)
    spectral(came_ref, goes_ref, ana_ref, syn_ref, filt_ref, spectra_ref)
    out_ref[:, :32, :] = goes_ref[...].reshape(PEERS, 32, CH).astype(BF16)


def fresh_spectral(arrived_ref, ana_ref, syn_ref, filters_ref, last_ref, came_ref, goes_ref):
    came = arrived_ref[:, 32:, :].astype(F32)
    last = last_ref[0]
    for u in range(3):
        came_ref[256 * u : 256 * u + 256, :] = came[:, 8 * u : 8 * u + 8].reshape(256, CH)
        real, imag = padded_filter(filters_ref.at[u])
        t = jnp.where(last == 1, 3, u)
        parts = [came_ref[pl.ds(256 * u + r, LANES, stride=2), :] for r in range(2)]
        spectra = matmul(ana_ref[t], jnp.concatenate(parts, axis=1).astype(BF16))
        values = matmul(syn_ref[t], filter_step(spectra, real, imag), ((0,), (0,)))
        for r in range(2):
            goes_ref[pl.ds(256 * u + r, LANES, stride=2), :] = values[:, r * CH : (r + 1) * CH]
    groups = [goes_ref[256 * u : 256 * u + 256, :].reshape(PEERS, 8, CH) for u in range(3)]
    return jnp.concatenate(groups, axis=1).astype(BF16)


def spectral_back_kernel(
    arrived_ref,
    spectra_ref,
    ana_ref,
    syn_ref,
    filt_ref,
    shares_ref,
    out_ref,
    came_ref,
    goes_ref,
):
    came_ref[...] = arrived_ref[:, :32, :].reshape(LANES * 8, CH).astype(F32)
    real, imag = padded_filter(filt_ref)
    total_real = jnp.zeros((LANES, CH), F32)
    total_imag = jnp.zeros((LANES, CH), F32)
    for t in range(ROWS):
        parts = [came_ref[pl.ds(r * ROWS + t, LANES, stride=8), :] for r in range(2)]
        grads = matmul(syn_ref[t], jnp.concatenate(parts, axis=1).astype(BF16))
        first, second = grads[:, :CH], grads[:, CH:]
        spectra = spectra_ref[t].astype(F32)
        s_first, s_second = spectra[:, :CH], spectra[:, CH:]
        total_real = total_real + (first * s_first + second * s_second)
        total_imag = total_imag + (second * s_first - first * s_second)
        grad_spectra = jnp.concatenate(
            [real * first + imag * second, real * second - imag * first], axis=1
        ).astype(BF16)
        coeffs = matmul(ana_ref[t], grad_spectra, ((0,), (0,)))
        for r in range(2):
            goes_ref[pl.ds(r * ROWS + t, LANES, stride=8), :] = coeffs[:, r * CH : (r + 1) * CH]
    out_ref[:, :32, :] = goes_ref[...].reshape(PEERS, 32, CH).astype(BF16)
    filter_part = jnp.concatenate([total_real, total_imag], axis=0).reshape(PEERS, 8, CH)
    sums = jnp.concatenate([shares_ref[...].astype(F32), filter_part], axis=1)
    out_ref[:, 32:, :] = sums.astype(BF16)


PLACES = {}
for _name, _rows, _columns in (
    ("contract", HID, CH),
    ("expand", CH, HID),
    ("inverse", NLON, 256),
    ("fresh_inverse", NLON, 256),
    ("inverse_t", 256, NLON),
    ("contract_t", CH, HID),
    ("expand_t", HID, CH),
):
    PLACES[_name] = (sum(r * -(-c // CH) for _, r, c in PLACES.values()), _rows, _columns)
PACKED_ROWS = sum(r * -(-c // CH) for _, r, c in PLACES.values())


def unpacked(packed_ref, name):
    row, rows, columns = PLACES[name]
    blocks = [
        packed_ref[row + n * rows : row + (n + 1) * rows, :] for n in range(-(-columns // CH))
    ]
    return jnp.concatenate(blocks, axis=1)[:, :columns] if len(blocks) > 1 else blocks[0]


def live(cycle_ref, j):
    return jnp.where(cycle_ref[j] < NLAT, 1.0, 0.0).astype(F32)


def mlp_kernel(
    x_ref,
    values_ref,
    lent_a_ref,
    lent_b_ref,
    lent_c_ref,
    packed_ref,
    cycle_ref,
    out_ref,
    work_ref,
):
    names = ("fresh_inverse", "expand", "contract")
    inverse, expand, contract = [unpacked(packed_ref, name) for name in names]
    own = values_ref[:, 32:, :].astype(F32)
    lent = [ref[...].astype(F32) for ref in (lent_a_ref, lent_b_ref, lent_c_ref)]
    for u in range(3):
        work_ref[256 * u : 256 * u + 256, :] = own[:, 8 * u : 8 * u + 8].reshape(256, CH)
    work_ref[768:, :] = (lent[0] + lent[1] + lent[2]).reshape(256, CH)
    for j in range(ROWS):
        parts = [
            work_ref[pl.ds(place // 2 * 256 + j * 2 + place % 2, PEERS, stride=8), :]
            for place in range(8)
        ]
        values = jnp.concatenate(parts, axis=0).astype(BF16)
        mixed = x_ref[j].astype(F32) + matmul(inverse, values)
        pre = matmul(mixed.astype(BF16), expand)
        hidden = (0.5 * pre * (1.0 + lax.erf(pre * ROOT_HALF))).astype(BF16)
        result = mixed + matmul(hidden, contract)
        out_ref[j] = (result * live(cycle_ref, j)).astype(BF16)


def mlp_back_kernel(
    x_ref,
    values_ref,
    cotangent_ref,
    packed_ref,
    cycle_ref,
    ana_ref,
    syn_ref,
    filters_ref,
    last_ref,
    out_ref,
    grad_mixed_ref,
    shares_ref,
    mixed_ref,
    masked_ref,
    hidden_ref,
    grad_pre_ref,
    came_ref,
    goes_ref,
):
    names = ("inverse", "inverse_t", "expand", "contract_t", "expand_t")
    inverse, inverse_t, expand, contract_t, expand_t = [unpacked(packed_ref, n) for n in names]
    for half in range(2):
        values = from_blocks(values_ref, half)
        grad_values = []
        for h in range(2):
            j = 2 * half + h
            rows = slice(j * NLON, (j + 1) * NLON)
            mixed = x_ref[j].astype(F32) + matmul(inverse, values[h])
            mixed_b = mixed.astype(BF16)
            masked_f = cotangent_ref[j].astype(F32) * live(cycle_ref, j)
            masked = masked_f.astype(BF16)
            mixed_ref[rows, :] = mixed_b
            masked_ref[rows, :] = masked
            pre = matmul(mixed_b, expand)
            normal = 0.5 * (1.0 + lax.erf(pre * ROOT_HALF))
            hidden_ref[rows, :] = (pre * normal).astype(BF16)
            slope = normal + pre * jnp.exp(-0.5 * pre * pre) * INV_ROOT_TAU
            grad_hidden = matmul(masked, contract_t)
            grad_pre = (grad_hidden * slope).astype(BF16)
            grad_pre_ref[rows, :] = grad_pre
            grad_mixed = masked_f + matmul(grad_pre, expand_t)
            grad_mixed_ref[j] = grad_mixed.astype(BF16)
            grad_values.append(matmul(inverse_t, grad_mixed.astype(BF16)))
        to_blocks(out_ref, half, grad_values)
    out_ref[:, 32:, :] = fresh_spectral(
        values_ref,
        ana_ref,
        syn_ref,
        filters_ref,
        last_ref,
        came_ref,
        goes_ref,
    )
    quarter = HID // 4
    pairs = ((grad_pre_ref, mixed_ref), (hidden_ref, masked_ref))
    for side, (wide_ref, narrow_ref) in enumerate(pairs):
        grad = matmul(wide_ref[...], narrow_ref[...], ((0,), (0,))).astype(BF16)
        for d in range(4):
            shares_ref[side, d] = grad[d * quarter : (d + 1) * quarter]


def input_grad_kernel(coeffs_ref, grad_mixed_ref, forward_ref, cycle_ref, out_ref):
    for half in range(2):
        values = from_blocks(coeffs_ref, half)
        for h in range(2):
            j = 2 * half + h
            total = grad_mixed_ref[j].astype(F32) + matmul(forward_ref[...], values[h])
            out_ref[j] = (total * live(cycle_ref, j)).astype(BF16)


def piece_kernel(arrived_ref, out_ref):
    came = arrived_ref[:, 32:, :].astype(F32).reshape(PEERS // 2, 2, 16, CH)
    sums = came.sum(axis=0)
    piece = jnp.concatenate([sums[0, :8], sums[1, :8], sums[0, 8:] + sums[1, 8:]], axis=0)
    out_ref[...] = jnp.broadcast_to(piece[None], out_ref.shape).astype(BF16)


def filter_rows_kernel(pieces_ref, out_ref):
    rows = pieces_ref[...].astype(F32)[:, 16:].reshape(128, CH).astype(BF16)
    out_ref[...] = jnp.broadcast_to(rows[None], out_ref.shape)


def result_kernel(
    pieces_ref,
    other_ref,
    filter_rows_ref,
    core_ref,
    next_ref,
    back_ref,
    expand_ref,
    reduce_ref,
    filter_ref,
    next_out_ref,
    back_out_ref,
):
    next_out_ref[...] = next_ref[...]
    back_out_ref[...] = back_ref[...]
    first = core_ref[0] == 0
    filters = [filter_rows_ref[4 * c : 4 * c + 4].astype(F32).sum(axis=0) for c in range(2)]
    for p in range(PEERS):
        mine, other = pieces_ref[p // 2].astype(F32), other_ref[p // 2].astype(F32)
        piece = jnp.where(first, mine, other) if p % 2 == 0 else jnp.where(first, other, mine)
        expand_ref[p * 6 : p * 6 + 6, :] = piece[:6]
        reduce_ref[p * 6 : p * 6 + 6, :] = piece[8:14]
        side, at = divmod(p, PEERS // 2)
        if at < NLAT // 8:
            rows = filters[p % 2][p // 2 * 8 : p // 2 * 8 + 8]
            filter_ref[side, at * 8 : at * 8 + 8, :] = rows


def call(
    kernel, outs, args, scratch=(), flops=0, transcendentals=0, smem=(), hbm=(), limit=VMEM_LIMIT
):
    places = {n: pltpu.SMEM for n in smem} | {n: pl.ANY for n in hbm}
    specs = [pl.BlockSpec(memory_space=places.get(n, pltpu.VMEM)) for n in range(len(args))]
    moved = sum(a.size * a.dtype.itemsize for a in (*args, *outs))
    return pl.pallas_call(
        kernel,
        out_shape=outs,
        in_specs=specs,
        out_specs=[pl.BlockSpec(memory_space=pltpu.VMEM)] * len(outs),
        scratch_shapes=list(scratch),
        compiler_params=pltpu.CompilerParams(vmem_limit_bytes=limit),
        cost_estimate=pl.CostEstimate(
            flops=flops, bytes_accessed=moved, transcendentals=transcendentals
        ),
    )(*args)


PAIRED = jax.ShapeDtypeStruct((PEERS, 56, CH), BF16)
OWN = jax.ShapeDtypeStruct((PEERS, 24, CH), BF16)
LENT = jax.ShapeDtypeStruct((PEERS, 8, CH), BF16)
SUMMED = jax.ShapeDtypeStruct((PEERS, 48, CH), BF16)
BLOCKS = jax.ShapeDtypeStruct((PEERS, 32, CH), BF16)
TOKENS = jax.ShapeDtypeStruct((ROWS, NLON, CH), BF16)
SPECTRAL_SCRATCH = (pltpu.VMEM((LANES * 8, CH), F32), pltpu.VMEM((LANES * 8, CH), F32))


CORE_SWAP = [(0, 1), (1, 0)]


def exchange(blocks, axes):
    return lax.all_to_all(blocks, axes, split_axis=0, concat_axis=0, tiled=True)


def from_behind(block, axis, distance):
    devices = range(lax.axis_size(axis))
    route = [(i - distance, i) for i in devices if i - distance in devices]
    return lax.ppermute(block, axis, route)


def to_last(block):
    return [lax.ppermute(block, "pipe", [(p, 3)]) for p in range(3)]


def halved(blocks, axis, route, kept):
    mine = lax.dynamic_index_in_dim(blocks, kept, 0, keepdims=False)
    sent = lax.dynamic_index_in_dim(blocks, 1 - kept, 0, keepdims=False)
    came = lax.ppermute(sent, axis, route)
    return (mine.astype(F32) + came.astype(F32)).astype(BF16)


def around(block, axis, distance):
    count = lax.axis_size(axis)
    return lax.ppermute(block, axis, [(i, (i + distance) % count) for i in range(count)])


def scattered_total(blocks, axis):
    count = lax.axis_size(axis)
    me = lax.axis_index(axis)

    def block_of(distance):
        return lax.dynamic_index_in_dim(blocks, (me + distance) % count, 0, keepdims=False)

    came = [around(block_of(k), axis, k) for k in range(1, count)]
    return sum((block.astype(F32) for block in came), block_of(0).astype(F32))


def share_blocks_of(shares):
    kept = halved(shares, "sp_1", CORE_SWAP, lax.axis_index("sp_1"))
    kept = scattered_total(kept, "dp").astype(BF16)
    return jnp.pad(kept.reshape(PEERS, 6, CH), ((0, 0), (0, 2), (0, 0)))


def on_device(
    tables_np,
    orders_np,
    fresh_input,
    saved_input,
    output_grad,
    expand_weight,
    reduce_weight,
    filter_weight,
    cycle_table,
):
    position = lax.axis_index(SP)
    fresh, saved, cotangent = fresh_input[0, 0], saved_input[0, 0], output_grad[0, 0]
    expand, contract, filt = expand_weight[0], reduce_weight[0], filter_weight[0]
    forward_np, inverse_np, fresh_forward_np, fresh_inverse_np = tables_np
    forward = jnp.asarray(forward_np)
    fresh_forward_t = jnp.asarray(np.ascontiguousarray(fresh_forward_np.T))
    fresh_inverse = jnp.asarray(fresh_inverse_np)
    last = lax.axis_index("pipe") == 3
    forward_t = jnp.asarray(np.ascontiguousarray(forward_np.T))
    inverse = jnp.asarray(inverse_np)
    inverse_t = jnp.asarray(np.ascontiguousarray(inverse_np.T))
    own_cycles = lax.dynamic_slice_in_dim(cycle_table, position * ROWS, ROWS)
    dft = 2 * ROWS * 256 * NLON * CH
    leg = 2 * 16 * 128 * 128 * CH
    mlp = 2 * ROWS * NLON * CH * HID

    saved_blocks = call(
        saved_coeffs_kernel,
        [BLOCKS],
        [saved, forward_t],
        (
            pltpu.VMEM((ROWS, NLON, CH), BF16),
            pltpu.VMEM((256, NLON), BF16),
            pltpu.SemaphoreType.DMA((ROWS + 1,)),
        ),
        flops=dft,
        hbm=(0, 1),
        limit=60 * 1024 * 1024,
    )[0]
    saved_at_orders = exchange(saved_blocks, SP)
    kept = [contract, expand, inverse, fresh_inverse, inverse_t]
    fresh_own, fresh_lent, packed = call(
        fresh_coeffs_kernel,
        [OWN, LENT, jax.ShapeDtypeStruct((PACKED_ROWS, CH), BF16)],
        [fresh, fresh_forward_t, *kept],
        [pltpu.VMEM((LANES * 8, CH), F32)],
        flops=dft,
    )
    fresh_blocks = jnp.where(last, jnp.concatenate(to_last(fresh_lent), axis=1), fresh_own)

    lat_live = (cycle_table < NLAT).astype(F32)
    colatitude = math.pi * (jnp.minimum(cycle_table, NLAT - 1).astype(F32) + 0.5) / NLAT
    sine = jnp.sin(colatitude)
    geo = jnp.stack(
        [jnp.cos(colatitude), jnp.log(sine), math.pi / NLAT * sine * lat_live, lat_live]
    )
    order_rows = lax.dynamic_index_in_dim(jnp.asarray(orders_np), position, 0, keepdims=False)
    tables = jax.ShapeDtypeStruct((ROWS, LANES, LANES), BF16)
    ana, syn = call(
        tables_kernel,
        [tables, tables],
        [geo, order_rows],
        [pltpu.VMEM((LANES * 8, LANES), F32)],
        flops=4_000_000,
    )

    spectra_shape = jax.ShapeDtypeStruct((ROWS, LANES, 2 * CH), BF16)
    values_fresh, spectra = call(
        saved_spectral_kernel,
        [PAIRED, spectra_shape],
        [saved_at_orders, ana, syn, filt, fresh_blocks],
        SPECTRAL_SCRATCH,
        flops=leg,
    )
    lent_filt, values_fresh = lax.optimization_barrier((filt, values_fresh))
    fresh_filters = jnp.where(last, jnp.stack(to_last(lent_filt)), filt[None])
    values_fresh = exchange(values_fresh, SP)

    narrow = pltpu.VMEM((ROWS * NLON, CH), BF16)
    wide = pltpu.VMEM((ROWS * NLON, HID), BF16)
    grads_fresh, grad_mixed, shares = call(
        mlp_back_kernel,
        [
            PAIRED,
            TOKENS,
            jax.ShapeDtypeStruct((2, 4, HID // 4, CH), BF16),
        ],
        [
            saved,
            values_fresh,
            cotangent,
            packed,
            own_cycles,
            ana,
            syn,
            fresh_filters,
            last.astype(jnp.int32)[None],
        ],
        [narrow, narrow, wide, wide, *SPECTRAL_SCRATCH],
        flops=5 * mlp + 2 * dft + leg,
        transcendentals=2 * ROWS * NLON * HID,
        smem=(4, 8),
    )
    grads_fresh = exchange(grads_fresh, SP)
    share_blocks = share_blocks_of(shares)

    lent_values = [
        lax.ppermute(grads_fresh[:, 32 + 8 * p : 40 + 8 * p], "pipe", [(3, p)]) for p in range(3)
    ]
    block = call(
        mlp_kernel,
        [TOKENS],
        [fresh, grads_fresh, *lent_values, packed, own_cycles],
        [pltpu.VMEM((LANES * 8, CH), F32)],
        flops=2 * mlp + dft,
        transcendentals=ROWS * NLON * HID,
        smem=(6,),
    )[0]
    next_input = from_behind(block, "pipe", 1)
    coeffs_summed = call(
        spectral_back_kernel,
        [SUMMED],
        [grads_fresh, spectra, ana, syn, filt, share_blocks],
        SPECTRAL_SCRATCH,
        flops=leg,
    )[0]
    coeffs_summed = exchange(coeffs_summed, SP)
    coeffs_summed, _ = lax.optimization_barrier((coeffs_summed, block))
    pieces = call(
        piece_kernel, [jax.ShapeDtypeStruct((PEERS // 2, 24, CH), BF16)], [coeffs_summed]
    )[0]
    pieces = exchange(pieces, "sp_0")
    filter_rows = call(
        filter_rows_kernel, [jax.ShapeDtypeStruct((8, 128, CH), BF16)], [pieces]
    )[0]
    filter_rows = exchange(filter_rows, ("sp_1", "dp"))
    other_pieces = lax.ppermute(pieces, "sp_1", CORE_SWAP)
    input_grad = call(
        input_grad_kernel,
        [TOKENS],
        [coeffs_summed, grad_mixed, forward, own_cycles],
        flops=dft,
        smem=(3,),
    )[0]
    sent_back = from_behind(input_grad, "pipe", -1)
    part = jax.ShapeDtypeStruct((HID // 4, CH), F32)
    core = lax.axis_index("sp_1").astype(jnp.int32)[None]
    expand_grad, reduce_grad, filter_grad, next_input, sent_back = call(
        result_kernel,
        [part, part, jax.ShapeDtypeStruct((2, NLAT, CH), F32), TOKENS, TOKENS],
        [pieces, other_pieces, filter_rows, core, next_input, sent_back],
        smem=(3,),
    )
    return (
        next_input[None, None],
        sent_back[None, None],
        expand_grad.T[None],
        reduce_grad[None],
        filter_grad[None],
    )


def solution(mesh):
    finer = Mesh(
        mesh.devices.reshape(mesh.shape["pipe"], 16, 2, mesh.shape["dp"]),
        ("pipe", "sp_0", "sp_1", "dp"),
    )
    in_specs = (
        P("pipe", "dp", SP, None, None),
        P("pipe", "dp", SP, None, None),
        P("pipe", "dp", SP, None, None),
        P("pipe", None, None),
        P("pipe", None, None),
        P("pipe", None, None, None),
        P(),
    )
    out_specs = (
        P("pipe", "dp", SP, None, None),
        P("pipe", "dp", SP, None, None),
        P("pipe", None, "dp"),
        P("pipe", "dp", None),
        P("pipe", None, None, None),
    )
    program = functools.partial(on_device, fourier_constants(), order_constants())
    return jax.shard_map(
        program, mesh=finer, in_specs=in_specs, out_specs=out_specs, check_vma=False
    )
```

```python
import functools
import math

import jax
import jax.numpy as jnp
import numpy as np
from jax import lax
from jax.experimental import pallas as pl
from jax.experimental.pallas import tpu as pltpu
from jax.sharding import Mesh
from jax.sharding import PartitionSpec as P

NLAT = 120
NLON = 240
CH = 128
HID = 768
ROWS = 4
PEERS = 32
VMEM_LIMIT = 16 * 1024 * 1024
LANES = 128
SP = ("sp_0", "sp_1")

ROOT_HALF = 0.7071067811865476
INV_ROOT_TAU = 0.3989422804014327
F32 = jnp.float32
BF16 = jnp.bfloat16


def fourier_constants():
    order = np.arange(128)
    live = (order < NLAT).astype(np.float64)
    value = np.minimum(order, NLAT - 1)
    phase = 2.0 * math.pi / NLON * ((np.arange(NLON)[:, None] * value[None, :]) % NLON)
    scaled = live * (2.0 * math.pi / NLON)
    forward = np.stack([np.cos(phase) * scaled, -np.sin(phase) * scaled], axis=1)
    factor = np.where(value == 0, 1.0, 2.0) * live / (2.0 * math.pi)
    inverse = np.stack([np.cos(phase) * factor, -np.sin(phase) * factor], axis=1)

    def arranged(table, places):
        table = table.reshape(NLON, 2, PEERS, ROWS).transpose(0, *places)
        return table.reshape(NLON, 256).astype(np.float32).astype(jnp.bfloat16)

    saved, fresh = (2, 1, 3), (3, 1, 2)
    return [arranged(table, places) for places in (saved, fresh) for table in (forward, inverse)]


def order_constants():
    table = np.zeros((PEERS, 3, 8, LANES), np.float32)
    for position in range(PEERS):
        for row in range(8):
            slot = position * ROWS + row % ROWS
            m = min(slot, NLAT - 1)
            log_start = 0.5 * (
                math.log((2.0 * m + 1.0) / (4.0 * math.pi))
                + math.lgamma(2.0 * m + 1.0)
                - 2.0 * math.lgamma(m + 1.0)
                - m * math.log(4.0)
            )
            table[position, 0, row] = m
            table[position, 1, row] = log_start
            table[position, 2, row] = float(slot < NLAT)
    return table


def tables_kernel(geo_ref, order_ref, ana_ref, syn_ref, work_ref):
    shape = (8, LANES)
    cosine = jnp.broadcast_to(geo_ref[0:1, :], shape)
    log_sine = jnp.broadcast_to(geo_ref[1:2, :], shape)
    weight = geo_ref[2:3, :]
    m = order_ref[0]
    keep = order_ref[2] * jnp.broadcast_to(geo_ref[3:4, :], shape)
    starting = jnp.exp(order_ref[1] + m * log_sine)
    squares = m * m
    previous = jnp.zeros(shape, F32)
    earlier = previous
    for degree in range(NLAT):
        upper = max(4.0 * degree * degree - 1.0, 0.0)
        lower = max(4.0 * (degree - 1.0) ** 2 - 1.0, 1.0)
        ratio_main = jnp.sqrt(upper / jnp.maximum(float(degree * degree) - squares, 1.0))
        ratio_back = jnp.sqrt(jnp.maximum((degree - 1.0) ** 2 - squares, 0.0) / lower)
        rising = ratio_main * (cosine * previous - ratio_back * earlier)
        current = jnp.where(m == float(degree), starting, jnp.where(m < float(degree), rising, 0.0))
        work_ref[degree * 8 : degree * 8 + 8, :] = current * keep
        previous, earlier = current, previous
    work_ref[NLAT * 8 :, :] = jnp.zeros((LANES * 8 - NLAT * 8, LANES), F32)
    for t in range(ROWS):
        table = work_ref[pl.ds(t, LANES, stride=8), :]
        syn_ref[t] = table.astype(BF16)
        ana_ref[t] = (table * weight).astype(BF16)


def to_blocks(out_ref, half, pair):
    blocks = [part.reshape(PEERS, 8, CH) for part in pair]
    out_ref[:, 16 * half : 16 * half + 16, :] = jnp.concatenate(blocks, axis=1).astype(BF16)


def from_blocks(block_ref, half):
    pair = block_ref[:, 16 * half : 16 * half + 16, :].astype(F32)
    return [pair[:, 8 * h : 8 * h + 8].reshape(256, CH).astype(BF16) for h in range(2)]


def matmul(left, right, dims=((1,), (0,))):
    return lax.dot_general(left, right, (dims, ((), ())), preferred_element_type=F32)


def fetch(source, target, sem):
    copy = pltpu.make_async_copy(source, target, sem)
    copy.start()
    return copy


def saved_coeffs_kernel(x_hbm, forward_hbm, out_ref, x_ref, forward_ref, sems):
    table = fetch(forward_hbm, forward_ref, sems.at[ROWS])
    cycles = [fetch(x_hbm.at[j], x_ref.at[j], sems.at[j]) for j in range(ROWS)]
    table.wait()
    for half in range(2):
        cycles[2 * half].wait()
        cycles[2 * half + 1].wait()
        to_blocks(out_ref, half, [matmul(forward_ref[...], x_ref[2 * half + h]) for h in range(2)])


def fresh_coeffs_kernel(x_ref, forward_ref, *rest):
    *sources, own_ref, lent_ref, packed_ref, work_ref = rest
    row = 0
    for source in sources:
        rows, columns = source.shape
        for start in range(0, columns, CH):
            width = min(CH, columns - start)
            packed_ref[row : row + rows, :width] = source[:, start : start + width]
            row += rows
    for j in range(ROWS):
        coeffs = matmul(forward_ref[...], x_ref[j])
        for place in range(8):
            target = pl.ds(place // 2 * 256 + j * 2 + place % 2, PEERS, stride=8)
            work_ref[target, :] = coeffs[place * PEERS : (place + 1) * PEERS]
    groups = [work_ref[256 * u : 256 * u + 256, :].reshape(PEERS, 8, CH) for u in range(ROWS)]
    own_ref[...] = jnp.concatenate(groups[:3], axis=1).astype(BF16)
    lent_ref[...] = groups[3].astype(BF16)


def padded_filter(filt_ref):
    rest = jnp.zeros((LANES - NLAT, CH), F32)
    return [jnp.concatenate([filt_ref[part], rest], axis=0) for part in range(2)]


def filter_step(spectra, real, imag):
    first, second = spectra[:, :CH], spectra[:, CH:]
    return jnp.concatenate(
        [real * first - imag * second, real * second + imag * first], axis=1
    ).astype(BF16)


def spectral(came_ref, goes_ref, ana_ref, syn_ref, filt_ref, spectra_ref):
    real, imag = padded_filter(filt_ref)
    for t in range(ROWS):
        parts = [came_ref[pl.ds(r * ROWS + t, LANES, stride=8), :] for r in range(2)]
        spectra = matmul(ana_ref[t], jnp.concatenate(parts, axis=1).astype(BF16))
        spectra_ref[t] = spectra.astype(BF16)
        values = matmul(syn_ref[t], filter_step(spectra, real, imag), ((0,), (0,)))
        for r in range(2):
            goes_ref[pl.ds(r * ROWS + t, LANES, stride=8), :] = values[:, r * CH : (r + 1) * CH]


def saved_spectral_kernel(
    arrived_ref, ana_ref, syn_ref, filt_ref, beside_ref, out_ref, spectra_ref, came_ref, goes_ref
):
    out_ref[:, 32:, :] = beside_ref[...]
    came_ref[...] = arrived_ref[...].reshape(LANES * 8, CH).astype(F32)
    spectral(came_ref, goes_ref, ana_ref, syn_ref, filt_ref, spectra_ref)
    out_ref[:, :32, :] = goes_ref[...].reshape(PEERS, 32, CH).astype(BF16)


def fresh_spectral(arrived_ref, ana_ref, syn_ref, filters_ref, last_ref, came_ref, goes_ref):
    came = arrived_ref[:, 32:, :].astype(F32)
    last = last_ref[0]
    for u in range(3):
        came_ref[256 * u : 256 * u + 256, :] = came[:, 8 * u : 8 * u + 8].reshape(256, CH)
        real, imag = padded_filter(filters_ref.at[u])
        t = jnp.where(last == 1, 3, u)
        parts = [came_ref[pl.ds(256 * u + r, LANES, stride=2), :] for r in range(2)]
        spectra = matmul(ana_ref[t], jnp.concatenate(parts, axis=1).astype(BF16))
        values = matmul(syn_ref[t], filter_step(spectra, real, imag), ((0,), (0,)))
        for r in range(2):
            goes_ref[pl.ds(256 * u + r, LANES, stride=2), :] = values[:, r * CH : (r + 1) * CH]
    groups = [goes_ref[256 * u : 256 * u + 256, :].reshape(PEERS, 8, CH) for u in range(3)]
    return jnp.concatenate(groups, axis=1).astype(BF16)


def spectral_back_kernel(
    arrived_ref,
    spectra_ref,
    ana_ref,
    syn_ref,
    filt_ref,
    shares_ref,
    out_ref,
    came_ref,
    goes_ref,
):
    came_ref[...] = arrived_ref[:, :32, :].reshape(LANES * 8, CH).astype(F32)
    real, imag = padded_filter(filt_ref)
    total_real = jnp.zeros((LANES, CH), F32)
    total_imag = jnp.zeros((LANES, CH), F32)
    for t in range(ROWS):
        parts = [came_ref[pl.ds(r * ROWS + t, LANES, stride=8), :] for r in range(2)]
        grads = matmul(syn_ref[t], jnp.concatenate(parts, axis=1).astype(BF16))
        first, second = grads[:, :CH], grads[:, CH:]
        spectra = spectra_ref[t].astype(F32)
        s_first, s_second = spectra[:, :CH], spectra[:, CH:]
        total_real = total_real + (first * s_first + second * s_second)
        total_imag = total_imag + (second * s_first - first * s_second)
        grad_spectra = jnp.concatenate(
            [real * first + imag * second, real * second - imag * first], axis=1
        ).astype(BF16)
        coeffs = matmul(ana_ref[t], grad_spectra, ((0,), (0,)))
        for r in range(2):
            goes_ref[pl.ds(r * ROWS + t, LANES, stride=8), :] = coeffs[:, r * CH : (r + 1) * CH]
    out_ref[:, :32, :] = goes_ref[...].reshape(PEERS, 32, CH).astype(BF16)
    filter_part = jnp.concatenate([total_real, total_imag], axis=0).reshape(PEERS, 8, CH)
    sums = jnp.concatenate([shares_ref[...].astype(F32), filter_part], axis=1)
    out_ref[:, 32:, :] = sums.astype(BF16)


PLACES = {}
for _name, _rows, _columns in (
    ("contract", HID, CH),
    ("expand", CH, HID),
    ("inverse", NLON, 256),
    ("fresh_inverse", NLON, 256),
    ("inverse_t", 256, NLON),
    ("cotangent", ROWS * NLON, CH),
    ("saved", ROWS * NLON, CH),
):
    PLACES[_name] = (sum(r * -(-c // CH) for _, r, c in PLACES.values()), _rows, _columns)
PACKED_ROWS = sum(r * -(-c // CH) for _, r, c in PLACES.values())


def unpacked(packed_ref, name):
    row, rows, columns = PLACES[name]
    blocks = [
        packed_ref[row + n * rows : row + (n + 1) * rows, :] for n in range(-(-columns // CH))
    ]
    return jnp.concatenate(blocks, axis=1)[:, :columns] if len(blocks) > 1 else blocks[0]


def live(cycle_ref, j):
    return jnp.where(cycle_ref[j] < NLAT, 1.0, 0.0).astype(F32)


def mlp_kernel(
    x_ref,
    values_ref,
    lent_a_ref,
    lent_b_ref,
    lent_c_ref,
    packed_ref,
    cycle_ref,
    out_ref,
    work_ref,
):
    names = ("fresh_inverse", "expand", "contract")
    inverse, expand, contract = [unpacked(packed_ref, name) for name in names]
    own = values_ref[:, 32:, :].astype(F32)
    lent = [ref[...].astype(F32) for ref in (lent_a_ref, lent_b_ref, lent_c_ref)]
    for u in range(3):
        work_ref[256 * u : 256 * u + 256, :] = own[:, 8 * u : 8 * u + 8].reshape(256, CH)
    work_ref[768:, :] = (lent[0] + lent[1] + lent[2]).reshape(256, CH)
    for j in range(ROWS):
        parts = [
            work_ref[pl.ds(place // 2 * 256 + j * 2 + place % 2, PEERS, stride=8), :]
            for place in range(8)
        ]
        values = jnp.concatenate(parts, axis=0).astype(BF16)
        mixed = x_ref[j].astype(F32) + matmul(inverse, values)
        pre = matmul(mixed.astype(BF16), expand)
        hidden = (0.5 * pre * (1.0 + lax.erf(pre * ROOT_HALF))).astype(BF16)
        result = mixed + matmul(hidden, contract)
        out_ref[j] = (result * live(cycle_ref, j)).astype(BF16)


def mlp_back_kernel(
    values_ref,
    packed_ref,
    cycle_ref,
    ana_ref,
    syn_ref,
    filters_ref,
    last_ref,
    out_ref,
    grad_mixed_ref,
    shares_ref,
    mixed_ref,
    masked_ref,
    hidden_ref,
    grad_pre_ref,
    came_ref,
    goes_ref,
):
    names = ("inverse", "inverse_t", "expand", "contract")
    inverse, inverse_t, expand, contract = [unpacked(packed_ref, name) for name in names]
    cotangent = unpacked(packed_ref, "cotangent")
    saved = unpacked(packed_ref, "saved")
    for half in range(2):
        values = from_blocks(values_ref, half)
        grad_values = []
        for h in range(2):
            j = 2 * half + h
            rows = slice(j * NLON, (j + 1) * NLON)
            mixed = saved[rows].astype(F32) + matmul(inverse, values[h])
            mixed_b = mixed.astype(BF16)
            masked_f = cotangent[rows].astype(F32) * live(cycle_ref, j)
            masked = masked_f.astype(BF16)
            mixed_ref[rows, :] = mixed_b
            masked_ref[rows, :] = masked
            pre = matmul(mixed_b, expand)
            normal = 0.5 * (1.0 + lax.erf(pre * ROOT_HALF))
            hidden_ref[rows, :] = (pre * normal).astype(BF16)
            slope = normal + pre * jnp.exp(-0.5 * pre * pre) * INV_ROOT_TAU
            grad_hidden = matmul(masked, contract, ((1,), (1,)))
            grad_pre = (grad_hidden * slope).astype(BF16)
            grad_pre_ref[rows, :] = grad_pre
            grad_mixed = masked_f + matmul(grad_pre, expand, ((1,), (1,)))
            grad_mixed_ref[j] = grad_mixed.astype(BF16)
            grad_values.append(matmul(inverse_t, grad_mixed.astype(BF16)))
        to_blocks(out_ref, half, grad_values)
    out_ref[:, 32:, :] = fresh_spectral(
        values_ref,
        ana_ref,
        syn_ref,
        filters_ref,
        last_ref,
        came_ref,
        goes_ref,
    )
    quarter = HID // 4
    pairs = ((grad_pre_ref, mixed_ref), (hidden_ref, masked_ref))
    for side, (wide_ref, narrow_ref) in enumerate(pairs):
        grad = matmul(wide_ref[...], narrow_ref[...], ((0,), (0,))).astype(BF16)
        for d in range(4):
            shares_ref[side, d] = grad[d * quarter : (d + 1) * quarter]


def input_grad_kernel(coeffs_ref, grad_mixed_ref, forward_ref, cycle_ref, out_ref):
    for half in range(2):
        values = from_blocks(coeffs_ref, half)
        for h in range(2):
            j = 2 * half + h
            total = grad_mixed_ref[j].astype(F32) + matmul(forward_ref[...], values[h])
            out_ref[j] = (total * live(cycle_ref, j)).astype(BF16)


def piece_kernel(arrived_ref, out_ref):
    came = arrived_ref[:, 32:, :].astype(F32).reshape(PEERS // 2, 2, 16, CH)
    sums = came.sum(axis=0)
    piece = jnp.concatenate([sums[0, :8], sums[1, :8], sums[0, 8:] + sums[1, 8:]], axis=0)
    out_ref[...] = jnp.broadcast_to(piece[None], out_ref.shape).astype(BF16)


def filter_rows_kernel(pieces_ref, out_ref):
    rows = pieces_ref[...].astype(F32)[:, 16:].reshape(128, CH).astype(BF16)
    out_ref[...] = jnp.broadcast_to(rows[None], out_ref.shape)


def result_kernel(
    pieces_ref,
    other_ref,
    filter_rows_ref,
    core_ref,
    next_ref,
    back_ref,
    expand_ref,
    reduce_ref,
    filter_ref,
    next_out_ref,
    back_out_ref,
):
    next_out_ref[...] = next_ref[...]
    back_out_ref[...] = back_ref[...]
    first = core_ref[0] == 0
    filters = [filter_rows_ref[4 * c : 4 * c + 4].astype(F32).sum(axis=0) for c in range(2)]
    for p in range(PEERS):
        mine, other = pieces_ref[p // 2].astype(F32), other_ref[p // 2].astype(F32)
        piece = jnp.where(first, mine, other) if p % 2 == 0 else jnp.where(first, other, mine)
        expand_ref[p * 6 : p * 6 + 6, :] = piece[:6]
        reduce_ref[p * 6 : p * 6 + 6, :] = piece[8:14]
        side, at = divmod(p, PEERS // 2)
        if at < NLAT // 8:
            rows = filters[p % 2][p // 2 * 8 : p // 2 * 8 + 8]
            filter_ref[side, at * 8 : at * 8 + 8, :] = rows


def call(
    kernel, outs, args, scratch=(), flops=0, transcendentals=0, smem=(), hbm=(), limit=VMEM_LIMIT
):
    places = {n: pltpu.SMEM for n in smem} | {n: pl.ANY for n in hbm}
    specs = [pl.BlockSpec(memory_space=places.get(n, pltpu.VMEM)) for n in range(len(args))]
    moved = sum(a.size * a.dtype.itemsize for a in (*args, *outs))
    return pl.pallas_call(
        kernel,
        out_shape=outs,
        in_specs=specs,
        out_specs=[pl.BlockSpec(memory_space=pltpu.VMEM)] * len(outs),
        scratch_shapes=list(scratch),
        compiler_params=pltpu.CompilerParams(vmem_limit_bytes=limit),
        cost_estimate=pl.CostEstimate(
            flops=flops, bytes_accessed=moved, transcendentals=transcendentals
        ),
    )(*args)


PAIRED = jax.ShapeDtypeStruct((PEERS, 56, CH), BF16)
OWN = jax.ShapeDtypeStruct((PEERS, 24, CH), BF16)
LENT = jax.ShapeDtypeStruct((PEERS, 8, CH), BF16)
SUMMED = jax.ShapeDtypeStruct((PEERS, 48, CH), BF16)
BLOCKS = jax.ShapeDtypeStruct((PEERS, 32, CH), BF16)
TOKENS = jax.ShapeDtypeStruct((ROWS, NLON, CH), BF16)
SPECTRAL_SCRATCH = (pltpu.VMEM((LANES * 8, CH), F32), pltpu.VMEM((LANES * 8, CH), F32))


CORE_SWAP = [(0, 1), (1, 0)]


def exchange(blocks, axes):
    return lax.all_to_all(blocks, axes, split_axis=0, concat_axis=0, tiled=True)


def from_behind(block, axis, distance):
    devices = range(lax.axis_size(axis))
    route = [(i - distance, i) for i in devices if i - distance in devices]
    return lax.ppermute(block, axis, route)


def to_last(block):
    return [lax.ppermute(block, "pipe", [(p, 3)]) for p in range(3)]


def halved(blocks, axis, route, kept):
    mine = lax.dynamic_index_in_dim(blocks, kept, 0, keepdims=False)
    sent = lax.dynamic_index_in_dim(blocks, 1 - kept, 0, keepdims=False)
    came = lax.ppermute(sent, axis, route)
    return (mine.astype(F32) + came.astype(F32)).astype(BF16)


def around(block, axis, distance):
    count = lax.axis_size(axis)
    return lax.ppermute(block, axis, [(i, (i + distance) % count) for i in range(count)])


def scattered_total(blocks, axis):
    count = lax.axis_size(axis)
    me = lax.axis_index(axis)

    def block_of(distance):
        return lax.dynamic_index_in_dim(blocks, (me + distance) % count, 0, keepdims=False)

    came = [around(block_of(k), axis, k) for k in range(1, count)]
    return sum((block.astype(F32) for block in came), block_of(0).astype(F32))


def share_blocks_of(shares):
    kept = halved(shares, "sp_1", CORE_SWAP, lax.axis_index("sp_1"))
    kept = scattered_total(kept, "dp").astype(BF16)
    return jnp.pad(kept.reshape(PEERS, 6, CH), ((0, 0), (0, 2), (0, 0)))


def on_device(
    tables_np,
    orders_np,
    fresh_input,
    saved_input,
    output_grad,
    expand_weight,
    reduce_weight,
    filter_weight,
    cycle_table,
):
    position = lax.axis_index(SP)
    fresh, saved, cotangent = fresh_input[0, 0], saved_input[0, 0], output_grad[0, 0]
    expand, contract, filt = expand_weight[0], reduce_weight[0], filter_weight[0]
    forward_np, inverse_np, fresh_forward_np, fresh_inverse_np = tables_np
    forward = jnp.asarray(forward_np)
    fresh_forward_t = jnp.asarray(np.ascontiguousarray(fresh_forward_np.T))
    fresh_inverse = jnp.asarray(fresh_inverse_np)
    last = lax.axis_index("pipe") == 3
    forward_t = jnp.asarray(np.ascontiguousarray(forward_np.T))
    inverse = jnp.asarray(inverse_np)
    inverse_t = jnp.asarray(np.ascontiguousarray(inverse_np.T))
    own_cycles = lax.dynamic_slice_in_dim(cycle_table, position * ROWS, ROWS)
    dft = 2 * ROWS * 256 * NLON * CH
    leg = 2 * 16 * 128 * 128 * CH
    mlp = 2 * ROWS * NLON * CH * HID

    saved_blocks = call(
        saved_coeffs_kernel,
        [BLOCKS],
        [saved, forward_t],
        (
            pltpu.VMEM((ROWS, NLON, CH), BF16),
            pltpu.VMEM((256, NLON), BF16),
            pltpu.SemaphoreType.DMA((ROWS + 1,)),
        ),
        flops=dft,
        hbm=(0, 1),
        limit=60 * 1024 * 1024,
    )[0]
    saved_at_orders = exchange(saved_blocks, SP)
    kept = [contract, expand, inverse, fresh_inverse, inverse_t]
    kept += [tokens.reshape(ROWS * NLON, CH) for tokens in (cotangent, saved,)]
    fresh_own, fresh_lent, packed = call(
        fresh_coeffs_kernel,
        [OWN, LENT, jax.ShapeDtypeStruct((PACKED_ROWS, CH), BF16)],
        [fresh, fresh_forward_t, *kept],
        [pltpu.VMEM((LANES * 8, CH), F32)],
        flops=dft,
    )
    fresh_blocks = jnp.where(last, jnp.concatenate(to_last(fresh_lent), axis=1), fresh_own)

    lat_live = (cycle_table < NLAT).astype(F32)
    colatitude = math.pi * (jnp.minimum(cycle_table, NLAT - 1).astype(F32) + 0.5) / NLAT
    sine = jnp.sin(colatitude)
    geo = jnp.stack(
        [jnp.cos(colatitude), jnp.log(sine), math.pi / NLAT * sine * lat_live, lat_live]
    )
    order_rows = lax.dynamic_index_in_dim(jnp.asarray(orders_np), position, 0, keepdims=False)
    tables = jax.ShapeDtypeStruct((ROWS, LANES, LANES), BF16)
    ana, syn = call(
        tables_kernel,
        [tables, tables],
        [geo, order_rows],
        [pltpu.VMEM((LANES * 8, LANES), F32)],
        flops=4_000_000,
    )

    spectra_shape = jax.ShapeDtypeStruct((ROWS, LANES, 2 * CH), BF16)
    values_fresh, spectra = call(
        saved_spectral_kernel,
        [PAIRED, spectra_shape],
        [saved_at_orders, ana, syn, filt, fresh_blocks],
        SPECTRAL_SCRATCH,
        flops=leg,
    )
    lent_filt, values_fresh = lax.optimization_barrier((filt, values_fresh))
    fresh_filters = jnp.where(last, jnp.stack(to_last(lent_filt)), filt[None])
    values_fresh = exchange(values_fresh, SP)

    narrow = pltpu.VMEM((ROWS * NLON, CH), BF16)
    wide = pltpu.VMEM((ROWS * NLON, HID), BF16)
    grads_fresh, grad_mixed, shares = call(
        mlp_back_kernel,
        [
            PAIRED,
            TOKENS,
            jax.ShapeDtypeStruct((2, 4, HID // 4, CH), BF16),
        ],
        [
            values_fresh,
            packed,
            own_cycles,
            ana,
            syn,
            fresh_filters,
            last.astype(jnp.int32)[None],
        ],
        [narrow, narrow, wide, wide, *SPECTRAL_SCRATCH],
        flops=5 * mlp + 2 * dft + leg,
        transcendentals=2 * ROWS * NLON * HID,
        smem=(2, 6),
    )
    grads_fresh = exchange(grads_fresh, SP)
    share_blocks = share_blocks_of(shares)

    lent_values = [
        lax.ppermute(grads_fresh[:, 32 + 8 * p : 40 + 8 * p], "pipe", [(3, p)]) for p in range(3)
    ]
    block = call(
        mlp_kernel,
        [TOKENS],
        [fresh, grads_fresh, *lent_values, packed, own_cycles],
        [pltpu.VMEM((LANES * 8, CH), F32)],
        flops=2 * mlp + dft,
        transcendentals=ROWS * NLON * HID,
        smem=(6,),
    )[0]
    next_input = from_behind(block, "pipe", 1)
    coeffs_summed = call(
        spectral_back_kernel,
        [SUMMED],
        [grads_fresh, spectra, ana, syn, filt, share_blocks],
        SPECTRAL_SCRATCH,
        flops=leg,
    )[0]
    coeffs_summed = exchange(coeffs_summed, SP)
    coeffs_summed, _ = lax.optimization_barrier((coeffs_summed, block))
    pieces = call(
        piece_kernel, [jax.ShapeDtypeStruct((PEERS // 2, 24, CH), BF16)], [coeffs_summed]
    )[0]
    pieces = exchange(pieces, "sp_0")
    filter_rows = call(
        filter_rows_kernel, [jax.ShapeDtypeStruct((8, 128, CH), BF16)], [pieces]
    )[0]
    filter_rows = exchange(filter_rows, ("sp_1", "dp"))
    other_pieces = lax.ppermute(pieces, "sp_1", CORE_SWAP)
    input_grad = call(
        input_grad_kernel,
        [TOKENS],
        [coeffs_summed, grad_mixed, forward, own_cycles],
        flops=dft,
        smem=(3,),
    )[0]
    sent_back = from_behind(input_grad, "pipe", -1)
    part = jax.ShapeDtypeStruct((HID // 4, CH), F32)
    core = lax.axis_index("sp_1").astype(jnp.int32)[None]
    expand_grad, reduce_grad, filter_grad, next_input, sent_back = call(
        result_kernel,
        [part, part, jax.ShapeDtypeStruct((2, NLAT, CH), F32), TOKENS, TOKENS],
        [pieces, other_pieces, filter_rows, core, next_input, sent_back],
        smem=(3,),
    )
    return (
        next_input[None, None],
        sent_back[None, None],
        expand_grad.T[None],
        reduce_grad[None],
        filter_grad[None],
    )


def solution(mesh):
    finer = Mesh(
        mesh.devices.reshape(mesh.shape["pipe"], 16, 2, mesh.shape["dp"]),
        ("pipe", "sp_0", "sp_1", "dp"),
    )
    in_specs = (
        P("pipe", "dp", SP, None, None),
        P("pipe", "dp", SP, None, None),
        P("pipe", "dp", SP, None, None),
        P("pipe", None, None),
        P("pipe", None, None),
        P("pipe", None, None, None),
        P(),
    )
    out_specs = (
        P("pipe", "dp", SP, None, None),
        P("pipe", "dp", SP, None, None),
        P("pipe", None, "dp"),
        P("pipe", "dp", None),
        P("pipe", None, None, None),
    )
    program = functools.partial(on_device, fourier_constants(), order_constants())
    return jax.shard_map(
        program, mesh=finer, in_specs=in_specs, out_specs=out_specs, check_vma=False
    )
```
